32 devices in a mesh: section: 2 (over x), tensor: 2 (over core), seq: 8 (over z, y).
Axes of the slice: x: 2, y: 2, z: 4, core: 2. Of those that a mesh axis runs over, the one named last changes fastest.
Arguments:
- block_input: bfloat16 [4, 1024, 768], P(None, 'seq'), may hold values from -6 to 6
- out_grad: bfloat16 [4, 1024, 768], P(None, 'seq'), may hold values from -6 to 6
- doc_lengths: int32 [4, 1], replicated, may hold values from 0 to 1024, as said below
- ln1_gain: float32 [2, 768], P('section'), may hold values from 0.1 to 1.9
- ln1_bias: float32 [2, 768], P('section'), may hold values from -2 to 2
- qkv_weight: bfloat16 [2, 768, 3, 768], P('section', None, None, 'tensor'), may hold values from -0.21875 to 0.21875
- qv_bias: float32 [2, 2, 768], P('section', None, 'tensor'), may hold values from -3 to 3
- out_weight: bfloat16 [2, 768, 768], P('section', 'tensor'), may hold values from -1.25 to 1.25
- out_bias: float32 [2, 768], P('section'), may hold values from -2 to 2
- ln2_gain: float32 [2, 768], P('section'), may hold values from 0.1 to 1.9
- ln2_bias: float32 [2, 768], P('section'), may hold values from -2 to 2
- fc1_weight: bfloat16 [2, 768, 3072], P('section', None, 'tensor'), may hold values from -0.21875 to 0.21875
- fc1_bias: float32 [2, 3072], P('section', 'tensor'), may hold values from -2 to 2
- fc2_weight: bfloat16 [2, 3072, 768], P('section', 'tensor'), may hold values from -0.109375 to 0.109375
- fc2_bias: float32 [2, 768], P('section'), may hold values from -2 to 2
Outputs:
- layer_outputs: bfloat16 [2, 4, 1024, 768], P('section', None, 'seq')
- layer_grads: bfloat16 [2, 4, 1024, 768], P('section', None, 'seq')
- ln1_gain_grad: float32 [2, 768], P('section', 'seq')
- ln1_bias_grad: float32 [2, 768], P('section', 'seq')
- qkv_weight_grad: float32 [2, 768, 3, 768], P('section', 'seq', None, 'tensor')
- qv_bias_grad: float32 [2, 2, 768], P('section', None, ('tensor', 'seq'))
- out_weight_grad: float32 [2, 768, 768], P('section', ('tensor', 'seq'))
- out_bias_grad: float32 [2, 768], P('section', 'seq')
- ln2_gain_grad: float32 [2, 768], P('section', 'seq')
- ln2_bias_grad: float32 [2, 768], P('section', 'seq')
- fc1_weight_grad: float32 [2, 768, 3072], P('section', 'seq', 'tensor')
- fc1_bias_grad: float32 [2, 3072], P('section', ('tensor', 'seq'))
- fc2_weight_grad: float32 [2, 3072, 768], P('section', ('tensor', 'seq'))
- fc2_bias_grad: float32 [2, 768], P('section', 'seq')
The draws below stay inside these ranges and needn't reach their ends.
Inputs may be any that keep to these rules, and one draw needn't show every extreme that they name: `doc_lengths`: row m lists the lengths of micro-batch m's documents in order, followed by zeros, and sums to 1024. In one row, drawn from the seed, a single document holds all 1024 tokens; in every other row each document has 1024 to 2048 tokens.
All inputs are finite; a program needn't handle non-finite values.
Results may differ from the reference program's by a relative error of at most 0.02.
Values may be sent and summed in bfloat16 or wider, within the bound.
No kernel may reach another device: no remote copies, remote signals or barrier semaphores. Data moves between devices by JAX's collectives and lax.ppermute only.
A program may use at most 192 MiB of HBM per device.

```python
import math
import jax
import jax.numpy as jnp
from jax import lax

HEADS = 12
HEAD_DIM = 64
FF = 3072
MB = 4
DOC_MIN = 1024
D = 768
LAYERS = 2
TOKENS = 1024
DOCS = 1


def packed_row(key):
    count_cap = TOKENS // DOC_MIN
    docs_used = max(1, min(count_cap, 2 * TOKENS // (3 * DOC_MIN) + 1))
    spare_tokens = TOKENS - docs_used * DOC_MIN
    weights = jax.random.randint(key, (docs_used,), 64, 129, dtype=jnp.int32)
    shares = spare_tokens * weights // jnp.sum(weights, dtype=jnp.int32)
    leftover = spare_tokens - jnp.sum(shares, dtype=jnp.int32)
    shares = shares + (jnp.arange(docs_used, dtype=jnp.int32) < leftover).astype(jnp.int32)
    lengths = DOC_MIN + shares
    return jnp.concatenate([lengths, jnp.zeros((count_cap - docs_used,), jnp.int32)])


def draw_doc_lengths(key, part):
    key = jax.random.fold_in(key, 7)
    span_key, row_key = jax.random.split(key)
    row_keys = jax.random.split(row_key, MB)
    packed = jax.vmap(packed_row)(row_keys)
    spanning = jnp.zeros((DOCS,), jnp.int32).at[0].set(TOKENS)
    chosen = jax.random.randint(span_key, (), 0, MB, dtype=jnp.int32)
    return jnp.where((jnp.arange(MB, dtype=jnp.int32) == chosen)[:, None], spanning[None, :], packed)


def shard_levels(key, extent, cuts, smallest, high):
    def one(axis_at, shards_of):
        heights = jax.random.uniform(jax.random.fold_in(jax.random.fold_in(key, 6), axis_at), (shards_of,), jnp.float32, smallest / len(cuts), high / len(cuts))
        return jnp.repeat(jnp.exp(heights), extent[axis_at] // shards_of).reshape((-1,) + (1,) * (len(extent) - axis_at - 1))

    factor_of = one(*cuts[0])
    for cut in cuts[1:]:
        factor_of = factor_of * one(*cut)
    return factor_of


def gaussian(rng, extent, deviation, reach, cuts=(), kind=jnp.bfloat16):
    factor_of = shard_levels(rng, extent, cuts, -0.22, 0.18) if cuts else 1.0
    values = jax.random.normal(rng, extent, jnp.float32) * deviation * factor_of
    return jnp.minimum(jnp.maximum(values, -reach), reach).astype(kind)


def setup_inputs(seed: int = 0) -> dict:
    streams_of = jax.random.split(jax.random.key(seed), 16)
    return {
        "block_input": gaussian(streams_of[0], (MB, TOKENS, D), 1.0, 6.0, ((1, 8),)),
        "out_grad": gaussian(streams_of[1], (MB, TOKENS, D), 1.0, 6.0, ((1, 8),)),
        "doc_lengths": draw_doc_lengths(jax.random.fold_in(streams_of[15], 71), 0),
        "ln1_gain": jnp.clip(1.0 + 0.18 * jax.random.normal(streams_of[3], (LAYERS, D), jnp.float32), 0.1, 1.9),
        "ln1_bias": gaussian(streams_of[4], (LAYERS, D), 0.3, 2.0, ((0, 2),), jnp.float32),
        "qkv_weight": gaussian(streams_of[5], (LAYERS, D, 3, D), D ** -0.5, 0.21875, ((0, 2), (3, 2))),
        "qv_bias": gaussian(streams_of[6], (LAYERS, 2, D), 0.5, 3.0, ((0, 2), (2, 2)), jnp.float32),
        "out_weight": gaussian(streams_of[7], (LAYERS, D, D), (max(8, D // 32)) ** -0.5, 1.25, ((0, 2), (1, 2))),
        "out_bias": gaussian(streams_of[8], (LAYERS, D), 0.3, 2.0, ((0, 2),), jnp.float32),
        "ln2_gain": jnp.clip(1.0 + 0.18 * jax.random.normal(streams_of[9], (LAYERS, D), jnp.float32), 0.1, 1.9),
        "ln2_bias": gaussian(streams_of[10], (LAYERS, D), 0.3, 2.0, ((0, 2),), jnp.float32),
        "fc1_weight": gaussian(streams_of[11], (LAYERS, D, FF), D ** -0.5, 0.21875, ((0, 2), (2, 2))),
        "fc1_bias": gaussian(streams_of[12], (LAYERS, FF), 0.3, 2.0, ((0, 2), (1, 2)), jnp.float32),
        "fc2_weight": gaussian(streams_of[13], (LAYERS, FF, D), FF ** -0.5, 0.109375, ((0, 2), (1, 2))),
        "fc2_bias": gaussian(streams_of[14], (LAYERS, D), 0.3, 2.0, ((0, 2),), jnp.float32),
    }


EPS = 1e-05
NEG = -1e+30
HIGHEST = lax.Precision.HIGHEST

@jax.custom_vjp
def low(v):
    return lax.optimization_barrier(v.astype(jnp.bfloat16)).astype(jnp.float32)

@jax.custom_vjp
def low_back(v):
    return v

def low_keep(v):
    return (low(v), None)

def low_pass(kept, grad):
    return (grad,)

def back_keep(v):
    return (v, None)

def back_low(kept, grad):
    return (low(grad),)
low.defvjp(low_keep, low_pass)
low_back.defvjp(back_keep, back_low)

def layer_norm(values, gain, shift):
    mean = lax.optimization_barrier(jnp.mean(values, axis=-1, keepdims=True))
    centred = values - mean
    spread = lax.optimization_barrier(jnp.mean(centred * centred, axis=-1, keepdims=True))
    return centred * lax.rsqrt(spread + EPS) * gain + shift

def doc_number(positions, lengths):
    bounds = jnp.cumsum(lengths, dtype=jnp.int32)
    return lax.optimization_barrier(jnp.sum((positions[:, None] >= bounds[None, :]).astype(jnp.int32), axis=1, dtype=jnp.int32))

def attention(query, keys, values, lengths):
    positions = jnp.arange(TOKENS, dtype=jnp.int32)
    docs = doc_number(positions, lengths)
    rows = math.gcd(512, TOKENS)
    count = TOKENS // rows

    def one_block(item):
        block_query, block_pos, block_doc = item
        scores = jnp.einsum('qhd,khd->hqk', block_query, keys, precision=HIGHEST) * HEAD_DIM ** (-0.5)
        scores = low_back(scores)
        allowed = (docs[None, :] == block_doc[:, None]) & (positions[None, :] <= block_pos[:, None])
        scores = jnp.where(allowed[None], scores, NEG)
        probs = low(jax.nn.softmax(scores, axis=-1))
        return jnp.einsum('hqk,khd->qhd', probs, values, precision=HIGHEST)
    blocks = (query.reshape(count, rows, HEADS, HEAD_DIM), positions.reshape(count, rows), docs.reshape(count, rows))
    result = lax.map(jax.checkpoint(one_block), blocks)
    return result.reshape(TOKENS, HEADS * HEAD_DIM)

def layer(inputs, weights, lengths):
    gain_one, bias_one, qkv_w, qv_b, out_w, out_b, gain_two, bias_two, up_w, up_b, down_w, down_b = weights
    normed = low(layer_norm(inputs, gain_one, bias_one))
    projected = jnp.dot(normed, qkv_w.reshape(D, 3 * D), precision=HIGHEST).reshape(TOKENS, 3, D)
    query = low_back(low(projected[:, 0] + qv_b[0]))
    keys = low_back(low(projected[:, 1]))
    values = low_back(low(projected[:, 2] + qv_b[1]))
    shape = (TOKENS, HEADS, HEAD_DIM)
    attended = attention(query.reshape(shape), keys.reshape(shape), values.reshape(shape), lengths)
    attended = low_back(low(attended))
    branch = low_back(jnp.dot(attended, out_w, precision=HIGHEST) + out_b)
    middle = inputs + branch
    normed_two = low(layer_norm(middle, gain_two, bias_two))
    hidden_pre = low_back(jnp.dot(normed_two, up_w, precision=HIGHEST) + up_b)
    hidden_low = low(jax.nn.gelu(hidden_pre))
    return middle + low_back(jnp.dot(hidden_low, down_w, precision=HIGHEST) + down_b)

def reference(block_input, out_grad, doc_lengths, ln1_gain, ln1_bias, qkv_weight, qv_bias, out_weight, out_bias, ln2_gain, ln2_bias, fc1_weight, fc1_bias, fc2_weight, fc2_bias):
    params = tuple((p.astype(jnp.float32) for p in (ln1_gain, ln1_bias, qkv_weight, qv_bias, out_weight, out_bias, ln2_gain, ln2_bias, fc1_weight, fc1_bias, fc2_weight, fc2_bias)))
    inputs = block_input.astype(jnp.float32)
    offsets = jnp.zeros(inputs.shape, jnp.float32)

    def forward(inputs, offsets, params):
        first_layer = tuple((p[0] for p in params))
        second_layer = tuple((p[1] for p in params))
        hiddens = []
        finals = []
        for micro in range(MB):
            hidden = low(layer(inputs[micro], first_layer, doc_lengths[micro]))
            hiddens.append(hidden)
            passed = low_back(hidden + offsets[micro])
            finals.append(layer(passed, second_layer, doc_lengths[micro]))
        return (jnp.stack(hiddens), jnp.stack(finals))
    (hiddens, finals), back = jax.vjp(forward, inputs, offsets, params)
    input_grad, hidden_grad, grads = back((jnp.zeros_like(hiddens), out_grad.astype(jnp.float32)))
    layer_outputs = jnp.stack([hiddens, finals]).astype(jnp.bfloat16)
    layer_grads = jnp.stack([input_grad, hidden_grad]).astype(jnp.bfloat16)
    return (layer_outputs, layer_grads, grads[0], grads[1], grads[2], grads[3], grads[4], grads[5], grads[6], grads[7], grads[8], grads[9], grads[10], grads[11])
```

```python
import math
from functools import partial

import jax
import jax.numpy as jnp
from jax import lax
from jax.experimental import pallas as pl
from jax.experimental.pallas import tpu as pltpu
from jax.sharding import PartitionSpec as P

HEAD_DIM = 64


EPS = 1e-05
NEG = -1e30


def passed_along(block, axis, distance):
    devices = range(lax.axis_size(axis))
    route = [(i - distance, i) for i in devices if i - distance in devices]
    return lax.ppermute(block, axis, route)


def layer_norm(values, gain, shift):
    mean = jnp.mean(values, axis=-1, keepdims=True)
    centred = values - mean
    spread = jnp.mean(centred * centred, axis=-1, keepdims=True)
    return centred * lax.rsqrt(spread + EPS) * gain + shift


def doc_number(positions, lengths):
    bounds = jnp.cumsum(lengths, dtype=jnp.int32)
    return jnp.sum(
        (positions[:, None] >= bounds[None, :]).astype(jnp.int32), axis=1, dtype=jnp.int32
    )


def block_width(total, tok_rows):
    return math.gcd(total // tok_rows, max(1, 1024 // tok_rows)) * tok_rows


def block_scores(query, keys, query_pos, query_doc, key_start, lengths):
    count = keys.shape[0]
    scores = jnp.einsum(
        "thd,khd->htk", query, keys, preferred_element_type=jnp.float32
    ) * HEAD_DIM ** (-0.5)
    key_pos = key_start + jnp.arange(count, dtype=jnp.int32)
    key_doc = doc_number(key_pos, lengths)
    allowed = (key_doc[None, :] == query_doc[:, None]) & (key_pos[None, :] <= query_pos[:, None])
    return (scores, allowed[None])


def split_pair(block, heads):
    count = block.shape[0]
    return (
        block[:, 0].reshape(count, heads, HEAD_DIM),
        block[:, 1].reshape(count, heads, HEAD_DIM),
    )


def attend(query, kv_all, query_pos, query_doc, lengths):
    rows, heads = (query.shape[0], query.shape[1])
    width = block_width(kv_all.shape[0], rows)
    blocks = kv_all.reshape(kv_all.shape[0] // width, width, 2, kv_all.shape[2])
    starts = jnp.arange(blocks.shape[0], dtype=jnp.int32) * width

    def total_step(carry, item):
        top, mass = carry
        block, start = item
        keys, values = split_pair(block, heads)
        scores, allowed = block_scores(query, keys, query_pos, query_doc, start, lengths)
        masked = jnp.where(allowed, scores, NEG)
        new_top = jnp.maximum(top, jnp.max(masked, axis=-1))
        weights = jnp.where(allowed, jnp.exp(masked - new_top[..., None]), 0.0)
        return ((new_top, mass * jnp.exp(top - new_top) + jnp.sum(weights, axis=-1)), None)

    start_carry = (jnp.full((heads, rows), NEG, jnp.float32), jnp.zeros((heads, rows), jnp.float32))
    (top, mass), _ = lax.scan(total_step, start_carry, (blocks, starts))
    log_total = top + jnp.log(mass)

    def value_step(running, item):
        block, start = item
        keys, values = split_pair(block, heads)
        scores, allowed = block_scores(query, keys, query_pos, query_doc, start, lengths)
        probs = jnp.where(allowed, jnp.exp(scores - log_total[..., None]), 0.0).astype(jnp.bfloat16)
        return (
            running + jnp.einsum("htk,khd->thd", probs, values, preferred_element_type=jnp.float32),
            None,
        )

    mixed, _ = lax.scan(
        value_step, jnp.zeros((rows, heads, HEAD_DIM), jnp.float32), (blocks, starts)
    )
    return (mixed, log_total)


def tensor_total(partial_value):
    return lax.psum(partial_value.astype(jnp.bfloat16), "tensor").astype(jnp.float32)


def tensor_back(partial_value):
    return lax.psum(partial_value.astype(jnp.bfloat16), "tensor").astype(jnp.float32)


def forward_layer(inputs, lengths, weights):
    (
        gain_one,
        bias_one,
        qkv_w,
        qv_b,
        out_w,
        out_b,
        gain_two,
        bias_two,
        up_w,
        up_b,
        down_w,
        down_b,
    ) = weights
    rows, width = inputs.shape
    inner = qkv_w.shape[2]
    heads = inner // HEAD_DIM
    normed = layer_norm(inputs, gain_one, bias_one).astype(jnp.bfloat16)
    projected = jnp.dot(
        normed, qkv_w.reshape(width, 3 * inner), preferred_element_type=jnp.float32
    ).reshape(rows, 3, inner)
    query = (projected[:, 0] + qv_b[0]).astype(jnp.bfloat16)
    keys = projected[:, 1].astype(jnp.bfloat16)
    values = (projected[:, 2] + qv_b[1]).astype(jnp.bfloat16)
    kv_pair = jnp.stack([keys, values], axis=1)
    kv_all = lax.all_gather(kv_pair, "seq", axis=0, tiled=True)
    query_pos = lax.axis_index("seq") * rows + jnp.arange(rows, dtype=jnp.int32)
    query_doc = doc_number(query_pos, lengths)
    mixed, log_total = attend(
        query.reshape(rows, heads, HEAD_DIM), kv_all, query_pos, query_doc, lengths
    )
    attended = mixed.reshape(rows, inner)
    attended_low = attended.astype(jnp.bfloat16)
    branch = tensor_total(jnp.dot(attended_low, out_w, preferred_element_type=jnp.float32)) + out_b
    middle = inputs + branch
    normed_two = layer_norm(middle, gain_two, bias_two).astype(jnp.bfloat16)
    hidden_pre = jnp.dot(normed_two, up_w, preferred_element_type=jnp.float32) + up_b
    hidden_low = jax.nn.gelu(hidden_pre).astype(jnp.bfloat16)
    result = middle + (
        tensor_total(jnp.dot(hidden_low, down_w, preferred_element_type=jnp.float32)) + down_b
    )
    kept = (
        inputs,
        normed,
        query,
        kv_pair,
        attended,
        log_total,
        middle,
        normed_two,
        hidden_pre,
        hidden_low,
        lengths,
        query_pos,
        query_doc,
    )
    return (result, kept)


def backward_layer(grad_out, kept, weights):
    (
        gain_one,
        bias_one,
        qkv_w,
        qv_b,
        out_w,
        out_b,
        gain_two,
        bias_two,
        up_w,
        up_b,
        down_w,
        down_b,
    ) = weights
    (
        inputs,
        normed,
        query,
        kv_pair,
        attended,
        log_total,
        middle,
        normed_two,
        hidden_pre,
        hidden_low,
        lengths,
        query_pos,
        query_doc,
    ) = kept[:13]
    kv_all = lax.all_gather(kv_pair, "seq", axis=0, tiled=True)
    single = jnp.float32
    rows, inner = attended.shape
    heads = inner // HEAD_DIM
    scale = HEAD_DIM ** (-0.5)
    down_in = grad_out.astype(jnp.bfloat16)
    down_b_grad = jnp.sum(down_in.astype(single), axis=0)
    down_w_grad = jnp.einsum("tf,td->fd", hidden_low, down_in, preferred_element_type=single)
    hidden_grad = jnp.einsum("td,fd->tf", down_in, down_w, preferred_element_type=single)
    _, gelu_back = jax.vjp(jax.nn.gelu, hidden_pre)
    pre_grad = gelu_back(hidden_grad)[0].astype(jnp.bfloat16)
    up_b_grad = jnp.sum(pre_grad.astype(single), axis=0)
    up_w_grad = jnp.einsum("td,tf->df", normed_two, pre_grad, preferred_element_type=single)
    normed_two_grad = tensor_back(
        jnp.einsum("tf,df->td", pre_grad, up_w, preferred_element_type=single)
    )
    _, norm_two_back = jax.vjp(layer_norm, middle, gain_two, bias_two)
    middle_extra, gain_two_grad, bias_two_grad = norm_two_back(normed_two_grad)
    middle_grad = grad_out + middle_extra
    branch_grad = middle_grad.astype(jnp.bfloat16)
    out_b_grad = jnp.sum(branch_grad.astype(single), axis=0)
    out_w_grad = jnp.einsum(
        "th,td->hd", attended.astype(jnp.bfloat16), branch_grad, preferred_element_type=single
    )
    attended_grad = jnp.einsum(
        "td,hd->th", branch_grad, out_w, preferred_element_type=single
    ).astype(jnp.bfloat16)
    grad_heads = attended_grad.reshape(rows, heads, HEAD_DIM)
    query_heads = query.reshape(rows, heads, HEAD_DIM)
    dot_total = jnp.sum(
        grad_heads.astype(single) * attended.reshape(rows, heads, HEAD_DIM), axis=-1
    ).T
    total = kv_all.shape[0]
    width = block_width(total, rows)
    blocks = kv_all.reshape(total // width, width, 2, inner)
    starts = jnp.arange(total // width, dtype=jnp.int32) * width

    def score_grads(block, start):
        keys, values = split_pair(block, heads)
        scores, allowed = block_scores(query_heads, keys, query_pos, query_doc, start, lengths)
        probs = jnp.where(allowed, jnp.exp(scores - log_total[..., None]), 0.0)
        prob_grad = jnp.einsum("thd,khd->htk", grad_heads, values, preferred_element_type=single)
        score_grad = jnp.where(allowed, probs * (prob_grad - dot_total[..., None]), 0.0).astype(
            jnp.bfloat16
        )
        return (keys, probs, score_grad)

    def joined_step(running, item):
        block, start = item
        keys, probs, score_grad = score_grads(block, start)
        running = running + jnp.einsum(
            "htk,khd->thd", score_grad, keys, preferred_element_type=single
        )
        key_grad = (
            jnp.einsum("htk,thd->khd", score_grad, query_heads, preferred_element_type=single)
            * scale
        )
        value_grad = jnp.einsum(
            "htk,thd->khd", probs.astype(jnp.bfloat16), grad_heads, preferred_element_type=single
        )
        return (
            running,
            jnp.stack([key_grad.reshape(width, inner), value_grad.reshape(width, inner)], axis=1),
        )

    query_acc, terms = lax.scan(
        joined_step, jnp.zeros((rows, heads, HEAD_DIM), single), (blocks, starts)
    )
    terms_all = terms.reshape(total, 2, inner)
    pair_grad = lax.psum_scatter(terms_all, "seq", scatter_dimension=0, tiled=True).astype(
        jnp.bfloat16
    )
    query_grad = (query_acc * scale).reshape(rows, inner).astype(jnp.bfloat16)
    proj_grad = jnp.concatenate([query_grad[:, None], pair_grad], axis=1)
    qv_b_grad = jnp.stack(
        [
            jnp.sum(query_grad.astype(single), axis=0),
            jnp.sum(pair_grad[:, 1].astype(single), axis=0),
        ]
    )
    qkv_w_grad = jnp.einsum("td,tch->dch", normed, proj_grad, preferred_element_type=single)
    normed_grad = tensor_back(
        jnp.einsum("tch,dch->td", proj_grad, qkv_w, preferred_element_type=single)
    )
    _, norm_one_back = jax.vjp(layer_norm, inputs, gain_one, bias_one)
    input_extra, gain_one_grad, bias_one_grad = norm_one_back(normed_grad)
    input_grad = middle_grad + input_extra
    grads = (
        gain_one_grad,
        bias_one_grad,
        qkv_w_grad,
        qv_b_grad,
        out_w_grad,
        out_b_grad,
        gain_two_grad,
        bias_two_grad,
        up_w_grad,
        up_b_grad,
        down_w_grad,
        down_b_grad,
    )
    return (input_grad, grads)


def local(
    block_input,
    out_grad,
    doc_lengths,
    ln1_gain,
    ln1_bias,
    qkv_weight,
    qv_bias,
    out_weight,
    out_bias,
    ln2_gain,
    ln2_bias,
    fc1_weight,
    fc1_bias,
    fc2_weight,
    fc2_bias,
):
    weights = (
        ln1_gain[0],
        ln1_bias[0],
        qkv_weight[0],
        qv_bias[0],
        out_weight[0],
        out_bias[0],
        ln2_gain[0],
        ln2_bias[0],
        fc1_weight[0],
        fc1_bias[0],
        fc2_weight[0],
        fc2_bias[0],
    )
    micro_count = block_input.shape[0]
    first = lax.axis_index("section") == 0
    received = jnp.zeros(block_input.shape[1:], jnp.bfloat16)
    outputs = []
    stored = []
    for tick in range(micro_count + 1):
        own = min(tick, micro_count - 1)
        prior = max(tick - 1, 0)
        layer_in = jnp.where(first, block_input[own], received).astype(jnp.float32)
        lengths = jnp.where(first, doc_lengths[own], doc_lengths[prior])
        result, kept = forward_layer(layer_in, lengths, weights)
        result_low = result.astype(jnp.bfloat16)
        outputs.append(result_low)
        stored.append(kept)
        received = passed_along(result_low, "section", 1)
    layer_out = jnp.stack(
        [jnp.where(first, outputs[m], outputs[m + 1]) for m in range(micro_count)]
    )
    totals = jax.tree.map(lambda w: jnp.zeros(w.shape, jnp.float32), weights)
    returned = jnp.zeros(block_input.shape[1:], jnp.bfloat16)
    input_grads = []
    for tick in range(micro_count + 1):
        mine = min(tick, micro_count - 1)
        valid = jnp.where(first, float(tick >= 1), float(tick < micro_count)).astype(jnp.float32)
        upstream = jnp.where(first, returned, out_grad[mine]).astype(jnp.float32)
        kept = jax.tree.map(
            lambda early, late: jnp.where(first, early, late),
            stored[max(tick - 1, 0)],
            stored[min(tick + 1, micro_count)],
        )
        input_grad, grads = backward_layer(upstream, kept, weights)
        totals = jax.tree.map(lambda total, grad: total + valid * grad, totals, grads)
        grad_low = input_grad.astype(jnp.bfloat16)
        input_grads.append(grad_low)
        returned = passed_along(grad_low, "section", -1)
    layer_grad = jnp.stack(
        [jnp.where(first, input_grads[m + 1], input_grads[m]) for m in range(micro_count)]
    )
    (
        gain_one_sum,
        bias_one_sum,
        qkv_sum,
        qv_sum,
        out_w_sum,
        out_b_sum,
        gain_two_sum,
        bias_two_sum,
        up_w_sum,
        up_b_sum,
        down_w_sum,
        down_b_sum,
    ) = totals
    summed = (
        lax.psum_scatter(gain_one_sum, "seq", scatter_dimension=0, tiled=True),
        lax.psum_scatter(bias_one_sum, "seq", scatter_dimension=0, tiled=True),
        lax.psum_scatter(qkv_sum, "seq", scatter_dimension=0, tiled=True),
        lax.psum_scatter(qv_sum, "seq", scatter_dimension=1, tiled=True),
        lax.psum_scatter(out_w_sum, "seq", scatter_dimension=0, tiled=True),
        lax.psum_scatter(out_b_sum, "seq", scatter_dimension=0, tiled=True),
        lax.psum_scatter(gain_two_sum, "seq", scatter_dimension=0, tiled=True),
        lax.psum_scatter(bias_two_sum, "seq", scatter_dimension=0, tiled=True),
        lax.psum_scatter(up_w_sum, "seq", scatter_dimension=0, tiled=True),
        lax.psum_scatter(up_b_sum, "seq", scatter_dimension=0, tiled=True),
        lax.psum_scatter(down_w_sum, "seq", scatter_dimension=0, tiled=True),
        lax.psum_scatter(down_b_sum, "seq", scatter_dimension=0, tiled=True),
    )
    return (
        layer_out[None],
        layer_grad[None],
        summed[0][None],
        summed[1][None],
        summed[2][None],
        summed[3][None],
        summed[4][None],
        summed[5][None],
        summed[6][None],
        summed[7][None],
        summed[8][None],
        summed[9][None],
        summed[10][None],
        summed[11][None],
    )


def swapped_cores(block):
    return lax.ppermute(block, "tensor", [(0, 1), (1, 0)])


def swapped_groups(block):
    return lax.ppermute(block, "seq", [(i, i ^ 1) for i in range(lax.axis_size("seq"))])


def held(value, *others):
    return lax.optimization_barrier((value, *others))[0]


def picked(block, which, axis):
    return lax.dynamic_index_in_dim(block, which, axis, keepdims=False)


def in_order(mine, other, place, axis):
    return jnp.where(
        place == 0, jnp.stack([mine, other], axis=axis), jnp.stack([other, mine], axis=axis)
    )


def micro_routes(count):
    groups = lax.axis_size("seq") // count
    return [
        [
            (m * groups + g, (m + step) % count * groups + g)
            for m in range(count)
            for g in range(groups)
        ]
        for step in range(1, count)
    ]


def across_micros(blocks, micro, count):
    parts = [picked(blocks, micro, 0)]
    for step, route in enumerate(micro_routes(count), 1):
        parts.append(lax.ppermute(picked(blocks, (micro + step) % count, 0), "seq", route))
    turned = jnp.stack([parts[0]] + parts[:0:-1], axis=0)
    return lax.dynamic_slice_in_dim(
        jnp.concatenate([turned, turned], axis=0), (count - micro) % count, count, axis=0
    )


def micro_total(blocks, micro, count):
    total = picked(blocks, micro, 0).astype(jnp.float32)
    for step, route in enumerate(micro_routes(count), 1):
        got = lax.ppermute(picked(blocks, (micro + step) % count, 0), "seq", route)
        total = total + got.astype(jnp.float32)
    return total


def both_cores(half, core):
    full = in_order(half, swapped_cores(half), core, 1)
    return full.reshape(half.shape[0], -1, half.shape[-1])


SINGLE = jnp.float32
LOW = jnp.bfloat16
Q_ROWS = 256
NT = (((1,), (1,)), ((), ()))
TN = (((0,), (0,)), ((), ()))
SCALARS = pl.BlockSpec(memory_space=pltpu.SMEM)
WHOLE = pl.BlockSpec(memory_space=pltpu.VMEM)


def kernel_call(body, name, shapes, scalars, arrays, flops, scratch=()):
    outs = [jax.ShapeDtypeStruct(shape, dtype) for shape, dtype in shapes]
    moved = sum(math.prod(a.shape) * a.dtype.itemsize for a in (*arrays, *outs))
    return pl.pallas_call(
        body,
        out_shape=outs,
        in_specs=[SCALARS] + [WHOLE] * len(arrays),
        out_specs=[WHOLE] * len(outs),
        scratch_shapes=list(scratch),
        compiler_params=pltpu.CompilerParams(vmem_limit_bytes=32 * 1024 * 1024),
        cost_estimate=pl.CostEstimate(flops=flops, bytes_accessed=moved, transcendentals=0),
        name=name,
    )(scalars, *arrays)


def row_norm(values):
    mean = jnp.mean(values, axis=-1, keepdims=True)
    centred = values - mean
    inverse = lax.rsqrt(jnp.mean(centred * centred, axis=-1, keepdims=True) + EPS)
    return centred * inverse, inverse


def norm_back(shaped, inverse, scaled):
    return inverse * (
        scaled
        - jnp.mean(scaled, axis=-1, keepdims=True)
        - shaped * jnp.mean(scaled * shaped, axis=-1, keepdims=True)
    )


def either(place, mine, other):
    return jnp.where(place == 0, mine, other), jnp.where(place == 0, other, mine)


def column_sum(values):
    return jnp.sum(values, axis=0, keepdims=True)


def norm_kernel(place_ref, x_ref, gain_ref, bias_ref, out_ref):
    for block in range(x_ref.shape[0]):
        shaped, _ = row_norm(x_ref[block].astype(SINGLE))
        out_ref[block] = (shaped * gain_ref[...] + bias_ref[...]).astype(LOW)


def doc_mask(place_ref, docs, first, rows, count):
    key_pos = lax.broadcasted_iota(jnp.int32, (rows, count), 1)
    query_pos = first + lax.broadcasted_iota(jnp.int32, (rows, 1), 0)
    start = jnp.zeros((rows, 1), jnp.int32)
    bound = jnp.int32(0)
    for doc in range(docs):
        bound = bound + place_ref[2 + doc]
        start = jnp.maximum(start, jnp.where(query_pos >= bound, bound, 0))
    return (key_pos <= query_pos) & (key_pos >= start)


def attend_kernel(heads, docs, kept, place_ref, mine_ref, core_ref, group_ref, far_ref, w_ref, b_ref, out_ref, send_ref, *rest):
    qkv_ref, n_ref, lse_ref = rest
    core, group = place_ref[0], place_ref[1]
    blocks, half, width = mine_ref.shape
    rows = 4 * half
    inner = heads * HEAD_DIM
    for block in range(blocks):
        near = either(core, mine_ref[block], core_ref[block])
        far = either(core, group_ref[block], far_ref[block])
        near, far = jnp.concatenate(near, axis=0), jnp.concatenate(far, axis=0)
        n_ref[block * rows : (block + 1) * rows, :] = jnp.concatenate(
            either(group, near, far), axis=0
        )
    for i in range(0, blocks * rows, rows):
        made = jnp.dot(n_ref[i : i + rows, :], w_ref[...], preferred_element_type=SINGLE)
        qkv_ref[i : i + rows, :] = (made + b_ref[...]).astype(LOW)
    lane = lax.broadcasted_iota(jnp.int32, (rows, 128), 1)
    for block in range(blocks):
        i = block * rows
        count = i + rows
        allowed = doc_mask(place_ref, docs, i, rows, count)
        totals = jnp.zeros((rows, 128), SINGLE)
        mixed = []
        for h in range(heads):
            at = h * HEAD_DIM
            query = qkv_ref[i:count, at : at + HEAD_DIM] * LOW(HEAD_DIM**-0.5)
            keys = qkv_ref[:count, inner + at : inner + at + HEAD_DIM]
            values = qkv_ref[:count, 2 * inner + at : 2 * inner + at + HEAD_DIM]
            scores = lax.dot_general(query, keys, NT, preferred_element_type=SINGLE)
            scores = jnp.where(allowed, scores, NEG)
            top = jnp.max(scores, axis=1, keepdims=True)
            weights = jnp.exp(scores - top)
            mass = jnp.sum(weights, axis=1, keepdims=True)
            probs = (weights * (1.0 / mass)).astype(LOW)
            mixed.append(jnp.dot(probs, values, preferred_element_type=SINGLE))
            totals = jnp.where(lane == h, top + jnp.log(mass), totals)
        out = jnp.concatenate(mixed, axis=1).astype(LOW)
        out_ref[block], send_ref[block] = either(group, out[: rows // 2], out[rows // 2 :])
        if kept:
            lse_ref[i:count, :] = totals


def attend_back_kernel(heads, docs, last, place_ref, qkv_ref, n_ref, w_ref, do_ref, do_far_ref, out_ref, send_ref, lse_ref, keep_ref, give_ref, *rest):
    if last:
        dw_ref, db_ref, acc_ref = rest
    else:
        (acc_ref,) = rest
    core, group = place_ref[0], place_ref[1]
    blocks = out_ref.shape[0]
    tokens = n_ref.shape[0]
    rows = tokens // blocks
    inner = heads * HEAD_DIM
    for block in range(blocks - 1, -1, -1):
        i = block * rows
        count = i + rows
        allowed = doc_mask(place_ref, docs, i, rows, count)
        grads = jnp.concatenate(either(group, do_ref[block], do_far_ref[block]), axis=0)
        outs = jnp.concatenate(either(group, out_ref[block], send_ref[block]), axis=0)
        for h in range(heads):
            at = h * HEAD_DIM
            query = qkv_ref[i:count, at : at + HEAD_DIM] * LOW(HEAD_DIM**-0.5)
            keys = qkv_ref[:count, inner + at : inner + at + HEAD_DIM]
            values = qkv_ref[:count, 2 * inner + at : 2 * inner + at + HEAD_DIM]
            grad = grads[:, at : at + HEAD_DIM]
            out = outs[:, at : at + HEAD_DIM]
            dots = jnp.sum(grad.astype(SINGLE) * out.astype(SINGLE), axis=1, keepdims=True)
            scores = lax.dot_general(query, keys, NT, preferred_element_type=SINGLE)
            probs = jnp.exp(jnp.where(allowed, scores, NEG) - lse_ref[i:count, h : h + 1])
            prob_grad = lax.dot_general(grad, values, NT, preferred_element_type=SINGLE)
            score_grad = (probs * (prob_grad - dots)).astype(LOW)
            query_grad = jnp.dot(score_grad, keys, preferred_element_type=SINGLE)
            acc_ref[at : at + HEAD_DIM, i:count] = query_grad.T * HEAD_DIM**-0.5
            at += inner
            key_grad = jnp.dot(query.T, score_grad, preferred_element_type=SINGLE)
            value_grad = jnp.dot(grad.T, probs.astype(LOW), preferred_element_type=SINGLE)
            if block == blocks - 1:
                acc_ref[at : at + HEAD_DIM, :] = key_grad
                acc_ref[at + inner : at + inner + HEAD_DIM, :] = value_grad
            else:
                acc_ref[at : at + HEAD_DIM, :count] += key_grad
                acc_ref[at + inner : at + inner + HEAD_DIM, :count] += value_grad
    for block in range(blocks):
        i = block * rows
        part = acc_ref[:, i : i + rows].T.astype(LOW)
        made = lax.dot_general(part, w_ref[...], NT, preferred_element_type=SINGLE).astype(LOW)
        near, far = either(group, made[: rows // 2], made[rows // 2 :])
        for place, side in ((0, near), (1, far)):
            keep_ref[place, block], give_ref[place, block] = either(
                core, side[: rows // 4], side[rows // 4 :]
            )
    if last:
        low = acc_ref[...].astype(LOW)
        dw_ref[...] = jnp.dot(low, n_ref[...], preferred_element_type=SINGLE).T.astype(LOW)
        sums = jnp.sum(low.astype(SINGLE), axis=1, keepdims=True)
        db_ref[...] = jnp.broadcast_to(sums, db_ref.shape)


def project_kernel(place_ref, mine_ref, far_ref, w_ref, out_ref):
    group = place_ref[1]
    own = mine_ref.shape[1]
    near_w = w_ref[pl.ds(pl.multiple_of(group * own, own), own), :]
    far_w = w_ref[pl.ds(pl.multiple_of((1 - group) * own, own), own), :]
    out_ref[...] = (
        jnp.dot(mine_ref[...], near_w, preferred_element_type=SINGLE)
        + jnp.dot(far_ref[...], far_w, preferred_element_type=SINGLE)
    ).astype(LOW)


def halves(core, mine_ref, other_ref, block):
    return jnp.concatenate(either(core, mine_ref[block], other_ref[block]), axis=0)


def feed_kernel(kept, place_ref, x_ref, x_far_ref, part_ref, far_ref, out_b_ref, gain_ref, bias_ref, up_ref, up_b_ref, down_ref, down_b_ref, base_ref, give_ref, *rest):
    core = place_ref[0]
    blocks, half, _ = x_ref.shape
    step = 2 * half
    for first in range(0, blocks, 2):
        rows = slice(first * step, (first + 2) * step)
        x = jnp.concatenate(
            [halves(core, x_ref, x_far_ref, block) for block in (first, first + 1)], axis=0
        )
        middle = (
            x.astype(SINGLE)
            + (part_ref[rows, :].astype(SINGLE) + far_ref[rows, :].astype(SINGLE))
            + out_b_ref[...]
        )
        shaped, _ = row_norm(middle)
        normed = (shaped * gain_ref[...] + bias_ref[...]).astype(LOW)
        pre = jnp.dot(normed, up_ref[...], preferred_element_type=SINGLE) + up_b_ref[...]
        hidden = jax.nn.gelu(pre).astype(LOW)
        made = jnp.dot(hidden, down_ref[...], preferred_element_type=SINGLE)
        if kept:
            middle_ref, normed_ref, pre_ref, hidden_ref = rest
            middle_ref[rows, :] = middle
            normed_ref[rows, :] = normed
            pre_ref[rows, :] = pre
            hidden_ref[rows, :] = hidden
        for place in (0, 1):
            at = place * step
            mine, other = either(core, made[at : at + half], made[at + half : at + step])
            own = jnp.where(core == 0, middle[at : at + half], middle[at + half : at + step])
            base_ref[first + place] = own + mine + down_b_ref[...]
            give_ref[first + place] = other.astype(LOW)


def gelu_slope(value):
    rate = math.sqrt(2.0 / math.pi)
    squared = value * value
    bent = jnp.tanh(rate * value * (1.0 + 0.044715 * squared))
    return 0.5 * (1.0 + bent) + 0.5 * value * (1.0 - bent * bent) * (
        rate * (1.0 + 3 * 0.044715 * squared)
    )


def feed_back_kernel(last, place_ref, dy_ref, dy_far_ref, pre_ref, up_ref, down_ref, part_ref, dz_ref, *rest):
    core = place_ref[0]
    blocks, half, _ = dy_ref.shape
    step = 2 * half
    up_sum, down_sum = 0.0, 0.0
    for first in range(0, blocks, 2):
        rows = slice(first * step, (first + 2) * step)
        dz = jnp.concatenate(
            [halves(core, dy_ref, dy_far_ref, block) for block in (first, first + 1)], axis=0
        )
        dz_ref[rows, :] = dz
        grad = lax.dot_general(dz, down_ref[...], NT, preferred_element_type=SINGLE)
        pre_grad = (grad * gelu_slope(pre_ref[rows, :])).astype(LOW)
        part_ref[rows, :] = lax.dot_general(
            pre_grad, up_ref[...], NT, preferred_element_type=SINGLE
        ).astype(LOW)
        if last:
            rest[0][rows, :] = pre_grad
            up_sum = up_sum + column_sum(pre_grad.astype(SINGLE))
            down_sum = down_sum + column_sum(dz.astype(SINGLE))
    if last:
        rest[1][...] = up_sum
        rest[2][...] = down_sum


def project_back_kernel(last, place_ref, dz_ref, middle_ref, part_ref, far_ref, gain_ref, w_ref, mine_ref, give_ref, half_ref, *rest):
    core, group = place_ref[0], place_ref[1]
    own = mine_ref.shape[1]
    blocks, half, _ = half_ref.shape
    step = 2 * half
    near_w = w_ref[pl.ds(pl.multiple_of(group * own, own), own), :]
    far_w = w_ref[pl.ds(pl.multiple_of((1 - group) * own, own), own), :]
    sums = [0.0, 0.0, 0.0]
    for first in range(0, blocks, 2):
        rows = slice(first * step, (first + 2) * step)
        shaped, inverse = row_norm(middle_ref[rows, :])
        grad = part_ref[rows, :].astype(SINGLE) + far_ref[rows, :].astype(SINGLE)
        total = dz_ref[rows, :].astype(SINGLE) + norm_back(shaped, inverse, grad * gain_ref[...])
        low = total.astype(LOW)
        mine_ref[rows, :] = lax.dot_general(
            low, near_w, NT, preferred_element_type=SINGLE
        ).astype(LOW)
        give_ref[rows, :] = lax.dot_general(
            low, far_w, NT, preferred_element_type=SINGLE
        ).astype(LOW)
        for place in (0, 1):
            at = place * step
            half_ref[first + place] = jnp.where(
                core == 0, total[at : at + half], total[at + half : at + step]
            )
        if last:
            rest[0][rows, :] = low
            for at, part in enumerate((low.astype(SINGLE), grad * shaped, grad)):
                sums[at] = sums[at] + column_sum(part)
    if last:
        for at in range(3):
            rest[1][at : at + 1, :] = sums[at]


def norm_back_kernel(last, place_ref, x_ref, keep_ref, core_ref, group_ref, rest_ref, gain_ref, dx_ref, *rest):
    sums = [0.0, 0.0]
    for block in range(x_ref.shape[0]):
        shaped, inverse = row_norm(x_ref[block].astype(SINGLE))
        grad = (
            keep_ref[0, block].astype(SINGLE)
            + core_ref[0, block].astype(SINGLE)
            + group_ref[block].astype(SINGLE)
        )
        back = norm_back(shaped, inverse, grad * gain_ref[...])
        dx_ref[block] = (rest_ref[block] + back).astype(LOW)
        if last:
            for at, part in enumerate((grad * shaped, grad)):
                sums[at] = sums[at] + column_sum(part)
    if last:
        for at in range(2):
            rest[0][at : at + 1, :] = sums[at]


def micro_local(
    block_input,
    out_grad,
    doc_lengths,
    ln1_gain,
    ln1_bias,
    qkv_weight,
    qv_bias,
    out_weight,
    out_bias,
    ln2_gain,
    ln2_bias,
    fc1_weight,
    fc1_bias,
    fc2_weight,
    fc2_bias,
):
    micros, rows, width = block_input.shape
    size = lax.axis_size("seq")
    place = lax.axis_index("seq")
    groups = size // micros
    micro, group = place // groups, place % groups
    core = lax.axis_index("tensor")
    first = lax.axis_index("section") == 0
    inner = out_weight.shape[1]
    own = inner // groups
    heads = own // HEAD_DIM
    hidden = fc1_weight.shape[2]
    docs = doc_lengths.shape[1]
    tokens = rows * size
    local_rows = tokens // groups
    half = rows // 2
    out_w, up_w, down_w = out_weight[0], fc1_weight[0], fc2_weight[0]
    qkv_w = picked(qkv_weight[0].reshape(width, 3, groups, own), group, 2).reshape(width, 3 * own)
    qv_own = picked(qv_bias[0].reshape(2, groups, own), group, 1)
    qkv_b = jnp.concatenate([qv_own[0], jnp.zeros((own,), SINGLE), qv_own[1]])[None]
    scalars = jnp.concatenate(
        [jnp.stack([core, group]).astype(jnp.int32), picked(doc_lengths, micro, 0)]
    )
    half_shape = (micros, half, width)
    head_shape = (micros, rows, own)
    dense = 2 * local_rows * width
    pairs = 2 * heads * HEAD_DIM * tokens * tokens * 5 // 8

    def run(body, name, shapes, arrays, flops, scratch=()):
        return kernel_call(body, name, shapes, scalars, arrays, flops, scratch)

    def normed_once(mine):
        return run(
            norm_kernel, "norm", [(half_shape, LOW)], [mine, ln1_gain, ln1_bias], 8 * mine.size
        )[0]

    def forward(mine, kept):
        normed_half = normed_once(mine)
        core_half = swapped_cores(normed_half)
        group_half = swapped_groups(normed_half)
        far_half = swapped_cores(group_half)
        other = swapped_cores(mine)
        made = [((tokens, 3 * own), LOW), ((tokens, width), LOW), ((tokens, 128), SINGLE)]
        out = run(
            partial(attend_kernel, heads, docs, kept),
            "attend",
            [(head_shape, LOW)] * 2 + (made if kept else []),
            [normed_half, core_half, group_half, far_half, qkv_w, qkv_b],
            2 * pairs + dense * 6 * own,
            () if kept else [pltpu.VMEM(*item) for item in made],
        )
        got = swapped_groups(out[1])
        mixed = out[0].reshape(local_rows, own), got.reshape(local_rows, own)
        (part,) = run(
            project_kernel, "project", [((local_rows, width), LOW)], [*mixed, out_w], dense * inner
        )
        far_part = swapped_cores(part)
        saved = [
            ((local_rows, width), SINGLE),
            ((local_rows, width), LOW),
            ((local_rows, hidden), SINGLE),
            ((local_rows, hidden), LOW),
        ]
        base, give, *rest = run(
            partial(feed_kernel, kept),
            "feed",
            [(half_shape, SINGLE), (half_shape, LOW)] + (saved if kept else []),
            [
                mine,
                other,
                part,
                far_part,
                out_bias,
                ln2_gain,
                ln2_bias,
                up_w,
                fc1_bias,
                down_w,
                fc2_bias,
            ],
            2 * dense * hidden,
        )
        result = (base + swapped_cores(give).astype(SINGLE)).astype(LOW)
        return result, (mine, out, mixed, rest)

    def backward(grad_half, stored, last):
        mine, (out_mine, out_send, qkv, normed, totals), mixed, rest = stored
        middle, normed_two, pre, hidden_low = rest
        extra = [((local_rows, hidden), LOW), ((1, hidden), SINGLE), ((1, width), SINGLE)]
        part, dz, *feed_rest = run(
            partial(feed_back_kernel, last),
            "feed_back",
            [((local_rows, width), LOW)] * 2 + (extra if last else []),
            [grad_half, swapped_cores(grad_half), pre, up_w, down_w],
            2 * dense * hidden,
        )
        if last:
            down_grad = lax.dot_general(
                hidden_low, dz, TN, preferred_element_type=SINGLE
            ).astype(LOW)
            down_parts = down_grad.reshape(micros, groups, -1, width)
            cut = width // 2
            down_keep = picked(down_parts, group, 1)
            down_give = picked(down_parts, 1 - group, 1)
            down_got = [swapped_groups(down_give[..., :cut])]
            part = held(part, down_give)
        far_part = swapped_cores(part)
        extra = [((local_rows, width), LOW), ((3, width), SINGLE)]
        do_mine, do_give, rest_half, *project_rest = run(
            partial(project_back_kernel, last),
            "project_back",
            [((local_rows, own), LOW)] * 2 + [(half_shape, SINGLE)] + (extra if last else []),
            [dz, middle, part, far_part, ln2_gain, out_w],
            dense * inner,
        )
        do_got = swapped_groups(do_give)
        extra = [((width, 3 * own), LOW), ((3 * own, 128), SINGLE)]
        keep, give, *attend_rest = run(
            partial(attend_back_kernel, heads, docs, last),
            "attend_back",
            [((2, *half_shape), LOW)] * 2 + (extra if last else []),
            [
                qkv,
                normed,
                qkv_w,
                do_mine.reshape(head_shape),
                do_got.reshape(head_shape),
                out_mine,
                out_send,
                totals,
            ],
            5 * pairs + dense * 6 * own,
            [pltpu.VMEM((3 * own, tokens), SINGLE)],
        )
        core_got = swapped_cores(give)
        group_give = (keep[1].astype(SINGLE) + core_got[1].astype(SINGLE)).astype(LOW)
        group_got = swapped_groups(group_give)
        dx, *norm_rest = run(
            partial(norm_back_kernel, last),
            "norm_back",
            [(half_shape, LOW)] + ([((2, width), SINGLE)] if last else []),
            [mine, keep, core_got, group_got, rest_half, ln1_gain],
            20 * mine.size,
        )
        if not last:
            return dx, None

        def joined(kept, got):
            return (kept.astype(SINGLE) + got.astype(SINGLE)).astype(LOW)

        pre_grad, up_sum, down_sum = feed_rest
        branch, branch_sums = project_rest
        qkv_part, qkv_sums = attend_rest

        up_parts = (
            lax.dot_general(normed_two, pre_grad, TN, preferred_element_type=SINGLE)
            .astype(LOW)
            .reshape(micros, groups, -1, hidden)
        )
        up_cut = hidden // 2
        up_keep = picked(up_parts, group, 1)
        up_give = picked(up_parts, 1 - group, 1)
        down_got.append(swapped_groups(held(down_give[..., cut:], do_got)))
        down_grad = [
            micro_total(joined(down_keep[..., :cut], down_got[0]), micro, micros),
            micro_total(joined(down_keep[..., cut:], down_got[1]), micro, micros),
        ]
        up_give = held(up_give, group_got)
        up_grad = [
            micro_total(joined(up_keep[..., piece], swapped_groups(up_give[..., piece])), micro, micros)
            for piece in (slice(0, up_cut), slice(up_cut, hidden))
        ]

        mixed_w = [
            lax.dot_general(side, branch, TN, preferred_element_type=SINGLE).astype(LOW)
            for side in mixed
        ]
        out_parts = in_order(*mixed_w, group, 0).reshape(size, -1, width)

        sums = qkv_sums[:, 0].reshape(3, own)
        qv_sum = jnp.stack([sums[0], sums[2]])
        qv_sum = in_order(qv_sum, jnp.zeros_like(qv_sum), group, 1).reshape(2, inner)
        one = norm_rest[0]
        one = one + swapped_cores(one)
        vectors = jnp.concatenate(
            [
                part.reshape(-1, size, part.shape[-1] // size).transpose(1, 0, 2).reshape(size, -1)
                for part in (one, branch_sums, down_sum, qv_sum, up_sum)
            ],
            axis=1,
        )
        length = vectors.shape[1]
        lines = -(-length // width)
        lines += -lines % 16
        vectors = jnp.pad(vectors, ((0, 0), (0, lines * width - length)))
        small = jnp.concatenate([vectors.astype(LOW).reshape(size, lines, width), out_parts], axis=1)
        small = small.reshape(micros, groups, -1, width)
        small_total = micro_total(
            joined(
                picked(small, group, 1), swapped_groups(picked(small, 1 - group, 1))
            ),
            micro,
            micros,
        )
        vector = small_total[:lines].reshape(-1)[:length]
        out_w_grad = small_total[lines:]

        qkv_sum = micro_total(qkv_part.reshape(micros, -1, 3 * own), micro, micros).reshape(
            groups, -1, 3, own
        )
        qkv_got = swapped_groups(picked(qkv_sum, 1 - group, 0).astype(LOW)).astype(SINGLE)
        qkv_w_grad = in_order(picked(qkv_sum, group, 0), qkv_got, group, 2).reshape(-1, 3, inner)

        cut = width // size
        rowed = vector[: 6 * cut].reshape(6, cut)
        wide = inner // size
        qv_grad = vector[6 * cut : 6 * cut + 2 * wide].reshape(2, wide)
        up_b_grad = vector[6 * cut + 2 * wide :]
        return dx, (
            rowed[0],
            rowed[1],
            qkv_w_grad,
            qv_grad,
            out_w_grad,
            rowed[2],
            rowed[3],
            rowed[4],
            jnp.concatenate(up_grad, axis=1),
            up_b_grad,
            jnp.concatenate(down_grad, axis=1),
            rowed[5],
        )

    def placed_back(mine):
        return both_cores(across_micros(mine, micro, micros), core)[None]

    begun = jnp.where(first, block_input, out_grad).reshape(micros, 2, half, width)
    begun = across_micros(picked(begun, core, 1), micro, micros)
    early, _ = forward(begun, False)
    received = passed_along(early, "section", 1)
    final, stored = forward(jnp.where(first, begun, received), True)
    early_grad, _ = backward(begun, stored, False)
    returned = passed_along(early_grad, "section", -1)
    final_grad, grads = backward(jnp.where(first, returned, begun), stored, True)
    return (
        placed_back(final),
        placed_back(final_grad),
        *(grad[None] for grad in grads),
    )


def solution(mesh):
    placed = (
        P(None, "seq", None),
        P(None, "seq", None),
        P(),
        P("section", None),
        P("section", None),
        P("section", None, None, "tensor"),
        P("section", None, "tensor"),
        P("section", "tensor", None),
        P("section", None),
        P("section", None),
        P("section", None),
        P("section", None, "tensor"),
        P("section", "tensor"),
        P("section", "tensor", None),
        P("section", None),
    )

    def chosen(*arrays):
        pairs = mesh.shape["seq"] == 2 * arrays[0].shape[0]
        cores = mesh.shape["tensor"] == 2 and mesh.shape["section"] == 2
        heads = arrays[7].shape[1] // HEAD_DIM
        if pairs and cores and heads % 2 == 0:
            return micro_local(*arrays)
        return local(*arrays)

    return jax.shard_map(
        chosen,
        mesh=mesh,
        in_specs=placed,
        out_specs=(
            P("section", None, "seq", None),
            P("section", None, "seq", None),
            P("section", "seq"),
            P("section", "seq"),
            P("section", "seq", None, "tensor"),
            P("section", None, ("tensor", "seq")),
            P("section", ("tensor", "seq"), None),
            P("section", "seq"),
            P("section", "seq"),
            P("section", "seq"),
            P("section", "seq", "tensor"),
            P("section", ("tensor", "seq")),
            P("section", ("tensor", "seq"), None),
            P("section", "seq"),
        ),
        check_vma=False,
    )
```

```python
import math
from functools import partial

import jax
import jax.numpy as jnp
from jax import lax
from jax.experimental import pallas as pl
from jax.experimental.pallas import tpu as pltpu
from jax.sharding import PartitionSpec as P

HEAD_DIM = 64


EPS = 1e-05
NEG = -1e30


def passed_along(block, axis, distance):
    devices = range(lax.axis_size(axis))
    route = [(i - distance, i) for i in devices if i - distance in devices]
    return lax.ppermute(block, axis, route)


def layer_norm(values, gain, shift):
    mean = jnp.mean(values, axis=-1, keepdims=True)
    centred = values - mean
    spread = jnp.mean(centred * centred, axis=-1, keepdims=True)
    return centred * lax.rsqrt(spread + EPS) * gain + shift


def doc_number(positions, lengths):
    bounds = jnp.cumsum(lengths, dtype=jnp.int32)
    return jnp.sum(
        (positions[:, None] >= bounds[None, :]).astype(jnp.int32), axis=1, dtype=jnp.int32
    )


def block_width(total, tok_rows):
    return math.gcd(total // tok_rows, max(1, 1024 // tok_rows)) * tok_rows


def block_scores(query, keys, query_pos, query_doc, key_start, lengths):
    count = keys.shape[0]
    scores = jnp.einsum(
        "thd,khd->htk", query, keys, preferred_element_type=jnp.float32
    ) * HEAD_DIM ** (-0.5)
    key_pos = key_start + jnp.arange(count, dtype=jnp.int32)
    key_doc = doc_number(key_pos, lengths)
    allowed = (key_doc[None, :] == query_doc[:, None]) & (key_pos[None, :] <= query_pos[:, None])
    return (scores, allowed[None])


def split_pair(block, heads):
    count = block.shape[0]
    return (
        block[:, 0].reshape(count, heads, HEAD_DIM),
        block[:, 1].reshape(count, heads, HEAD_DIM),
    )


def attend(query, kv_all, query_pos, query_doc, lengths):
    rows, heads = (query.shape[0], query.shape[1])
    width = block_width(kv_all.shape[0], rows)
    blocks = kv_all.reshape(kv_all.shape[0] // width, width, 2, kv_all.shape[2])
    starts = jnp.arange(blocks.shape[0], dtype=jnp.int32) * width

    def total_step(carry, item):
        top, mass = carry
        block, start = item
        keys, values = split_pair(block, heads)
        scores, allowed = block_scores(query, keys, query_pos, query_doc, start, lengths)
        masked = jnp.where(allowed, scores, NEG)
        new_top = jnp.maximum(top, jnp.max(masked, axis=-1))
        weights = jnp.where(allowed, jnp.exp(masked - new_top[..., None]), 0.0)
        return ((new_top, mass * jnp.exp(top - new_top) + jnp.sum(weights, axis=-1)), None)

    start_carry = (jnp.full((heads, rows), NEG, jnp.float32), jnp.zeros((heads, rows), jnp.float32))
    (top, mass), _ = lax.scan(total_step, start_carry, (blocks, starts))
    log_total = top + jnp.log(mass)

    def value_step(running, item):
        block, start = item
        keys, values = split_pair(block, heads)
        scores, allowed = block_scores(query, keys, query_pos, query_doc, start, lengths)
        probs = jnp.where(allowed, jnp.exp(scores - log_total[..., None]), 0.0).astype(jnp.bfloat16)
        return (
            running + jnp.einsum("htk,khd->thd", probs, values, preferred_element_type=jnp.float32),
            None,
        )

    mixed, _ = lax.scan(
        value_step, jnp.zeros((rows, heads, HEAD_DIM), jnp.float32), (blocks, starts)
    )
    return (mixed, log_total)


def tensor_total(partial_value):
    return lax.psum(partial_value.astype(jnp.bfloat16), "tensor").astype(jnp.float32)


def tensor_back(partial_value):
    return lax.psum(partial_value.astype(jnp.bfloat16), "tensor").astype(jnp.float32)


def forward_layer(inputs, lengths, weights):
    (
        gain_one,
        bias_one,
        qkv_w,
        qv_b,
        out_w,
        out_b,
        gain_two,
        bias_two,
        up_w,
        up_b,
        down_w,
        down_b,
    ) = weights
    rows, width = inputs.shape
    inner = qkv_w.shape[2]
    heads = inner // HEAD_DIM
    normed = layer_norm(inputs, gain_one, bias_one).astype(jnp.bfloat16)
    projected = jnp.dot(
        normed, qkv_w.reshape(width, 3 * inner), preferred_element_type=jnp.float32
    ).reshape(rows, 3, inner)
    query = (projected[:, 0] + qv_b[0]).astype(jnp.bfloat16)
    keys = projected[:, 1].astype(jnp.bfloat16)
    values = (projected[:, 2] + qv_b[1]).astype(jnp.bfloat16)
    kv_pair = jnp.stack([keys, values], axis=1)
    kv_all = lax.all_gather(kv_pair, "seq", axis=0, tiled=True)
    query_pos = lax.axis_index("seq") * rows + jnp.arange(rows, dtype=jnp.int32)
    query_doc = doc_number(query_pos, lengths)
    mixed, log_total = attend(
        query.reshape(rows, heads, HEAD_DIM), kv_all, query_pos, query_doc, lengths
    )
    attended = mixed.reshape(rows, inner)
    attended_low = attended.astype(jnp.bfloat16)
    branch = tensor_total(jnp.dot(attended_low, out_w, preferred_element_type=jnp.float32)) + out_b
    middle = inputs + branch
    normed_two = layer_norm(middle, gain_two, bias_two).astype(jnp.bfloat16)
    hidden_pre = jnp.dot(normed_two, up_w, preferred_element_type=jnp.float32) + up_b
    hidden_low = jax.nn.gelu(hidden_pre).astype(jnp.bfloat16)
    result = middle + (
        tensor_total(jnp.dot(hidden_low, down_w, preferred_element_type=jnp.float32)) + down_b
    )
    kept = (
        inputs,
        normed,
        query,
        kv_pair,
        attended,
        log_total,
        middle,
        normed_two,
        hidden_pre,
        hidden_low,
        lengths,
        query_pos,
        query_doc,
    )
    return (result, kept)


def backward_layer(grad_out, kept, weights):
    (
        gain_one,
        bias_one,
        qkv_w,
        qv_b,
        out_w,
        out_b,
        gain_two,
        bias_two,
        up_w,
        up_b,
        down_w,
        down_b,
    ) = weights
    (
        inputs,
        normed,
        query,
        kv_pair,
        attended,
        log_total,
        middle,
        normed_two,
        hidden_pre,
        hidden_low,
        lengths,
        query_pos,
        query_doc,
    ) = kept[:13]
    kv_all = lax.all_gather(kv_pair, "seq", axis=0, tiled=True)
    single = jnp.float32
    rows, inner = attended.shape
    heads = inner // HEAD_DIM
    scale = HEAD_DIM ** (-0.5)
    down_in = grad_out.astype(jnp.bfloat16)
    down_b_grad = jnp.sum(down_in.astype(single), axis=0)
    down_w_grad = jnp.einsum("tf,td->fd", hidden_low, down_in, preferred_element_type=single)
    hidden_grad = jnp.einsum("td,fd->tf", down_in, down_w, preferred_element_type=single)
    _, gelu_back = jax.vjp(jax.nn.gelu, hidden_pre)
    pre_grad = gelu_back(hidden_grad)[0].astype(jnp.bfloat16)
    up_b_grad = jnp.sum(pre_grad.astype(single), axis=0)
    up_w_grad = jnp.einsum("td,tf->df", normed_two, pre_grad, preferred_element_type=single)
    normed_two_grad = tensor_back(
        jnp.einsum("tf,df->td", pre_grad, up_w, preferred_element_type=single)
    )
    _, norm_two_back = jax.vjp(layer_norm, middle, gain_two, bias_two)
    middle_extra, gain_two_grad, bias_two_grad = norm_two_back(normed_two_grad)
    middle_grad = grad_out + middle_extra
    branch_grad = middle_grad.astype(jnp.bfloat16)
    out_b_grad = jnp.sum(branch_grad.astype(single), axis=0)
    out_w_grad = jnp.einsum(
        "th,td->hd", attended.astype(jnp.bfloat16), branch_grad, preferred_element_type=single
    )
    attended_grad = jnp.einsum(
        "td,hd->th", branch_grad, out_w, preferred_element_type=single
    ).astype(jnp.bfloat16)
    grad_heads = attended_grad.reshape(rows, heads, HEAD_DIM)
    query_heads = query.reshape(rows, heads, HEAD_DIM)
    dot_total = jnp.sum(
        grad_heads.astype(single) * attended.reshape(rows, heads, HEAD_DIM), axis=-1
    ).T
    total = kv_all.shape[0]
    width = block_width(total, rows)
    blocks = kv_all.reshape(total // width, width, 2, inner)
    starts = jnp.arange(total // width, dtype=jnp.int32) * width

    def score_grads(block, start):
        keys, values = split_pair(block, heads)
        scores, allowed = block_scores(query_heads, keys, query_pos, query_doc, start, lengths)
        probs = jnp.where(allowed, jnp.exp(scores - log_total[..., None]), 0.0)
        prob_grad = jnp.einsum("thd,khd->htk", grad_heads, values, preferred_element_type=single)
        score_grad = jnp.where(allowed, probs * (prob_grad - dot_total[..., None]), 0.0).astype(
            jnp.bfloat16
        )
        return (keys, probs, score_grad)

    def joined_step(running, item):
        block, start = item
        keys, probs, score_grad = score_grads(block, start)
        running = running + jnp.einsum(
            "htk,khd->thd", score_grad, keys, preferred_element_type=single
        )
        key_grad = (
            jnp.einsum("htk,thd->khd", score_grad, query_heads, preferred_element_type=single)
            * scale
        )
        value_grad = jnp.einsum(
            "htk,thd->khd", probs.astype(jnp.bfloat16), grad_heads, preferred_element_type=single
        )
        return (
            running,
            jnp.stack([key_grad.reshape(width, inner), value_grad.reshape(width, inner)], axis=1),
        )

    query_acc, terms = lax.scan(
        joined_step, jnp.zeros((rows, heads, HEAD_DIM), single), (blocks, starts)
    )
    terms_all = terms.reshape(total, 2, inner)
    pair_grad = lax.psum_scatter(terms_all, "seq", scatter_dimension=0, tiled=True).astype(
        jnp.bfloat16
    )
    query_grad = (query_acc * scale).reshape(rows, inner).astype(jnp.bfloat16)
    proj_grad = jnp.concatenate([query_grad[:, None], pair_grad], axis=1)
    qv_b_grad = jnp.stack(
        [
            jnp.sum(query_grad.astype(single), axis=0),
            jnp.sum(pair_grad[:, 1].astype(single), axis=0),
        ]
    )
    qkv_w_grad = jnp.einsum("td,tch->dch", normed, proj_grad, preferred_element_type=single)
    normed_grad = tensor_back(
        jnp.einsum("tch,dch->td", proj_grad, qkv_w, preferred_element_type=single)
    )
    _, norm_one_back = jax.vjp(layer_norm, inputs, gain_one, bias_one)
    input_extra, gain_one_grad, bias_one_grad = norm_one_back(normed_grad)
    input_grad = middle_grad + input_extra
    grads = (
        gain_one_grad,
        bias_one_grad,
        qkv_w_grad,
        qv_b_grad,
        out_w_grad,
        out_b_grad,
        gain_two_grad,
        bias_two_grad,
        up_w_grad,
        up_b_grad,
        down_w_grad,
        down_b_grad,
    )
    return (input_grad, grads)


def local(
    block_input,
    out_grad,
    doc_lengths,
    ln1_gain,
    ln1_bias,
    qkv_weight,
    qv_bias,
    out_weight,
    out_bias,
    ln2_gain,
    ln2_bias,
    fc1_weight,
    fc1_bias,
    fc2_weight,
    fc2_bias,
):
    weights = (
        ln1_gain[0],
        ln1_bias[0],
        qkv_weight[0],
        qv_bias[0],
        out_weight[0],
        out_bias[0],
        ln2_gain[0],
        ln2_bias[0],
        fc1_weight[0],
        fc1_bias[0],
        fc2_weight[0],
        fc2_bias[0],
    )
    micro_count = block_input.shape[0]
    first = lax.axis_index("section") == 0
    received = jnp.zeros(block_input.shape[1:], jnp.bfloat16)
    outputs = []
    stored = []
    for tick in range(micro_count + 1):
        own = min(tick, micro_count - 1)
        prior = max(tick - 1, 0)
        layer_in = jnp.where(first, block_input[own], received).astype(jnp.float32)
        lengths = jnp.where(first, doc_lengths[own], doc_lengths[prior])
        result, kept = forward_layer(layer_in, lengths, weights)
        result_low = result.astype(jnp.bfloat16)
        outputs.append(result_low)
        stored.append(kept)
        received = passed_along(result_low, "section", 1)
    layer_out = jnp.stack(
        [jnp.where(first, outputs[m], outputs[m + 1]) for m in range(micro_count)]
    )
    totals = jax.tree.map(lambda w: jnp.zeros(w.shape, jnp.float32), weights)
    returned = jnp.zeros(block_input.shape[1:], jnp.bfloat16)
    input_grads = []
    for tick in range(micro_count + 1):
        mine = min(tick, micro_count - 1)
        valid = jnp.where(first, float(tick >= 1), float(tick < micro_count)).astype(jnp.float32)
        upstream = jnp.where(first, returned, out_grad[mine]).astype(jnp.float32)
        kept = jax.tree.map(
            lambda early, late: jnp.where(first, early, late),
            stored[max(tick - 1, 0)],
            stored[min(tick + 1, micro_count)],
        )
        input_grad, grads = backward_layer(upstream, kept, weights)
        totals = jax.tree.map(lambda total, grad: total + valid * grad, totals, grads)
        grad_low = input_grad.astype(jnp.bfloat16)
        input_grads.append(grad_low)
        returned = passed_along(grad_low, "section", -1)
    layer_grad = jnp.stack(
        [jnp.where(first, input_grads[m + 1], input_grads[m]) for m in range(micro_count)]
    )
    (
        gain_one_sum,
        bias_one_sum,
        qkv_sum,
        qv_sum,
        out_w_sum,
        out_b_sum,
        gain_two_sum,
        bias_two_sum,
        up_w_sum,
        up_b_sum,
        down_w_sum,
        down_b_sum,
    ) = totals
    summed = (
        lax.psum_scatter(gain_one_sum, "seq", scatter_dimension=0, tiled=True),
        lax.psum_scatter(bias_one_sum, "seq", scatter_dimension=0, tiled=True),
        lax.psum_scatter(qkv_sum, "seq", scatter_dimension=0, tiled=True),
        lax.psum_scatter(qv_sum, "seq", scatter_dimension=1, tiled=True),
        lax.psum_scatter(out_w_sum, "seq", scatter_dimension=0, tiled=True),
        lax.psum_scatter(out_b_sum, "seq", scatter_dimension=0, tiled=True),
        lax.psum_scatter(gain_two_sum, "seq", scatter_dimension=0, tiled=True),
        lax.psum_scatter(bias_two_sum, "seq", scatter_dimension=0, tiled=True),
        lax.psum_scatter(up_w_sum, "seq", scatter_dimension=0, tiled=True),
        lax.psum_scatter(up_b_sum, "seq", scatter_dimension=0, tiled=True),
        lax.psum_scatter(down_w_sum, "seq", scatter_dimension=0, tiled=True),
        lax.psum_scatter(down_b_sum, "seq", scatter_dimension=0, tiled=True),
    )
    return (
        layer_out[None],
        layer_grad[None],
        summed[0][None],
        summed[1][None],
        summed[2][None],
        summed[3][None],
        summed[4][None],
        summed[5][None],
        summed[6][None],
        summed[7][None],
        summed[8][None],
        summed[9][None],
        summed[10][None],
        summed[11][None],
    )


def swapped_cores(block):
    return lax.ppermute(block, "tensor", [(0, 1), (1, 0)])


def swapped_groups(block):
    return lax.ppermute(block, "seq", [(i, i ^ 1) for i in range(lax.axis_size("seq"))])


def together(*values):
    return lax.optimization_barrier(values)


def picked(block, which, axis):
    return lax.dynamic_index_in_dim(block, which, axis, keepdims=False)


def in_order(mine, other, place, axis):
    return jnp.where(
        place == 0, jnp.stack([mine, other], axis=axis), jnp.stack([other, mine], axis=axis)
    )


def micro_routes(count):
    groups = lax.axis_size("seq") // count
    return [
        [
            (m * groups + g, (m + step) % count * groups + g)
            for m in range(count)
            for g in range(groups)
        ]
        for step in range(1, count)
    ]


def from_micros(blocks, micro, count):
    parts = [picked(blocks, micro, 0)]
    for step, route in enumerate(micro_routes(count), 1):
        parts.append(lax.ppermute(picked(blocks, (micro + step) % count, 0), "seq", route))
    return jnp.stack(parts, axis=0)


def across_micros(blocks, micro, count):
    turned = jnp.roll(from_micros(blocks, micro, count)[::-1], 1, axis=0)
    return lax.dynamic_slice_in_dim(
        jnp.concatenate([turned, turned], axis=0), (count - micro) % count, count, axis=0
    )


def swapped_micros(block, bit, count):
    groups = lax.axis_size("seq") // count
    return lax.ppermute(
        block,
        "seq",
        [((m * groups) + g, (m ^ bit) * groups + g) for m in range(count) for g in range(groups)],
    )


def joined(kept, got):
    return (kept.astype(SINGLE) + got.astype(SINGLE)).astype(LOW)


SINGLE = jnp.float32
LOW = jnp.bfloat16
VMEM_BYTES = 32 * 1024 * 1024
NT = (((1,), (1,)), ((), ()))
TN = (((0,), (0,)), ((), ()))
SCALARS = pl.BlockSpec(memory_space=pltpu.SMEM)
WHOLE = pl.BlockSpec(memory_space=pltpu.VMEM)


def kernel_call(body, name, shapes, scalars, arrays, flops, scratch=()):
    outs = [jax.ShapeDtypeStruct(shape, dtype) for shape, dtype in shapes]
    moved = sum(math.prod(a.shape) * a.dtype.itemsize for a in (*arrays, *outs))
    return pl.pallas_call(
        body,
        out_shape=outs,
        in_specs=[SCALARS] + [WHOLE] * len(arrays),
        out_specs=[WHOLE] * len(outs),
        scratch_shapes=list(scratch),
        compiler_params=pltpu.CompilerParams(vmem_limit_bytes=VMEM_BYTES),
        cost_estimate=pl.CostEstimate(flops=flops, bytes_accessed=moved, transcendentals=0),
        name=name,
    )(scalars, *arrays)


def row_norm(values):
    mean = jnp.mean(values, axis=-1, keepdims=True)
    centred = values - mean
    inverse = lax.rsqrt(jnp.mean(centred * centred, axis=-1, keepdims=True) + EPS)
    return centred * inverse, inverse


def norm_back(shaped, inverse, scaled):
    return inverse * (
        scaled
        - jnp.mean(scaled, axis=-1, keepdims=True)
        - shaped * jnp.mean(scaled * shaped, axis=-1, keepdims=True)
    )


def either(place, mine, other):
    return jnp.where(place == 0, mine, other), jnp.where(place == 0, other, mine)


def column_sum(values):
    return jnp.sum(values, axis=0, keepdims=True)


def norm_kernel(place_ref, x_ref, gain_ref, bias_ref, out_ref):
    for block in range(x_ref.shape[0]):
        shaped, _ = row_norm(x_ref[block].astype(SINGLE))
        out_ref[block] = (shaped * gain_ref[...] + bias_ref[...]).astype(LOW)


def doc_mask(place_ref, docs, first, rows, count):
    key_pos = lax.broadcasted_iota(jnp.int32, (rows, count), 1)
    query_pos = first + lax.broadcasted_iota(jnp.int32, (rows, 1), 0)
    start = jnp.zeros((rows, 1), jnp.int32)
    bound = jnp.int32(0)
    for doc in range(docs):
        bound = bound + place_ref[3 + doc]
        start = jnp.maximum(start, jnp.where(query_pos >= bound, bound, 0))
    return (key_pos <= query_pos) & (key_pos >= start)


def put_side(ref, block, blocks, value):
    side, at = divmod(block, blocks // 2)
    own = value.shape[1]
    ref[at, :, side * own : (side + 1) * own] = value


def from_side(ref, block, blocks):
    side, at = divmod(block, blocks // 2)
    own = ref.shape[2] // 2
    return ref[at, :, side * own : (side + 1) * own]


def attend_kernel(heads, docs, kept, place_ref, *refs):
    core, group = place_ref[0], place_ref[1]
    mine, from_core, from_group, from_far = [refs[at : at + 2] for at in range(0, 8, 2)]
    w_ref, b_ref, out_ref, send_ref, *rest = refs[8:]
    if kept:
        qkv_ref, n_ref, lse_ref = rest
    else:
        own_ref, qkv_ref, n_ref, lse_ref = rest
        own = own_ref.shape[1] // 3
        for part in range(3):
            own_ref[:, part * own : (part + 1) * own] = jnp.where(
                group == 0, w_ref[part, :, :own], w_ref[part, :, own:]
            )
        w_ref = own_ref
    each, half, width = mine[0].shape
    blocks = 2 * each
    rows = 4 * half
    inner = heads * HEAD_DIM
    for block in range(blocks):
        piece, at = divmod(block, each)
        near = either(core, mine[piece][at], from_core[piece][at])
        far = either(core, from_group[piece][at], from_far[piece][at])
        near, far = jnp.concatenate(near, axis=0), jnp.concatenate(far, axis=0)
        n_ref[block * rows : (block + 1) * rows, :] = jnp.concatenate(
            either(group, near, far), axis=0
        )
    for i in range(0, blocks * rows, rows):
        made = jnp.dot(n_ref[i : i + rows, :], w_ref[...], preferred_element_type=SINGLE)
        qkv_ref[i : i + rows, :] = (made + b_ref[...]).astype(LOW)
    lane = lax.broadcasted_iota(jnp.int32, (rows, 128), 1)
    for block in range(blocks):
        i = block * rows
        count = i + rows
        allowed = doc_mask(place_ref, docs, i, rows, count)
        totals = jnp.zeros((rows, 128), SINGLE)
        mixed = []
        for h in range(heads):
            at = h * HEAD_DIM
            query = qkv_ref[i:count, at : at + HEAD_DIM] * LOW(HEAD_DIM**-0.5)
            keys = qkv_ref[:count, inner + at : inner + at + HEAD_DIM]
            values = qkv_ref[:count, 2 * inner + at : 2 * inner + at + HEAD_DIM]
            scores = lax.dot_general(query, keys, NT, preferred_element_type=SINGLE)
            scores = jnp.where(allowed, scores, NEG)
            top = jnp.max(scores, axis=1, keepdims=True)
            weights = jnp.exp(scores - top)
            mass = jnp.sum(weights, axis=1, keepdims=True)
            probs = (weights * (1.0 / mass)).astype(LOW)
            mixed.append(jnp.dot(probs, values, preferred_element_type=SINGLE))
            totals = jnp.where(lane == h, top + jnp.log(mass), totals)
        out = jnp.concatenate(mixed, axis=1).astype(LOW)
        out_ref[block], send = either(group, out[: rows // 2], out[rows // 2 :])
        put_side(send_ref, block, blocks, send)
        if kept:
            lse_ref[i:count, :] = totals


def attend_back_kernel(heads, docs, last, place_ref, qkv_ref, n_ref, w_ref, do_ref, do_far_ref, out_ref, send_ref, lse_ref, keep_ref, give_ref, *rest):
    if last:
        dw_ref, db_ref, acc_ref = rest
    else:
        (acc_ref,) = rest
    core, group = place_ref[0], place_ref[1]
    blocks = out_ref.shape[0]
    tokens = n_ref.shape[0]
    rows = tokens // blocks
    inner = heads * HEAD_DIM
    for block in range(blocks - 1, -1, -1):
        i = block * rows
        count = i + rows
        allowed = doc_mask(place_ref, docs, i, rows, count)
        far = from_side(do_far_ref, block, blocks)
        grads = jnp.concatenate(either(group, do_ref[block], far), axis=0)
        far = from_side(send_ref, block, blocks)
        outs = jnp.concatenate(either(group, out_ref[block], far), axis=0)
        for h in range(heads):
            at = h * HEAD_DIM
            query = qkv_ref[i:count, at : at + HEAD_DIM] * LOW(HEAD_DIM**-0.5)
            keys = qkv_ref[:count, inner + at : inner + at + HEAD_DIM]
            values = qkv_ref[:count, 2 * inner + at : 2 * inner + at + HEAD_DIM]
            grad = grads[:, at : at + HEAD_DIM]
            out = outs[:, at : at + HEAD_DIM]
            dots = jnp.sum(grad.astype(SINGLE) * out.astype(SINGLE), axis=1, keepdims=True)
            scores = lax.dot_general(query, keys, NT, preferred_element_type=SINGLE)
            probs = jnp.exp(jnp.where(allowed, scores, NEG) - lse_ref[i:count, h : h + 1])
            prob_grad = lax.dot_general(grad, values, NT, preferred_element_type=SINGLE)
            score_grad = (probs * (prob_grad - dots)).astype(LOW)
            query_grad = jnp.dot(score_grad, keys, preferred_element_type=SINGLE)
            acc_ref[at : at + HEAD_DIM, i:count] = query_grad.T * HEAD_DIM**-0.5
            at += inner
            key_grad = jnp.dot(query.T, score_grad, preferred_element_type=SINGLE)
            value_grad = jnp.dot(grad.T, probs.astype(LOW), preferred_element_type=SINGLE)
            if block == blocks - 1:
                acc_ref[at : at + HEAD_DIM, :] = key_grad
                acc_ref[at + inner : at + inner + HEAD_DIM, :] = value_grad
            else:
                acc_ref[at : at + HEAD_DIM, :count] += key_grad
                acc_ref[at + inner : at + inner + HEAD_DIM, :count] += value_grad
    for block in range(blocks):
        i = block * rows
        part = acc_ref[:, i : i + rows].T.astype(LOW)
        made = lax.dot_general(part, w_ref[...], NT, preferred_element_type=SINGLE).astype(LOW)
        near, far = either(group, made[: rows // 2], made[rows // 2 :])
        for place, side in ((0, near), (1, far)):
            keep_ref[place, block], give_ref[place, block] = either(
                core, side[: rows // 4], side[rows // 4 :]
            )
    if last:
        low = acc_ref[...].astype(LOW)
        dw_ref[...] = jnp.dot(low, n_ref[...], preferred_element_type=SINGLE).T.astype(LOW)
        ones = jnp.ones((db_ref.shape[0], low.shape[1]), LOW)
        db_ref[...] = lax.dot_general(ones, low, NT, preferred_element_type=SINGLE)


def project_kernel(place_ref, mine_ref, far_ref, w_ref, out_ref, *rest):
    group = place_ref[1]
    blocks, rows, own = mine_ref.shape
    near_w = w_ref[pl.ds(pl.multiple_of(group * own, own), own), :]
    far_w = w_ref[pl.ds(pl.multiple_of((1 - group) * own, own), own), :]
    for first in range(0, blocks, 2):
        pair = (first, first + 1)
        mine = jnp.concatenate([mine_ref[block] for block in pair], axis=0)
        far = jnp.concatenate([from_side(far_ref, block, blocks) for block in pair], axis=0)
        at = slice(first * rows, (first + 2) * rows)
        out_ref[at, :] = (
            jnp.dot(mine, near_w, preferred_element_type=SINGLE)
            + jnp.dot(far, far_w, preferred_element_type=SINGLE)
        ).astype(LOW)
        if rest:
            rest[0][at, :own], rest[0][at, own:] = either(group, mine, far)


def halves(core, mine_ref, other_ref, block):
    return jnp.concatenate(either(core, mine_ref[block], other_ref[block]), axis=0)


def feed_kernel(kept, place_ref, x_ref, x_far_ref, part_ref, far_ref, out_b_ref, gain_ref, bias_ref, up_ref, up_b_ref, down_ref, down_b_ref, base_ref, give_ref, *rest):
    core = place_ref[0]
    blocks, half, _ = x_ref.shape
    step = 2 * half
    for first in range(0, blocks, 2):
        rows = slice(first * step, (first + 2) * step)
        x = jnp.concatenate(
            [halves(core, x_ref, x_far_ref, block) for block in (first, first + 1)], axis=0
        )
        middle = (
            x.astype(SINGLE)
            + (part_ref[rows, :].astype(SINGLE) + far_ref[rows, :].astype(SINGLE))
            + out_b_ref[...]
        )
        shaped, _ = row_norm(middle)
        normed = (shaped * gain_ref[...] + bias_ref[...]).astype(LOW)
        pre = jnp.dot(normed, up_ref[...], preferred_element_type=SINGLE) + up_b_ref[...]
        hidden = jax.nn.gelu(pre).astype(LOW)
        made = jnp.dot(hidden, down_ref[...], preferred_element_type=SINGLE)
        if kept:
            middle_ref, normed_ref, pre_ref, own_ref, other_ref = rest
            middle_ref[rows, :] = middle
            normed_ref[rows, :] = normed
            pre_ref[rows, :] = pre
            cut = own_ref.shape[1]
            own_ref[rows, :], other_ref[rows, :] = hidden[:, :cut], hidden[:, cut:]
        for place in (0, 1):
            at = place * step
            mine, other = either(core, made[at : at + half], made[at + half : at + step])
            own = jnp.where(core == 0, middle[at : at + half], middle[at + half : at + step])
            base_ref[first + place] = own + mine + down_b_ref[...]
            give_ref[first + place] = other.astype(LOW)


def gelu_slope(value):
    rate = math.sqrt(2.0 / math.pi)
    squared = value * value
    bent = jnp.tanh(rate * value * (1.0 + 0.044715 * squared))
    return 0.5 * (1.0 + bent) + 0.5 * value * (1.0 - bent * bent) * (
        rate * (1.0 + 3 * 0.044715 * squared)
    )


def feed_back_kernel(last, place_ref, dy_ref, dy_far_ref, pre_ref, up_ref, down_ref, part_ref, dz_ref, *rest):
    core = place_ref[0]
    blocks, half, _ = dy_ref.shape
    step = 2 * half
    up_sum, down_sum = 0.0, 0.0
    for first in range(0, blocks, 2):
        rows = slice(first * step, (first + 2) * step)
        dz = jnp.concatenate(
            [halves(core, dy_ref, dy_far_ref, block) for block in (first, first + 1)], axis=0
        )
        dz_ref[rows, :] = dz
        grad = lax.dot_general(dz, down_ref[...], NT, preferred_element_type=SINGLE)
        pre_grad = (grad * gelu_slope(pre_ref[rows, :])).astype(LOW)
        part_ref[rows, :] = lax.dot_general(
            pre_grad, up_ref[...], NT, preferred_element_type=SINGLE
        ).astype(LOW)
        if last:
            cut = rest[0].shape[1]
            rest[0][rows, :], rest[1][rows, :] = pre_grad[:, :cut], pre_grad[:, cut:]
            up_sum = up_sum + column_sum(pre_grad.astype(SINGLE))
            down_sum = down_sum + column_sum(dz.astype(SINGLE))
    if last:
        rest[2][...] = up_sum
        rest[3][...] = down_sum


def project_back_kernel(last, place_ref, dz_ref, middle_ref, part_ref, far_ref, gain_ref, w_ref, mine_ref, give_ref, half_ref, *rest):
    core, group = place_ref[0], place_ref[1]
    own = mine_ref.shape[2]
    blocks, half, _ = half_ref.shape
    step = 2 * half
    near_w = w_ref[pl.ds(pl.multiple_of(group * own, own), own), :]
    far_w = w_ref[pl.ds(pl.multiple_of((1 - group) * own, own), own), :]
    sums = [0.0, 0.0, 0.0]
    for first in range(0, blocks, 2):
        rows = slice(first * step, (first + 2) * step)
        shaped, inverse = row_norm(middle_ref[rows, :])
        grad = part_ref[rows, :].astype(SINGLE) + far_ref[rows, :].astype(SINGLE)
        total = dz_ref[rows, :].astype(SINGLE) + norm_back(shaped, inverse, grad * gain_ref[...])
        low = total.astype(LOW)
        mine = lax.dot_general(low, near_w, NT, preferred_element_type=SINGLE).astype(LOW)
        give = lax.dot_general(low, far_w, NT, preferred_element_type=SINGLE).astype(LOW)
        for place in (0, 1):
            at = place * step
            mine_ref[first + place] = mine[at : at + step]
            put_side(give_ref, first + place, blocks, give[at : at + step])
            half_ref[first + place] = jnp.where(
                core == 0, total[at : at + half], total[at + half : at + step]
            )
        if last:
            rest[0][rows, :] = low
            for at, part in enumerate((low.astype(SINGLE), grad * shaped, grad)):
                sums[at] = sums[at] + column_sum(part)
    if last:
        for at in range(3):
            rest[1][at : at + 1, :] = sums[at]


def norm_back_kernel(last, place_ref, x_ref, keep_ref, core_ref, group_ref, rest_ref, gain_ref, dx_ref, *rest):
    sums = [0.0, 0.0]
    for block in range(x_ref.shape[0]):
        shaped, inverse = row_norm(x_ref[block].astype(SINGLE))
        grad = (
            keep_ref[0, block].astype(SINGLE)
            + core_ref[0, block].astype(SINGLE)
            + group_ref[block].astype(SINGLE)
        )
        back = norm_back(shaped, inverse, grad * gain_ref[...])
        dx_ref[block] = (rest_ref[block] + back).astype(LOW)
        if last:
            for at, part in enumerate((grad * shaped, grad)):
                sums[at] = sums[at] + column_sum(part)
    if last:
        for at in range(2):
            rest[0][at : at + 1, :] = sums[at]


def place_kernel(place_ref, mine_ref, other_ref, out_ref):
    core, micro = place_ref[0], place_ref[2]
    blocks, half, _ = mine_ref.shape
    for step in range(blocks):
        at = lax.rem(micro + blocks - step, blocks)
        out_ref[at] = halves(core, mine_ref, other_ref, step)


def pack_kernel(place_ref, one_ref, one_far_ref, branch_ref, down_ref, up_ref, qkv_ref, out_ref):
    group = place_ref[1]
    count = out_ref.shape[0]
    cut = one_ref.shape[1] // count
    wide = up_ref.shape[1] // count
    own = qkv_ref.shape[1] // 3
    slim = 2 * own // count
    full = jnp.concatenate(
        [one_ref[...] + one_far_ref[...], branch_ref[...], down_ref[...]], axis=0
    )
    out_ref[...] = jnp.zeros_like(out_ref)
    nothing = jnp.zeros((1, own), SINGLE)
    hidden = up_ref.shape[1]
    by_group = either(group, up_ref[:, : hidden // 2], up_ref[:, hidden // 2 :])
    for at in range(count):
        out_ref[at, 0:6, 0:cut] = full[:, at * cut : (at + 1) * cut].astype(LOW)
        up = by_group[at % 2][:, at // 2 * wide : (at // 2 + 1) * wide]
        out_ref[at, 6:7, 0:wide] = up.astype(LOW)
    for row, part in ((7, 0), (8, 2)):
        mine = qkv_ref[0:1, part * own : (part + 1) * own]
        both = jnp.concatenate(either(group, mine, nothing), axis=1)
        for at in range(count):
            out_ref[at, row : row + 1, 0:slim] = both[:, at * slim : (at + 1) * slim].astype(LOW)


def unpack_kernel(place_ref, kept_ref, got_ref, *out_refs):
    total = kept_ref[...].astype(SINGLE) + got_ref[...].astype(SINGLE)
    for row in range(6):
        out_refs[row][...] = total[row : row + 1, : out_refs[row].shape[1]]
    out_refs[6][...] = total[6:7, : out_refs[6].shape[1]]
    out_refs[7][...] = total[7:9, : out_refs[7].shape[1]]


def reorder_kernel(blocks, place_ref, up_ref, bias_ref, down_ref, up_out, bias_out, down_out):
    group = place_ref[1]
    hidden, _ = down_ref.shape
    cut = hidden // blocks
    for at in range(blocks // 2):
        near = slice(2 * at * cut, (2 * at + 1) * cut)
        far = slice((2 * at + 1) * cut, (2 * at + 2) * cut)
        first = slice(at * cut, (at + 1) * cut)
        second = slice(hidden // 2 + at * cut, hidden // 2 + (at + 1) * cut)
        for source, out in ((up_ref, up_out), (bias_ref, bias_out)):
            out[:, first], out[:, second] = either(group, source[:, near], source[:, far])
        down_out[first, :], down_out[second, :] = either(group, down_ref[near, :], down_ref[far, :])


def columns_kernel(blocks, place_ref, mine_ref, got_ref, out_ref):
    group = place_ref[1]
    cut = out_ref.shape[1] // blocks
    both = either(group, mine_ref[...], got_ref[...].astype(SINGLE))
    for at in range(blocks):
        piece = slice(at // 2 * cut, (at // 2 + 1) * cut)
        out_ref[:, at * cut : (at + 1) * cut] = both[at % 2][:, piece]


def heads_kernel(place_ref, mine_ref, got_ref, out_ref):
    group = place_ref[1]
    own = mine_ref.shape[1] // 3
    for part in range(3):
        at = slice(part * own, (part + 1) * own)
        out_ref[:, part, :] = jnp.concatenate(
            either(group, mine_ref[:, at], got_ref[:, at].astype(SINGLE)), axis=1
        )


def micro_local(
    block_input,
    out_grad,
    doc_lengths,
    ln1_gain,
    ln1_bias,
    qkv_weight,
    qv_bias,
    out_weight,
    out_bias,
    ln2_gain,
    ln2_bias,
    fc1_weight,
    fc1_bias,
    fc2_weight,
    fc2_bias,
):
    micros, rows, width = block_input.shape
    size = lax.axis_size("seq")
    place = lax.axis_index("seq")
    groups = size // micros
    micro, group = place // groups, place % groups
    core = lax.axis_index("tensor")
    first = lax.axis_index("section") == 0
    inner = out_weight.shape[1]
    own = inner // groups
    heads = own // HEAD_DIM
    hidden = fc1_weight.shape[2]
    docs = doc_lengths.shape[1]
    tokens = rows * size
    local_rows = tokens // groups
    half = rows // 2
    out_w, up_w, down_w = out_weight[0], fc1_weight[0], fc2_weight[0]
    qkv_w = jnp.transpose(qkv_weight[0], (1, 0, 2))
    qv_own = picked(qv_bias[0].reshape(2, groups, own), group, 1)
    qkv_b = jnp.concatenate([qv_own[0], jnp.zeros((own,), SINGLE), qv_own[1]])[None]
    scalars = jnp.concatenate(
        [jnp.stack([core, group, micro]).astype(jnp.int32), picked(doc_lengths, micro, 0)]
    )
    half_shape = (micros, half, width)
    up_w, up_b, down_w = kernel_call(
        partial(reorder_kernel, size),
        "reorder",
        [(up_w.shape, LOW), (fc1_bias.shape, SINGLE), (down_w.shape, LOW)],
        scalars,
        [up_w, fc1_bias, down_w],
        0,
    )
    head_shape = (micros, rows, own)
    side_shape = (micros // 2, rows, 2 * own)
    dense = 2 * local_rows * width
    pairs = 2 * heads * HEAD_DIM * tokens * tokens * 5 // 8

    def run(body, name, shapes, arrays, flops, scratch=()):
        return kernel_call(body, name, shapes, scalars, arrays, flops, scratch)

    def in_pieces(block):
        cut = block.shape[0] // 2
        return [block[:cut], block[cut:]]

    def normed_once(mine):
        return run(
            norm_kernel, "norm", [(mine.shape, LOW)], [mine, ln1_gain, ln1_bias], 8 * mine.size
        )[0]

    def forward(pieces, kept, qkv_w):
        mine = jnp.concatenate(pieces, axis=0)
        normed = [normed_once(piece) for piece in pieces]
        core_half = [swapped_cores(piece) for piece in normed]
        group_half = [swapped_groups(piece) for piece in normed]
        far_half = [swapped_cores(piece) for piece in group_half]
        *pieces, other = together(*normed, *core_half, *group_half, *far_half, swapped_cores(mine))
        made = [((tokens, 3 * own), LOW), ((tokens, width), LOW), ((tokens, 128), SINGLE)]
        out = run(
            partial(attend_kernel, heads, docs, kept),
            "attend",
            [(head_shape, LOW), (side_shape, LOW)]
            + (made if kept else [((width, 3 * own), LOW)]),
            [*pieces, qkv_w, qkv_b],
            2 * pairs + dense * 6 * own,
            () if kept else [pltpu.VMEM(*item) for item in made],
        )
        got = swapped_groups(out[1])
        part, *mixed = run(
            project_kernel,
            "project",
            [((local_rows, width), LOW)] + ([((local_rows, inner), LOW)] if kept else []),
            [out[0], got, out_w],
            dense * inner,
        )
        far_part = swapped_cores(part)
        saved = [
            ((local_rows, width), SINGLE),
            ((local_rows, width), LOW),
            ((local_rows, hidden), SINGLE),
            ((local_rows, hidden // 2), LOW),
            ((local_rows, hidden // 2), LOW),
        ]
        base, give, *rest = run(
            partial(feed_kernel, kept),
            "feed",
            [(half_shape, SINGLE), (half_shape, LOW)] + (saved if kept else []),
            [
                mine,
                other,
                part,
                far_part,
                out_bias,
                ln2_gain,
                ln2_bias,
                up_w,
                up_b,
                down_w,
                fc2_bias,
            ],
            2 * dense * hidden,
        )
        result = (base + swapped_cores(give).astype(SINGLE)).astype(LOW)
        return result, (mine, out, mixed, rest)

    def feed_back(grad_half, stored, last):
        pre = stored[3][2]
        extra = [((local_rows, hidden // 2), LOW)] * 2 + [
            ((1, hidden), SINGLE),
            ((1, width), SINGLE),
        ]
        return run(
            partial(feed_back_kernel, last),
            "feed_back",
            [((local_rows, width), LOW)] * 2 + (extra if last else []),
            [grad_half, swapped_cores(grad_half), pre, up_w, down_w],
            2 * dense * hidden,
        )

    def project_back(part, far_part, dz, stored, last):
        extra = [((local_rows, width), LOW), ((3, width), SINGLE)]
        return run(
            partial(project_back_kernel, last),
            "project_back",
            [(head_shape, LOW), (side_shape, LOW), (half_shape, SINGLE)]
            + (extra if last else []),
            [dz, stored[3][0], part, far_part, ln2_gain, out_w],
            dense * inner,
        )

    def attend_back(do_mine, do_got, stored, last, qkv_w):
        out_mine, out_send, qkv, normed, totals = stored[1]
        extra = [((width, 3 * own), LOW), ((8, 3 * own), SINGLE)]
        return run(
            partial(attend_back_kernel, heads, docs, last),
            "attend_back",
            [((2, *half_shape), LOW)] * 2 + (extra if last else []),
            [qkv, normed, qkv_w, do_mine, do_got, out_mine, out_send, totals],
            5 * pairs + dense * 6 * own,
            [pltpu.VMEM((3 * own, tokens), SINGLE)],
        )

    def core_sum(keep, give):
        core_got = swapped_cores(give)
        return core_got, joined(keep[1], core_got[1])

    def norm_back_once(mine, keep, core_got, group_got, rest_half, last):
        return run(
            partial(norm_back_kernel, last),
            "norm_back",
            [(mine.shape, LOW)] + ([((2, width), SINGLE)] if last else []),
            [mine, keep, core_got, group_got, rest_half, ln1_gain],
            20 * mine.size,
        )

    def backward(grad_half, stored, qkv_w):
        hidden_far = stored[3][4]
        cut = local_rows // 4
        hidden_one = swapped_groups(hidden_far[:cut])
        part, dz = feed_back(grad_half, stored, False)
        part, dz, hidden_one = together(part, dz, hidden_one)
        do_mine, do_give, rest_half = project_back(part, swapped_cores(part), dz, stored, False)
        do_got, hidden_far = together(swapped_groups(do_give), hidden_far)
        hidden_two = swapped_groups(hidden_far[cut : 3 * cut])
        keep, give = attend_back(do_mine, do_got, stored, False, qkv_w)
        keep, give, hidden_two = together(keep, give, hidden_two)
        dx = []
        for piece in range(2):
            at = slice(piece * micros // 2, (piece + 1) * micros // 2)
            near, far = keep[:, at], swapped_cores(give[:, at])
            group_got = swapped_groups(joined(near[1], far[1]))
            dx += norm_back_once(
                stored[0][at], near, far, group_got, rest_half[at], False
            )
        return dx, [hidden_one, hidden_two], hidden_far[3 * cut :]

    def weight_grad(*terms):
        made = sum(
            lax.dot_general(left, right, TN, preferred_element_type=SINGLE)
            for left, right in terms
        )
        return made.astype(LOW).reshape(2, 2, -1, made.shape[1])

    def group_parts(parts):
        return picked(parts, group, 2), picked(parts, 1 - group, 2)

    def near_parts(parts):
        return picked(parts, micro % 2, 1), picked(parts, 1 - micro % 2, 1)

    def far_parts(parts):
        return picked(parts, micro // 2, 0), picked(parts, 1 - micro // 2, 0)

    def near_swap(give):
        return swapped_micros(give, 1, micros)

    def far_swap(give):
        return swapped_micros(give, 2, micros)

    def total(kept, got):
        return kept.astype(SINGLE) + got.astype(SINGLE)

    def backward_last(grad_half, stored, hidden_got, normed_got, final, qkv_w):
        normed_two, hidden_own = stored[3][1], stored[3][3]
        cut = micros // 2
        dz_one = swapped_groups(grad_half[:cut])
        part, dz, pre_own, pre_give, up_sum, down_sum = feed_back(grad_half, stored, True)
        part, dz, dz_one, dz_two = together(part, dz, dz_one, grad_half[cut:])
        dz_two = swapped_groups(dz_two)
        do_mine, do_give, rest_half, branch, branch_sums = project_back(
            part, swapped_cores(part), dz, stored, True
        )
        do_give, dz_two = together(do_give, dz_two)

        dz_far = jnp.concatenate([dz_one, dz_two], axis=0)
        dz_far = in_order(dz_far, swapped_cores(dz_far), core, 1).reshape(local_rows, width)
        down_keep, down_give = near_parts(weight_grad((hidden_own, dz), (hidden_got, dz_far)))
        do_got, down_give, pre_give = together(swapped_groups(do_give), down_give, pre_give)

        cut = local_rows // 2
        pre_one = swapped_groups(pre_give[:cut])
        near_down = near_swap(down_give)
        keep, give, qkv_part, qkv_sums = attend_back(do_mine, do_got, stored, True, qkv_w)
        keep, give, qkv_part, near_down, pre_one, branch, final, normed_got = together(
            keep, give, qkv_part, near_down, pre_one, branch, final, normed_got
        )

        core_got, group_give = core_sum(keep, give)
        group_got = swapped_groups(group_give)
        pre_two = swapped_groups(pre_give[cut:])
        down_keep, down_give = far_parts(joined(down_keep, near_down))
        far_down = far_swap(down_give)
        qkv_keep, give = near_parts(qkv_part.reshape(2, 2, -1, 3 * own))
        near_qkv = near_swap(give)
        outputs = turned_back(final)
        normed_got = in_order(normed_got, swapped_cores(normed_got), core, 1)
        normed_got = normed_got.reshape(local_rows, width)
        out_keep, out_give = group_parts(
            weight_grad((stored[2][0], branch)).reshape(2, 2, groups, -1, width)
        )
        group_got, pre_two, far_down, out_give = together(group_got, pre_two, far_down, out_give)

        pre_got = jnp.concatenate([pre_one, pre_two], axis=0)
        up_keep, up_give = near_parts(weight_grad((normed_two, pre_own), (normed_got, pre_got)))
        near_up = near_swap(up_give)
        y_out = swapped_groups(out_give)
        dx, one = norm_back_once(stored[0], keep, core_got, group_got, rest_half, True)
        (vectors,) = run(
            pack_kernel,
            "pack",
            [((size, 16, 256), LOW)],
            [one, swapped_cores(one), branch_sums, down_sum, up_sum, qkv_sums],
            0,
        )
        vector_keep, give = group_parts(vectors.reshape(2, 2, groups, 16, 256))
        y_vector = swapped_groups(give)
        near_qkv, y_vector, dx = together(near_qkv, y_vector, dx)

        qkv_keep, give = far_parts(joined(qkv_keep, near_qkv))
        far_qkv = far_swap(give)
        moved = from_micros(dx, micro, micros)
        vector_keep, give = near_parts(joined(vector_keep, y_vector))
        near_vector = near_swap(give)
        y_out, near_vector, near_up = together(y_out, near_vector, near_up)

        up_keep, up_give = far_parts(joined(up_keep, near_up))
        far_up = far_swap(up_give)
        out_keep, give = near_parts(joined(out_keep, y_out))
        near_out = near_swap(give)
        vector_keep, give = far_parts(joined(vector_keep, near_vector))
        far_vector = far_swap(give)
        qkv_sum = total(qkv_keep, far_qkv).reshape(groups, -1, 3 * own)
        qkv_got = swapped_groups(picked(qkv_sum, 1 - group, 0).astype(LOW))
        near_out, far_vector, far_up, qkv_got, moved = together(
            near_out, far_vector, far_up, qkv_got, moved
        )

        out_keep, give = far_parts(joined(out_keep, near_out))
        far_out = far_swap(give)
        up_sum = total(up_keep, far_up).reshape(groups, -1, hidden // 2)
        up_got = swapped_groups(picked(up_sum, 1 - group, 0).astype(LOW))
        outputs_grad = turned_back(moved)
        down_grad = total(down_keep, far_down)
        (qkv_w_grad,) = run(
            heads_kernel,
            "heads",
            [((width // size, 3, inner), SINGLE)],
            [picked(qkv_sum, group, 0), qkv_got],
            0,
        )
        cut = width // size
        vector = run(
            unpack_kernel,
            "unpack",
            [((1, cut), SINGLE)] * 6
            + [((1, hidden // size), SINGLE), ((2, inner // size), SINGLE)],
            [vector_keep, far_vector],
            0,
        )
        (up_grad,) = run(
            partial(columns_kernel, size),
            "columns",
            [((cut, hidden), SINGLE)],
            [picked(up_sum, group, 0), up_got],
            0,
        )
        return (
            outputs,
            outputs_grad,
            vector[0],
            vector[1],
            qkv_w_grad[None],
            vector[7][None],
            total(out_keep, far_out)[None],
            vector[2],
            vector[3],
            vector[4],
            up_grad[None],
            vector[6],
            down_grad[None],
            vector[5],
        )

    def turned_back(moved):
        return run(
            place_kernel,
            "place",
            [((micros, rows, width), LOW)],
            [moved, swapped_cores(moved)],
            0,
        )[0][None]

    begun = jnp.where(first, block_input, out_grad).reshape(micros, 2, half, width)
    begun = across_micros(picked(begun, core, 1), micro, micros)
    begun, qkv_w, up_w, up_b, down_w = together(begun, qkv_w, up_w, up_b, down_w)
    early, (_, early_out, *_) = forward(in_pieces(begun), False, qkv_w)
    qkv_w = early_out[2]
    received = [passed_along(piece, "section", 1) for piece in in_pieces(early)]
    pieces = [jnp.where(first, *pair) for pair in zip(in_pieces(begun), received)]
    final, stored = forward(pieces, True, qkv_w)
    early_grad, hidden_got, hidden_far = backward(begun, stored, qkv_w)
    normed_far = picked(stored[3][1].reshape(micros, 2, half, width), core, 1)
    returned = [passed_along(early_grad[0], "section", -1)]
    last_grad, final, hidden_far, normed_far = together(
        early_grad[1], final, hidden_far, normed_far
    )
    returned.append(passed_along(last_grad, "section", -1))
    *returned, hidden_last, normed_got, moved = together(
        *returned,
        swapped_groups(hidden_far),
        swapped_groups(normed_far),
        from_micros(final, micro, micros),
    )
    hidden_got = jnp.concatenate([*hidden_got, hidden_last], axis=0)
    grad_half = jnp.where(first, jnp.concatenate(returned, axis=0), begun)
    return backward_last(grad_half, stored, hidden_got, normed_got, moved, qkv_w)


def solution(mesh):
    placed = (
        P(None, "seq", None),
        P(None, "seq", None),
        P(),
        P("section", None),
        P("section", None),
        P("section", None, None, "tensor"),
        P("section", None, "tensor"),
        P("section", "tensor", None),
        P("section", None),
        P("section", None),
        P("section", None),
        P("section", None, "tensor"),
        P("section", "tensor"),
        P("section", "tensor", None),
        P("section", None),
    )

    def chosen(*arrays):
        pairs = mesh.shape["seq"] == 2 * arrays[0].shape[0]
        cores = mesh.shape["tensor"] == 2 and mesh.shape["section"] == 2
        heads = arrays[7].shape[1] // HEAD_DIM
        if pairs and cores and heads % 2 == 0:
            return micro_local(*arrays)
        return local(*arrays)

    return jax.shard_map(
        chosen,
        mesh=mesh,
        in_specs=placed,
        out_specs=(
            P("section", None, "seq", None),
            P("section", None, "seq", None),
            P("section", "seq"),
            P("section", "seq"),
            P("section", "seq", None, "tensor"),
            P("section", None, ("tensor", "seq")),
            P("section", ("tensor", "seq"), None),
            P("section", "seq"),
            P("section", "seq"),
            P("section", "seq"),
            P("section", "seq", "tensor"),
            P("section", ("tensor", "seq")),
            P("section", ("tensor", "seq"), None),
            P("section", "seq"),
        ),
        check_vma=False,
    )
```

```python
import math
from functools import partial

import jax
import jax.numpy as jnp
from jax import lax
from jax.experimental import pallas as pl
from jax.experimental.pallas import tpu as pltpu
from jax.sharding import PartitionSpec as P

HEAD_DIM = 64


EPS = 1e-05
NEG = -1e30


def passed_along(block, axis, distance):
    devices = range(lax.axis_size(axis))
    route = [(i - distance, i) for i in devices if i - distance in devices]
    return lax.ppermute(block, axis, route)


def layer_norm(values, gain, shift):
    mean = jnp.mean(values, axis=-1, keepdims=True)
    centred = values - mean
    spread = jnp.mean(centred * centred, axis=-1, keepdims=True)
    return centred * lax.rsqrt(spread + EPS) * gain + shift


def doc_number(positions, lengths):
    bounds = jnp.cumsum(lengths, dtype=jnp.int32)
    return jnp.sum(
        (positions[:, None] >= bounds[None, :]).astype(jnp.int32), axis=1, dtype=jnp.int32
    )


def block_width(total, tok_rows):
    return math.gcd(total // tok_rows, max(1, 1024 // tok_rows)) * tok_rows


def block_scores(query, keys, query_pos, query_doc, key_start, lengths):
    count = keys.shape[0]
    scores = jnp.einsum(
        "thd,khd->htk", query, keys, preferred_element_type=jnp.float32
    ) * HEAD_DIM ** (-0.5)
    key_pos = key_start + jnp.arange(count, dtype=jnp.int32)
    key_doc = doc_number(key_pos, lengths)
    allowed = (key_doc[None, :] == query_doc[:, None]) & (key_pos[None, :] <= query_pos[:, None])
    return (scores, allowed[None])


def split_pair(block, heads):
    count = block.shape[0]
    return (
        block[:, 0].reshape(count, heads, HEAD_DIM),
        block[:, 1].reshape(count, heads, HEAD_DIM),
    )


def attend(query, kv_all, query_pos, query_doc, lengths):
    rows, heads = (query.shape[0], query.shape[1])
    width = block_width(kv_all.shape[0], rows)
    blocks = kv_all.reshape(kv_all.shape[0] // width, width, 2, kv_all.shape[2])
    starts = jnp.arange(blocks.shape[0], dtype=jnp.int32) * width

    def total_step(carry, item):
        top, mass = carry
        block, start = item
        keys, values = split_pair(block, heads)
        scores, allowed = block_scores(query, keys, query_pos, query_doc, start, lengths)
        masked = jnp.where(allowed, scores, NEG)
        new_top = jnp.maximum(top, jnp.max(masked, axis=-1))
        weights = jnp.where(allowed, jnp.exp(masked - new_top[..., None]), 0.0)
        return ((new_top, mass * jnp.exp(top - new_top) + jnp.sum(weights, axis=-1)), None)

    start_carry = (jnp.full((heads, rows), NEG, jnp.float32), jnp.zeros((heads, rows), jnp.float32))
    (top, mass), _ = lax.scan(total_step, start_carry, (blocks, starts))
    log_total = top + jnp.log(mass)

    def value_step(running, item):
        block, start = item
        keys, values = split_pair(block, heads)
        scores, allowed = block_scores(query, keys, query_pos, query_doc, start, lengths)
        probs = jnp.where(allowed, jnp.exp(scores - log_total[..., None]), 0.0).astype(jnp.bfloat16)
        return (
            running + jnp.einsum("htk,khd->thd", probs, values, preferred_element_type=jnp.float32),
            None,
        )

    mixed, _ = lax.scan(
        value_step, jnp.zeros((rows, heads, HEAD_DIM), jnp.float32), (blocks, starts)
    )
    return (mixed, log_total)


def tensor_total(partial_value):
    return lax.psum(partial_value.astype(jnp.bfloat16), "tensor").astype(jnp.float32)


def tensor_back(partial_value):
    return lax.psum(partial_value.astype(jnp.bfloat16), "tensor").astype(jnp.float32)


def forward_layer(inputs, lengths, weights):
    (
        gain_one,
        bias_one,
        qkv_w,
        qv_b,
        out_w,
        out_b,
        gain_two,
        bias_two,
        up_w,
        up_b,
        down_w,
        down_b,
    ) = weights
    rows, width = inputs.shape
    inner = qkv_w.shape[2]
    heads = inner // HEAD_DIM
    normed = layer_norm(inputs, gain_one, bias_one).astype(jnp.bfloat16)
    projected = jnp.dot(
        normed, qkv_w.reshape(width, 3 * inner), preferred_element_type=jnp.float32
    ).reshape(rows, 3, inner)
    query = (projected[:, 0] + qv_b[0]).astype(jnp.bfloat16)
    keys = projected[:, 1].astype(jnp.bfloat16)
    values = (projected[:, 2] + qv_b[1]).astype(jnp.bfloat16)
    kv_pair = jnp.stack([keys, values], axis=1)
    kv_all = lax.all_gather(kv_pair, "seq", axis=0, tiled=True)
    query_pos = lax.axis_index("seq") * rows + jnp.arange(rows, dtype=jnp.int32)
    query_doc = doc_number(query_pos, lengths)
    mixed, log_total = attend(
        query.reshape(rows, heads, HEAD_DIM), kv_all, query_pos, query_doc, lengths
    )
    attended = mixed.reshape(rows, inner)
    attended_low = attended.astype(jnp.bfloat16)
    branch = tensor_total(jnp.dot(attended_low, out_w, preferred_element_type=jnp.float32)) + out_b
    middle = inputs + branch
    normed_two = layer_norm(middle, gain_two, bias_two).astype(jnp.bfloat16)
    hidden_pre = jnp.dot(normed_two, up_w, preferred_element_type=jnp.float32) + up_b
    hidden_low = jax.nn.gelu(hidden_pre).astype(jnp.bfloat16)
    result = middle + (
        tensor_total(jnp.dot(hidden_low, down_w, preferred_element_type=jnp.float32)) + down_b
    )
    kept = (
        inputs,
        normed,
        query,
        kv_pair,
        attended,
        log_total,
        middle,
        normed_two,
        hidden_pre,
        hidden_low,
        lengths,
        query_pos,
        query_doc,
    )
    return (result, kept)


def backward_layer(grad_out, kept, weights):
    (
        gain_one,
        bias_one,
        qkv_w,
        qv_b,
        out_w,
        out_b,
        gain_two,
        bias_two,
        up_w,
        up_b,
        down_w,
        down_b,
    ) = weights
    (
        inputs,
        normed,
        query,
        kv_pair,
        attended,
        log_total,
        middle,
        normed_two,
        hidden_pre,
        hidden_low,
        lengths,
        query_pos,
        query_doc,
    ) = kept[:13]
    kv_all = lax.all_gather(kv_pair, "seq", axis=0, tiled=True)
    single = jnp.float32
    rows, inner = attended.shape
    heads = inner // HEAD_DIM
    scale = HEAD_DIM ** (-0.5)
    down_in = grad_out.astype(jnp.bfloat16)
    down_b_grad = jnp.sum(down_in.astype(single), axis=0)
    down_w_grad = jnp.einsum("tf,td->fd", hidden_low, down_in, preferred_element_type=single)
    hidden_grad = jnp.einsum("td,fd->tf", down_in, down_w, preferred_element_type=single)
    _, gelu_back = jax.vjp(jax.nn.gelu, hidden_pre)
    pre_grad = gelu_back(hidden_grad)[0].astype(jnp.bfloat16)
    up_b_grad = jnp.sum(pre_grad.astype(single), axis=0)
    up_w_grad = jnp.einsum("td,tf->df", normed_two, pre_grad, preferred_element_type=single)
    normed_two_grad = tensor_back(
        jnp.einsum("tf,df->td", pre_grad, up_w, preferred_element_type=single)
    )
    _, norm_two_back = jax.vjp(layer_norm, middle, gain_two, bias_two)
    middle_extra, gain_two_grad, bias_two_grad = norm_two_back(normed_two_grad)
    middle_grad = grad_out + middle_extra
    branch_grad = middle_grad.astype(jnp.bfloat16)
    out_b_grad = jnp.sum(branch_grad.astype(single), axis=0)
    out_w_grad = jnp.einsum(
        "th,td->hd", attended.astype(jnp.bfloat16), branch_grad, preferred_element_type=single
    )
    attended_grad = jnp.einsum(
        "td,hd->th", branch_grad, out_w, preferred_element_type=single
    ).astype(jnp.bfloat16)
    grad_heads = attended_grad.reshape(rows, heads, HEAD_DIM)
    query_heads = query.reshape(rows, heads, HEAD_DIM)
    dot_total = jnp.sum(
        grad_heads.astype(single) * attended.reshape(rows, heads, HEAD_DIM), axis=-1
    ).T
    total = kv_all.shape[0]
    width = block_width(total, rows)
    blocks = kv_all.reshape(total // width, width, 2, inner)
    starts = jnp.arange(total // width, dtype=jnp.int32) * width

    def score_grads(block, start):
        keys, values = split_pair(block, heads)
        scores, allowed = block_scores(query_heads, keys, query_pos, query_doc, start, lengths)
        probs = jnp.where(allowed, jnp.exp(scores - log_total[..., None]), 0.0)
        prob_grad = jnp.einsum("thd,khd->htk", grad_heads, values, preferred_element_type=single)
        score_grad = jnp.where(allowed, probs * (prob_grad - dot_total[..., None]), 0.0).astype(
            jnp.bfloat16
        )
        return (keys, probs, score_grad)

    def joined_step(running, item):
        block, start = item
        keys, probs, score_grad = score_grads(block, start)
        running = running + jnp.einsum(
            "htk,khd->thd", score_grad, keys, preferred_element_type=single
        )
        key_grad = (
            jnp.einsum("htk,thd->khd", score_grad, query_heads, preferred_element_type=single)
            * scale
        )
        value_grad = jnp.einsum(
            "htk,thd->khd", probs.astype(jnp.bfloat16), grad_heads, preferred_element_type=single
        )
        return (
            running,
            jnp.stack([key_grad.reshape(width, inner), value_grad.reshape(width, inner)], axis=1),
        )

    query_acc, terms = lax.scan(
        joined_step, jnp.zeros((rows, heads, HEAD_DIM), single), (blocks, starts)
    )
    terms_all = terms.reshape(total, 2, inner)
    pair_grad = lax.psum_scatter(terms_all, "seq", scatter_dimension=0, tiled=True).astype(
        jnp.bfloat16
    )
    query_grad = (query_acc * scale).reshape(rows, inner).astype(jnp.bfloat16)
    proj_grad = jnp.concatenate([query_grad[:, None], pair_grad], axis=1)
    qv_b_grad = jnp.stack(
        [
            jnp.sum(query_grad.astype(single), axis=0),
            jnp.sum(pair_grad[:, 1].astype(single), axis=0),
        ]
    )
    qkv_w_grad = jnp.einsum("td,tch->dch", normed, proj_grad, preferred_element_type=single)
    normed_grad = tensor_back(
        jnp.einsum("tch,dch->td", proj_grad, qkv_w, preferred_element_type=single)
    )
    _, norm_one_back = jax.vjp(layer_norm, inputs, gain_one, bias_one)
    input_extra, gain_one_grad, bias_one_grad = norm_one_back(normed_grad)
    input_grad = middle_grad + input_extra
    grads = (
        gain_one_grad,
        bias_one_grad,
        qkv_w_grad,
        qv_b_grad,
        out_w_grad,
        out_b_grad,
        gain_two_grad,
        bias_two_grad,
        up_w_grad,
        up_b_grad,
        down_w_grad,
        down_b_grad,
    )
    return (input_grad, grads)


def local(
    block_input,
    out_grad,
    doc_lengths,
    ln1_gain,
    ln1_bias,
    qkv_weight,
    qv_bias,
    out_weight,
    out_bias,
    ln2_gain,
    ln2_bias,
    fc1_weight,
    fc1_bias,
    fc2_weight,
    fc2_bias,
):
    weights = (
        ln1_gain[0],
        ln1_bias[0],
        qkv_weight[0],
        qv_bias[0],
        out_weight[0],
        out_bias[0],
        ln2_gain[0],
        ln2_bias[0],
        fc1_weight[0],
        fc1_bias[0],
        fc2_weight[0],
        fc2_bias[0],
    )
    micro_count = block_input.shape[0]
    first = lax.axis_index("section") == 0
    received = jnp.zeros(block_input.shape[1:], jnp.bfloat16)
    outputs = []
    stored = []
    for tick in range(micro_count + 1):
        own = min(tick, micro_count - 1)
        prior = max(tick - 1, 0)
        layer_in = jnp.where(first, block_input[own], received).astype(jnp.float32)
        lengths = jnp.where(first, doc_lengths[own], doc_lengths[prior])
        result, kept = forward_layer(layer_in, lengths, weights)
        result_low = result.astype(jnp.bfloat16)
        outputs.append(result_low)
        stored.append(kept)
        received = passed_along(result_low, "section", 1)
    layer_out = jnp.stack(
        [jnp.where(first, outputs[m], outputs[m + 1]) for m in range(micro_count)]
    )
    totals = jax.tree.map(lambda w: jnp.zeros(w.shape, jnp.float32), weights)
    returned = jnp.zeros(block_input.shape[1:], jnp.bfloat16)
    input_grads = []
    for tick in range(micro_count + 1):
        mine = min(tick, micro_count - 1)
        valid = jnp.where(first, float(tick >= 1), float(tick < micro_count)).astype(jnp.float32)
        upstream = jnp.where(first, returned, out_grad[mine]).astype(jnp.float32)
        kept = jax.tree.map(
            lambda early, late: jnp.where(first, early, late),
            stored[max(tick - 1, 0)],
            stored[min(tick + 1, micro_count)],
        )
        input_grad, grads = backward_layer(upstream, kept, weights)
        totals = jax.tree.map(lambda total, grad: total + valid * grad, totals, grads)
        grad_low = input_grad.astype(jnp.bfloat16)
        input_grads.append(grad_low)
        returned = passed_along(grad_low, "section", -1)
    layer_grad = jnp.stack(
        [jnp.where(first, input_grads[m + 1], input_grads[m]) for m in range(micro_count)]
    )
    (
        gain_one_sum,
        bias_one_sum,
        qkv_sum,
        qv_sum,
        out_w_sum,
        out_b_sum,
        gain_two_sum,
        bias_two_sum,
        up_w_sum,
        up_b_sum,
        down_w_sum,
        down_b_sum,
    ) = totals
    summed = (
        lax.psum_scatter(gain_one_sum, "seq", scatter_dimension=0, tiled=True),
        lax.psum_scatter(bias_one_sum, "seq", scatter_dimension=0, tiled=True),
        lax.psum_scatter(qkv_sum, "seq", scatter_dimension=0, tiled=True),
        lax.psum_scatter(qv_sum, "seq", scatter_dimension=1, tiled=True),
        lax.psum_scatter(out_w_sum, "seq", scatter_dimension=0, tiled=True),
        lax.psum_scatter(out_b_sum, "seq", scatter_dimension=0, tiled=True),
        lax.psum_scatter(gain_two_sum, "seq", scatter_dimension=0, tiled=True),
        lax.psum_scatter(bias_two_sum, "seq", scatter_dimension=0, tiled=True),
        lax.psum_scatter(up_w_sum, "seq", scatter_dimension=0, tiled=True),
        lax.psum_scatter(up_b_sum, "seq", scatter_dimension=0, tiled=True),
        lax.psum_scatter(down_w_sum, "seq", scatter_dimension=0, tiled=True),
        lax.psum_scatter(down_b_sum, "seq", scatter_dimension=0, tiled=True),
    )
    return (
        layer_out[None],
        layer_grad[None],
        summed[0][None],
        summed[1][None],
        summed[2][None],
        summed[3][None],
        summed[4][None],
        summed[5][None],
        summed[6][None],
        summed[7][None],
        summed[8][None],
        summed[9][None],
        summed[10][None],
        summed[11][None],
    )


def swapped_cores(block):
    return lax.ppermute(block, "tensor", [(0, 1), (1, 0)])


def swapped_groups(block):
    return lax.ppermute(block, "seq", [(i, i ^ 1) for i in range(lax.axis_size("seq"))])


def together(*values):
    return lax.optimization_barrier(values)


def picked(block, which, axis):
    return lax.dynamic_index_in_dim(block, which, axis, keepdims=False)


def in_order(mine, other, place, axis):
    return jnp.where(
        place == 0, jnp.stack([mine, other], axis=axis), jnp.stack([other, mine], axis=axis)
    )


def micro_routes(count):
    groups = lax.axis_size("seq") // count
    return [
        [
            (m * groups + g, (m + step) % count * groups + g)
            for m in range(count)
            for g in range(groups)
        ]
        for step in range(1, count)
    ]


def from_micros(blocks, micro, count):
    parts = [picked(blocks, micro, 0)]
    for step, route in enumerate(micro_routes(count), 1):
        parts.append(lax.ppermute(picked(blocks, (micro + step) % count, 0), "seq", route))
    return jnp.stack(parts, axis=0)


def across_micros(blocks, micro, count):
    turned = jnp.roll(from_micros(blocks, micro, count)[::-1], 1, axis=0)
    return lax.dynamic_slice_in_dim(
        jnp.concatenate([turned, turned], axis=0), (count - micro) % count, count, axis=0
    )


def swapped_micros(block, bit, count):
    groups = lax.axis_size("seq") // count
    return lax.ppermute(
        block,
        "seq",
        [((m * groups) + g, (m ^ bit) * groups + g) for m in range(count) for g in range(groups)],
    )


def joined(kept, got):
    return (kept.astype(SINGLE) + got.astype(SINGLE)).astype(LOW)


SINGLE = jnp.float32
LOW = jnp.bfloat16
VMEM_BYTES = 32 * 1024 * 1024
NT = (((1,), (1,)), ((), ()))
TN = (((0,), (0,)), ((), ()))
SCALARS = pl.BlockSpec(memory_space=pltpu.SMEM)
WHOLE = pl.BlockSpec(memory_space=pltpu.VMEM)


def kernel_call(body, name, shapes, scalars, arrays, flops, scratch=()):
    outs = [jax.ShapeDtypeStruct(shape, dtype) for shape, dtype in shapes]
    moved = sum(math.prod(a.shape) * a.dtype.itemsize for a in (*arrays, *outs))
    return pl.pallas_call(
        body,
        out_shape=outs,
        in_specs=[SCALARS] + [WHOLE] * len(arrays),
        out_specs=[WHOLE] * len(outs),
        scratch_shapes=list(scratch),
        compiler_params=pltpu.CompilerParams(vmem_limit_bytes=VMEM_BYTES),
        cost_estimate=pl.CostEstimate(flops=flops, bytes_accessed=moved, transcendentals=0),
        name=name,
    )(scalars, *arrays)


def row_norm(values):
    mean = jnp.mean(values, axis=-1, keepdims=True)
    centred = values - mean
    inverse = lax.rsqrt(jnp.mean(centred * centred, axis=-1, keepdims=True) + EPS)
    return centred * inverse, inverse


def norm_back(shaped, inverse, scaled):
    return inverse * (
        scaled
        - jnp.mean(scaled, axis=-1, keepdims=True)
        - shaped * jnp.mean(scaled * shaped, axis=-1, keepdims=True)
    )


def either(place, mine, other):
    return jnp.where(place == 0, mine, other), jnp.where(place == 0, other, mine)


def column_sum(values):
    return jnp.sum(values, axis=0, keepdims=True)


def norm_kernel(place_ref, x_ref, gain_ref, bias_ref, out_ref):
    for block in range(x_ref.shape[0]):
        shaped, _ = row_norm(x_ref[block].astype(SINGLE))
        out_ref[block] = (shaped * gain_ref[...] + bias_ref[...]).astype(LOW)


def doc_mask(place_ref, docs, first, rows, count):
    key_pos = lax.broadcasted_iota(jnp.int32, (rows, count), 1)
    query_pos = first + lax.broadcasted_iota(jnp.int32, (rows, 1), 0)
    start = jnp.zeros((rows, 1), jnp.int32)
    bound = jnp.int32(0)
    for doc in range(docs):
        bound = bound + place_ref[3 + doc]
        start = jnp.maximum(start, jnp.where(query_pos >= bound, bound, 0))
    return (key_pos <= query_pos) & (key_pos >= start)


def put_side(ref, block, blocks, value):
    side, at = divmod(block, blocks // 2)
    own = value.shape[1]
    ref[at, :, side * own : (side + 1) * own] = value


def from_side(ref, block, blocks):
    side, at = divmod(block, blocks // 2)
    own = ref.shape[2] // 2
    return ref[at, :, side * own : (side + 1) * own]


def attend_kernel(heads, docs, kept, place_ref, *refs):
    core, group = place_ref[0], place_ref[1]
    mine, from_core, from_group, from_far = [refs[at : at + 2] for at in range(0, 8, 2)]
    w_ref, b_ref, out_ref, send_ref, *rest = refs[8:]
    if kept:
        qkv_ref, n_ref, lse_ref = rest
    else:
        own_ref, qkv_ref, n_ref, lse_ref = rest
        own = own_ref.shape[1] // 3
        for part in range(3):
            own_ref[:, part * own : (part + 1) * own] = jnp.where(
                group == 0, w_ref[part, :, :own], w_ref[part, :, own:]
            )
        w_ref = own_ref
    each, half, width = mine[0].shape
    blocks = 2 * each
    rows = 4 * half
    inner = heads * HEAD_DIM
    for block in range(blocks):
        piece, at = divmod(block, each)
        near = either(core, mine[piece][at], from_core[piece][at])
        far = either(core, from_group[piece][at], from_far[piece][at])
        near, far = jnp.concatenate(near, axis=0), jnp.concatenate(far, axis=0)
        n_ref[block * rows : (block + 1) * rows, :] = jnp.concatenate(
            either(group, near, far), axis=0
        )
    for i in range(0, blocks * rows, rows):
        made = jnp.dot(n_ref[i : i + rows, :], w_ref[...], preferred_element_type=SINGLE)
        qkv_ref[i : i + rows, :] = (made + b_ref[...]).astype(LOW)
    lane = lax.broadcasted_iota(jnp.int32, (rows, 128), 1)
    for block in range(blocks):
        i = block * rows
        count = i + rows
        allowed = doc_mask(place_ref, docs, i, rows, count)
        totals = jnp.zeros((rows, 128), SINGLE)
        mixed = []
        for h in range(heads):
            at = h * HEAD_DIM
            query = qkv_ref[i:count, at : at + HEAD_DIM] * LOW(HEAD_DIM**-0.5)
            keys = qkv_ref[:count, inner + at : inner + at + HEAD_DIM]
            values = qkv_ref[:count, 2 * inner + at : 2 * inner + at + HEAD_DIM]
            scores = lax.dot_general(query, keys, NT, preferred_element_type=SINGLE)
            scores = jnp.where(allowed, scores, NEG)
            top = jnp.max(scores, axis=1, keepdims=True)
            weights = jnp.exp(scores - top)
            mass = jnp.sum(weights, axis=1, keepdims=True)
            made = jnp.dot(weights.astype(LOW), values, preferred_element_type=SINGLE)
            mixed.append(made * (1.0 / mass))
            totals = jnp.where(lane == h, top + jnp.log(mass), totals)
        out = jnp.concatenate(mixed, axis=1).astype(LOW)
        out_ref[block], send = either(group, out[: rows // 2], out[rows // 2 :])
        put_side(send_ref, block, blocks, send)
        if kept:
            lse_ref[i:count, :] = totals


def attend_back_kernel(heads, docs, last, place_ref, qkv_ref, n_ref, w_ref, do_ref, do_far_ref, out_ref, send_ref, lse_ref, keep_ref, give_ref, *rest):
    if last:
        dw_ref, db_ref, acc_ref = rest
    else:
        (acc_ref,) = rest
    core, group = place_ref[0], place_ref[1]
    blocks = out_ref.shape[0]
    tokens = n_ref.shape[0]
    rows = tokens // blocks
    inner = heads * HEAD_DIM
    for block in range(blocks - 1, -1, -1):
        i = block * rows
        count = i + rows
        allowed = doc_mask(place_ref, docs, i, rows, count)
        far = from_side(do_far_ref, block, blocks)
        grads = jnp.concatenate(either(group, do_ref[block], far), axis=0)
        far = from_side(send_ref, block, blocks)
        outs = jnp.concatenate(either(group, out_ref[block], far), axis=0)
        for h in range(heads):
            at = h * HEAD_DIM
            query = qkv_ref[i:count, at : at + HEAD_DIM] * LOW(HEAD_DIM**-0.5)
            keys = qkv_ref[:count, inner + at : inner + at + HEAD_DIM]
            values = qkv_ref[:count, 2 * inner + at : 2 * inner + at + HEAD_DIM]
            grad = grads[:, at : at + HEAD_DIM]
            out = outs[:, at : at + HEAD_DIM]
            dots = jnp.sum(grad.astype(SINGLE) * out.astype(SINGLE), axis=1, keepdims=True)
            scores = lax.dot_general(query, keys, NT, preferred_element_type=SINGLE)
            probs = jnp.exp(jnp.where(allowed, scores, NEG) - lse_ref[i:count, h : h + 1])
            prob_grad = lax.dot_general(grad, values, NT, preferred_element_type=SINGLE)
            score_grad = (probs * (prob_grad - dots)).astype(LOW)
            query_grad = jnp.dot(score_grad, keys, preferred_element_type=SINGLE)
            acc_ref[at : at + HEAD_DIM, i:count] = query_grad.T * HEAD_DIM**-0.5
            at += inner
            key_grad = jnp.dot(query.T, score_grad, preferred_element_type=SINGLE)
            value_grad = jnp.dot(grad.T, probs.astype(LOW), preferred_element_type=SINGLE)
            if block == blocks - 1:
                acc_ref[at : at + HEAD_DIM, :] = key_grad
                acc_ref[at + inner : at + inner + HEAD_DIM, :] = value_grad
            else:
                acc_ref[at : at + HEAD_DIM, :count] += key_grad
                acc_ref[at + inner : at + inner + HEAD_DIM, :count] += value_grad
    for block in range(blocks):
        i = block * rows
        part = acc_ref[:, i : i + rows].T.astype(LOW)
        made = lax.dot_general(part, w_ref[...], NT, preferred_element_type=SINGLE).astype(LOW)
        near, far = either(group, made[: rows // 2], made[rows // 2 :])
        for place, side in ((0, near), (1, far)):
            keep_ref[place, block], give_ref[place, block] = either(
                core, side[: rows // 4], side[rows // 4 :]
            )
    if last:
        low = acc_ref[...].astype(LOW)
        dw_ref[...] = jnp.dot(low, n_ref[...], preferred_element_type=SINGLE).T.astype(LOW)
        ones = jnp.ones((db_ref.shape[0], low.shape[1]), LOW)
        db_ref[...] = lax.dot_general(ones, low, NT, preferred_element_type=SINGLE)


def project_kernel(place_ref, mine_ref, far_ref, w_ref, out_ref, *rest):
    group = place_ref[1]
    blocks, rows, own = mine_ref.shape
    near_w = w_ref[pl.ds(pl.multiple_of(group * own, own), own), :]
    far_w = w_ref[pl.ds(pl.multiple_of((1 - group) * own, own), own), :]
    for first in range(0, blocks, 2):
        pair = (first, first + 1)
        mine = jnp.concatenate([mine_ref[block] for block in pair], axis=0)
        far = jnp.concatenate([from_side(far_ref, block, blocks) for block in pair], axis=0)
        at = slice(first * rows, (first + 2) * rows)
        out_ref[at, :] = (
            jnp.dot(mine, near_w, preferred_element_type=SINGLE)
            + jnp.dot(far, far_w, preferred_element_type=SINGLE)
        ).astype(LOW)
        if rest:
            rest[0][at, :own], rest[0][at, own:] = either(group, mine, far)


def halves(core, mine_ref, other_ref, block):
    return jnp.concatenate(either(core, mine_ref[block], other_ref[block]), axis=0)


def feed_kernel(kept, place_ref, x_ref, x_far_ref, part_ref, far_ref, out_b_ref, gain_ref, bias_ref, up_ref, up_b_ref, down_ref, down_b_ref, base_ref, give_ref, *rest):
    core = place_ref[0]
    blocks, half, _ = x_ref.shape
    step = 2 * half
    for first in range(0, blocks, 2):
        rows = slice(first * step, (first + 2) * step)
        x = jnp.concatenate(
            [halves(core, x_ref, x_far_ref, block) for block in (first, first + 1)], axis=0
        )
        middle = (
            x.astype(SINGLE)
            + (part_ref[rows, :].astype(SINGLE) + far_ref[rows, :].astype(SINGLE))
            + out_b_ref[...]
        )
        shaped, _ = row_norm(middle)
        normed = (shaped * gain_ref[...] + bias_ref[...]).astype(LOW)
        pre = jnp.dot(normed, up_ref[...], preferred_element_type=SINGLE) + up_b_ref[...]
        hidden = jax.nn.gelu(pre).astype(LOW)
        made = jnp.dot(hidden, down_ref[...], preferred_element_type=SINGLE)
        if kept:
            middle_ref, normed_ref, pre_ref, own_ref, other_ref = rest
            middle_ref[rows, :] = middle
            normed_ref[rows, :] = normed
            pre_ref[rows, :] = pre
            cut = own_ref.shape[1]
            own_ref[rows, :], other_ref[rows, :] = hidden[:, :cut], hidden[:, cut:]
        for place in (0, 1):
            at = place * step
            mine, other = either(core, made[at : at + half], made[at + half : at + step])
            own = jnp.where(core == 0, middle[at : at + half], middle[at + half : at + step])
            base_ref[first + place] = own + mine + down_b_ref[...]
            give_ref[first + place] = other.astype(LOW)


def gelu_slope(value):
    rate = math.sqrt(2.0 / math.pi)
    squared = value * value
    bent = jnp.tanh(rate * value * (1.0 + 0.044715 * squared))
    return 0.5 * (1.0 + bent) + 0.5 * value * (1.0 - bent * bent) * (
        rate * (1.0 + 3 * 0.044715 * squared)
    )


def feed_back_kernel(last, place_ref, dy_ref, dy_far_ref, pre_ref, up_ref, down_ref, part_ref, dz_ref, *rest):
    core = place_ref[0]
    blocks, half, _ = dy_ref.shape
    step = 2 * half
    up_sum, down_sum = 0.0, 0.0
    for first in range(0, blocks, 2):
        rows = slice(first * step, (first + 2) * step)
        dz = jnp.concatenate(
            [halves(core, dy_ref, dy_far_ref, block) for block in (first, first + 1)], axis=0
        )
        dz_ref[rows, :] = dz
        grad = lax.dot_general(dz, down_ref[...], NT, preferred_element_type=SINGLE)
        pre_grad = (grad * gelu_slope(pre_ref[rows, :])).astype(LOW)
        part_ref[rows, :] = lax.dot_general(
            pre_grad, up_ref[...], NT, preferred_element_type=SINGLE
        ).astype(LOW)
        if last:
            cut = rest[0].shape[1]
            rest[0][rows, :], rest[1][rows, :] = pre_grad[:, :cut], pre_grad[:, cut:]
            up_sum = up_sum + column_sum(pre_grad.astype(SINGLE))
            down_sum = down_sum + column_sum(dz.astype(SINGLE))
    if last:
        rest[2][...] = up_sum
        rest[3][...] = down_sum


def project_back_kernel(last, place_ref, dz_ref, middle_ref, part_ref, far_ref, gain_ref, w_ref, mine_ref, give_ref, half_ref, *rest):
    core, group = place_ref[0], place_ref[1]
    own = mine_ref.shape[2]
    blocks, half, _ = half_ref.shape
    step = 2 * half
    near_w = w_ref[pl.ds(pl.multiple_of(group * own, own), own), :]
    far_w = w_ref[pl.ds(pl.multiple_of((1 - group) * own, own), own), :]
    sums = [0.0, 0.0, 0.0]
    for first in range(0, blocks, 2):
        rows = slice(first * step, (first + 2) * step)
        shaped, inverse = row_norm(middle_ref[rows, :])
        grad = part_ref[rows, :].astype(SINGLE) + far_ref[rows, :].astype(SINGLE)
        total = dz_ref[rows, :].astype(SINGLE) + norm_back(shaped, inverse, grad * gain_ref[...])
        low = total.astype(LOW)
        mine = lax.dot_general(low, near_w, NT, preferred_element_type=SINGLE).astype(LOW)
        give = lax.dot_general(low, far_w, NT, preferred_element_type=SINGLE).astype(LOW)
        for place in (0, 1):
            at = place * step
            mine_ref[first + place] = mine[at : at + step]
            put_side(give_ref, first + place, blocks, give[at : at + step])
            half_ref[first + place] = jnp.where(
                core == 0, total[at : at + half], total[at + half : at + step]
            )
        if last:
            rest[0][rows, :] = low
            for at, part in enumerate((low.astype(SINGLE), grad * shaped, grad)):
                sums[at] = sums[at] + column_sum(part)
    if last:
        for at in range(3):
            rest[1][at : at + 1, :] = sums[at]


def norm_back_kernel(last, place_ref, x_ref, keep_ref, core_ref, group_ref, rest_ref, gain_ref, dx_ref, *rest):
    sums = [0.0, 0.0]
    for block in range(x_ref.shape[0]):
        shaped, inverse = row_norm(x_ref[block].astype(SINGLE))
        grad = (
            keep_ref[0, block].astype(SINGLE)
            + core_ref[0, block].astype(SINGLE)
            + group_ref[block].astype(SINGLE)
        )
        back = norm_back(shaped, inverse, grad * gain_ref[...])
        dx_ref[block] = (rest_ref[block] + back).astype(LOW)
        if last:
            for at, part in enumerate((grad * shaped, grad)):
                sums[at] = sums[at] + column_sum(part)
    if last:
        for at in range(2):
            rest[0][at : at + 1, :] = sums[at]


def place_kernel(place_ref, mine_ref, other_ref, out_ref):
    core, micro = place_ref[0], place_ref[2]
    blocks, half, _ = mine_ref.shape
    for step in range(blocks):
        at = lax.rem(micro + blocks - step, blocks)
        out_ref[at] = halves(core, mine_ref, other_ref, step)


def pack_kernel(place_ref, one_ref, one_far_ref, branch_ref, down_ref, up_ref, qkv_ref, out_ref):
    group = place_ref[1]
    count = out_ref.shape[0]
    cut = one_ref.shape[1] // count
    wide = up_ref.shape[1] // count
    own = qkv_ref.shape[1] // 3
    slim = 2 * own // count
    full = jnp.concatenate(
        [one_ref[...] + one_far_ref[...], branch_ref[...], down_ref[...]], axis=0
    )
    out_ref[...] = jnp.zeros_like(out_ref)
    nothing = jnp.zeros((1, own), SINGLE)
    hidden = up_ref.shape[1]
    by_group = either(group, up_ref[:, : hidden // 2], up_ref[:, hidden // 2 :])
    for at in range(count):
        out_ref[at, 0:6, 0:cut] = full[:, at * cut : (at + 1) * cut].astype(LOW)
        up = by_group[at % 2][:, at // 2 * wide : (at // 2 + 1) * wide]
        out_ref[at, 6:7, 0:wide] = up.astype(LOW)
    for row, part in ((7, 0), (8, 2)):
        mine = qkv_ref[0:1, part * own : (part + 1) * own]
        both = jnp.concatenate(either(group, mine, nothing), axis=1)
        for at in range(count):
            out_ref[at, row : row + 1, 0:slim] = both[:, at * slim : (at + 1) * slim].astype(LOW)


def unpack_kernel(place_ref, kept_ref, got_ref, *out_refs):
    total = kept_ref[...].astype(SINGLE) + got_ref[...].astype(SINGLE)
    for row in range(6):
        out_refs[row][...] = total[row : row + 1, : out_refs[row].shape[1]]
    out_refs[6][...] = total[6:7, : out_refs[6].shape[1]]
    out_refs[7][...] = total[7:9, : out_refs[7].shape[1]]


def reorder_kernel(blocks, place_ref, up_ref, bias_ref, down_ref, up_out, bias_out, down_out):
    group = place_ref[1]
    hidden, _ = down_ref.shape
    cut = hidden // blocks
    for at in range(blocks // 2):
        near = slice(2 * at * cut, (2 * at + 1) * cut)
        far = slice((2 * at + 1) * cut, (2 * at + 2) * cut)
        first = slice(at * cut, (at + 1) * cut)
        second = slice(hidden // 2 + at * cut, hidden // 2 + (at + 1) * cut)
        for source, out in ((up_ref, up_out), (bias_ref, bias_out)):
            out[:, first], out[:, second] = either(group, source[:, near], source[:, far])
        down_out[first, :], down_out[second, :] = either(group, down_ref[near, :], down_ref[far, :])


def columns_kernel(blocks, place_ref, mine_ref, got_ref, out_ref):
    group = place_ref[1]
    cut = out_ref.shape[1] // blocks
    both = either(group, mine_ref[...], got_ref[...].astype(SINGLE))
    for at in range(blocks):
        piece = slice(at // 2 * cut, (at // 2 + 1) * cut)
        out_ref[:, at * cut : (at + 1) * cut] = both[at % 2][:, piece]


def heads_kernel(place_ref, mine_ref, got_ref, out_ref):
    group = place_ref[1]
    own = mine_ref.shape[1] // 3
    for part in range(3):
        at = slice(part * own, (part + 1) * own)
        out_ref[:, part, :] = jnp.concatenate(
            either(group, mine_ref[:, at], got_ref[:, at].astype(SINGLE)), axis=1
        )


def micro_local(
    block_input,
    out_grad,
    doc_lengths,
    ln1_gain,
    ln1_bias,
    qkv_weight,
    qv_bias,
    out_weight,
    out_bias,
    ln2_gain,
    ln2_bias,
    fc1_weight,
    fc1_bias,
    fc2_weight,
    fc2_bias,
):
    micros, rows, width = block_input.shape
    size = lax.axis_size("seq")
    place = lax.axis_index("seq")
    groups = size // micros
    micro, group = place // groups, place % groups
    core = lax.axis_index("tensor")
    first = lax.axis_index("section") == 0
    inner = out_weight.shape[1]
    own = inner // groups
    heads = own // HEAD_DIM
    hidden = fc1_weight.shape[2]
    docs = doc_lengths.shape[1]
    tokens = rows * size
    local_rows = tokens // groups
    half = rows // 2
    out_w, up_w, down_w = out_weight[0], fc1_weight[0], fc2_weight[0]
    qkv_w = jnp.transpose(qkv_weight[0], (1, 0, 2))
    qv_own = picked(qv_bias[0].reshape(2, groups, own), group, 1)
    qkv_b = jnp.concatenate([qv_own[0], jnp.zeros((own,), SINGLE), qv_own[1]])[None]
    scalars = jnp.concatenate(
        [jnp.stack([core, group, micro]).astype(jnp.int32), picked(doc_lengths, micro, 0)]
    )
    half_shape = (micros, half, width)
    up_w, up_b, down_w = kernel_call(
        partial(reorder_kernel, size),
        "reorder",
        [(up_w.shape, LOW), (fc1_bias.shape, SINGLE), (down_w.shape, LOW)],
        scalars,
        [up_w, fc1_bias, down_w],
        0,
    )
    head_shape = (micros, rows, own)
    side_shape = (micros // 2, rows, 2 * own)
    dense = 2 * local_rows * width
    pairs = 2 * heads * HEAD_DIM * tokens * tokens * 5 // 8

    def run(body, name, shapes, arrays, flops, scratch=()):
        return kernel_call(body, name, shapes, scalars, arrays, flops, scratch)

    def in_pieces(block):
        cut = block.shape[0] // 2
        return [block[:cut], block[cut:]]

    def normed_once(mine):
        return run(
            norm_kernel, "norm", [(mine.shape, LOW)], [mine, ln1_gain, ln1_bias], 8 * mine.size
        )[0]

    def forward(pieces, kept, qkv_w):
        mine = jnp.concatenate(pieces, axis=0)
        normed = [normed_once(piece) for piece in pieces]
        core_half = [swapped_cores(piece) for piece in normed]
        group_half = [swapped_groups(piece) for piece in normed]
        far_half = [swapped_cores(piece) for piece in group_half]
        *pieces, other = together(*normed, *core_half, *group_half, *far_half, swapped_cores(mine))
        made = [((tokens, 3 * own), LOW), ((tokens, width), LOW), ((tokens, 128), SINGLE)]
        out = run(
            partial(attend_kernel, heads, docs, kept),
            "attend",
            [(head_shape, LOW), (side_shape, LOW)]
            + (made if kept else [((width, 3 * own), LOW)]),
            [*pieces, qkv_w, qkv_b],
            2 * pairs + dense * 6 * own,
            () if kept else [pltpu.VMEM(*item) for item in made],
        )
        got = swapped_groups(out[1])
        part, *mixed = run(
            project_kernel,
            "project",
            [((local_rows, width), LOW)] + ([((local_rows, inner), LOW)] if kept else []),
            [out[0], got, out_w],
            dense * inner,
        )
        far_part = swapped_cores(part)
        saved = [
            ((local_rows, width), SINGLE),
            ((local_rows, width), LOW),
            ((local_rows, hidden), SINGLE),
            ((local_rows, hidden // 2), LOW),
            ((local_rows, hidden // 2), LOW),
        ]
        base, give, *rest = run(
            partial(feed_kernel, kept),
            "feed",
            [(half_shape, SINGLE), (half_shape, LOW)] + (saved if kept else []),
            [
                mine,
                other,
                part,
                far_part,
                out_bias,
                ln2_gain,
                ln2_bias,
                up_w,
                up_b,
                down_w,
                fc2_bias,
            ],
            2 * dense * hidden,
        )
        result = (base + swapped_cores(give).astype(SINGLE)).astype(LOW)
        return result, (mine, out, mixed, rest)

    def feed_back(grad_half, stored, last):
        pre = stored[3][2]
        extra = [((local_rows, hidden // 2), LOW)] * 2 + [
            ((1, hidden), SINGLE),
            ((1, width), SINGLE),
        ]
        return run(
            partial(feed_back_kernel, last),
            "feed_back",
            [((local_rows, width), LOW)] * 2 + (extra if last else []),
            [grad_half, swapped_cores(grad_half), pre, up_w, down_w],
            2 * dense * hidden,
        )

    def project_back(part, far_part, dz, stored, last):
        extra = [((local_rows, width), LOW), ((3, width), SINGLE)]
        return run(
            partial(project_back_kernel, last),
            "project_back",
            [(head_shape, LOW), (side_shape, LOW), (half_shape, SINGLE)]
            + (extra if last else []),
            [dz, stored[3][0], part, far_part, ln2_gain, out_w],
            dense * inner,
        )

    def attend_back(do_mine, do_got, stored, last, qkv_w):
        out_mine, out_send, qkv, normed, totals = stored[1]
        extra = [((width, 3 * own), LOW), ((8, 3 * own), SINGLE)]
        return run(
            partial(attend_back_kernel, heads, docs, last),
            "attend_back",
            [((2, *half_shape), LOW)] * 2 + (extra if last else []),
            [qkv, normed, qkv_w, do_mine, do_got, out_mine, out_send, totals],
            5 * pairs + dense * 6 * own,
            [pltpu.VMEM((3 * own, tokens), SINGLE)],
        )

    def core_sum(keep, give):
        core_got = swapped_cores(give)
        return core_got, joined(keep[1], core_got[1])

    def norm_back_once(mine, keep, core_got, group_got, rest_half, last):
        return run(
            partial(norm_back_kernel, last),
            "norm_back",
            [(mine.shape, LOW)] + ([((2, width), SINGLE)] if last else []),
            [mine, keep, core_got, group_got, rest_half, ln1_gain],
            20 * mine.size,
        )

    def backward(grad_half, stored, qkv_w):
        hidden_far = stored[3][4]
        cut = local_rows // 4
        hidden_one = swapped_groups(hidden_far[:cut])
        part, dz = feed_back(grad_half, stored, False)
        part, dz, hidden_one = together(part, dz, hidden_one)
        do_mine, do_give, rest_half = project_back(part, swapped_cores(part), dz, stored, False)
        do_got, hidden_far = together(swapped_groups(do_give), hidden_far)
        hidden_two = swapped_groups(hidden_far[cut : 3 * cut])
        keep, give = attend_back(do_mine, do_got, stored, False, qkv_w)
        keep, give, hidden_two = together(keep, give, hidden_two)
        dx = []
        for piece in range(2):
            at = slice(piece * micros // 2, (piece + 1) * micros // 2)
            near, far = keep[:, at], swapped_cores(give[:, at])
            group_got = swapped_groups(joined(near[1], far[1]))
            dx += norm_back_once(
                stored[0][at], near, far, group_got, rest_half[at], False
            )
        return dx, [hidden_one, hidden_two], hidden_far[3 * cut :]

    def weight_grad(*terms):
        made = sum(
            lax.dot_general(left, right, TN, preferred_element_type=SINGLE)
            for left, right in terms
        )
        return made.astype(LOW).reshape(2, 2, -1, made.shape[1])

    def group_parts(parts):
        return picked(parts, group, 2), picked(parts, 1 - group, 2)

    def near_parts(parts):
        return picked(parts, micro % 2, 1), picked(parts, 1 - micro % 2, 1)

    def far_parts(parts):
        return picked(parts, micro // 2, 0), picked(parts, 1 - micro // 2, 0)

    def near_swap(give):
        return swapped_micros(give, 1, micros)

    def far_swap(give):
        return swapped_micros(give, 2, micros)

    def total(kept, got):
        return kept.astype(SINGLE) + got.astype(SINGLE)

    def backward_last(grad_half, stored, hidden_got, normed_got, final, qkv_w):
        normed_two, hidden_own = stored[3][1], stored[3][3]
        cut = micros // 2
        dz_one = swapped_groups(grad_half[:cut])
        part, dz, pre_own, pre_give, up_sum, down_sum = feed_back(grad_half, stored, True)
        part, dz, dz_one, dz_two = together(part, dz, dz_one, grad_half[cut:])
        dz_two = swapped_groups(dz_two)
        do_mine, do_give, rest_half, branch, branch_sums = project_back(
            part, swapped_cores(part), dz, stored, True
        )
        do_give, dz_two = together(do_give, dz_two)

        dz_far = jnp.concatenate([dz_one, dz_two], axis=0)
        dz_far = in_order(dz_far, swapped_cores(dz_far), core, 1).reshape(local_rows, width)
        down_keep, down_give = near_parts(weight_grad((hidden_own, dz), (hidden_got, dz_far)))
        do_got, down_give, pre_give = together(swapped_groups(do_give), down_give, pre_give)

        cut = local_rows // 2
        pre_one = swapped_groups(pre_give[:cut])
        near_down = near_swap(down_give)
        keep, give, qkv_part, qkv_sums = attend_back(do_mine, do_got, stored, True, qkv_w)
        keep, give, qkv_part, near_down, pre_one, branch, final, normed_got = together(
            keep, give, qkv_part, near_down, pre_one, branch, final, normed_got
        )

        core_got, group_give = core_sum(keep, give)
        group_got = swapped_groups(group_give)
        pre_two = swapped_groups(pre_give[cut:])
        down_keep, down_give = far_parts(joined(down_keep, near_down))
        far_down = far_swap(down_give)
        qkv_keep, give = near_parts(qkv_part.reshape(2, 2, -1, 3 * own))
        near_qkv = near_swap(give)
        outputs = turned_back(final)
        normed_got = in_order(normed_got, swapped_cores(normed_got), core, 1)
        normed_got = normed_got.reshape(local_rows, width)
        out_keep, out_give = group_parts(
            weight_grad((stored[2][0], branch)).reshape(2, 2, groups, -1, width)
        )
        group_got, pre_two, far_down, out_give = together(group_got, pre_two, far_down, out_give)

        pre_got = jnp.concatenate([pre_one, pre_two], axis=0)
        up_keep, up_give = near_parts(weight_grad((normed_two, pre_own), (normed_got, pre_got)))
        near_up = near_swap(up_give)
        y_out = swapped_groups(out_give)
        dx, one = norm_back_once(stored[0], keep, core_got, group_got, rest_half, True)
        (vectors,) = run(
            pack_kernel,
            "pack",
            [((size, 16, 256), LOW)],
            [one, swapped_cores(one), branch_sums, down_sum, up_sum, qkv_sums],
            0,
        )
        vector_keep, give = group_parts(vectors.reshape(2, 2, groups, 16, 256))
        y_vector = swapped_groups(give)
        near_qkv, y_vector, y_out, dx = together(near_qkv, y_vector, y_out, dx)

        qkv_keep, give = far_parts(joined(qkv_keep, near_qkv))
        far_qkv = far_swap(give)
        moved = from_micros(dx, micro, micros)
        vector_keep, give = near_parts(joined(vector_keep, y_vector))
        near_vector = near_swap(give)
        near_vector, near_up = together(near_vector, near_up)

        up_keep, up_give = far_parts(joined(up_keep, near_up))
        far_up = far_swap(up_give)
        out_keep, give = near_parts(joined(out_keep, y_out))
        near_out = near_swap(give)
        vector_keep, give = far_parts(joined(vector_keep, near_vector))
        far_vector = far_swap(give)
        qkv_sum = total(qkv_keep, far_qkv).reshape(groups, -1, 3 * own)
        qkv_got = swapped_groups(picked(qkv_sum, 1 - group, 0).astype(LOW))
        near_out, far_vector, far_up, qkv_got, moved = together(
            near_out, far_vector, far_up, qkv_got, moved
        )

        out_keep, give = far_parts(joined(out_keep, near_out))
        far_out = far_swap(give)
        up_sum = total(up_keep, far_up).reshape(groups, -1, hidden // 2)
        up_got = swapped_groups(picked(up_sum, 1 - group, 0).astype(LOW))
        outputs_grad = turned_back(moved)
        down_grad = total(down_keep, far_down)
        (qkv_w_grad,) = run(
            heads_kernel,
            "heads",
            [((width // size, 3, inner), SINGLE)],
            [picked(qkv_sum, group, 0), qkv_got],
            0,
        )
        cut = width // size
        vector = run(
            unpack_kernel,
            "unpack",
            [((1, cut), SINGLE)] * 6
            + [((1, hidden // size), SINGLE), ((2, inner // size), SINGLE)],
            [vector_keep, far_vector],
            0,
        )
        (up_grad,) = run(
            partial(columns_kernel, size),
            "columns",
            [((cut, hidden), SINGLE)],
            [picked(up_sum, group, 0), up_got],
            0,
        )
        return (
            outputs,
            outputs_grad,
            vector[0],
            vector[1],
            qkv_w_grad[None],
            vector[7][None],
            total(out_keep, far_out)[None],
            vector[2],
            vector[3],
            vector[4],
            up_grad[None],
            vector[6],
            down_grad[None],
            vector[5],
        )

    def turned_back(moved):
        return run(
            place_kernel,
            "place",
            [((micros, rows, width), LOW)],
            [moved, swapped_cores(moved)],
            0,
        )[0][None]

    begun = jnp.where(first, block_input, out_grad).reshape(micros, 2, half, width)
    begun = across_micros(picked(begun, core, 1), micro, micros)
    begun, qkv_w, up_w, up_b, down_w = together(begun, qkv_w, up_w, up_b, down_w)
    early, (_, early_out, *_) = forward(in_pieces(begun), False, qkv_w)
    qkv_w = early_out[2]
    received = [passed_along(piece, "section", 1) for piece in in_pieces(early)]
    pieces = [jnp.where(first, *pair) for pair in zip(in_pieces(begun), received)]
    final, stored = forward(pieces, True, qkv_w)
    early_grad, hidden_got, hidden_far = backward(begun, stored, qkv_w)
    normed_far = picked(stored[3][1].reshape(micros, 2, half, width), core, 1)
    returned = [passed_along(early_grad[0], "section", -1)]
    last_grad, final, hidden_far, normed_far = together(
        early_grad[1], final, hidden_far, normed_far
    )
    returned.append(passed_along(last_grad, "section", -1))
    *returned, hidden_last, normed_got, moved = together(
        *returned,
        swapped_groups(hidden_far),
        swapped_groups(normed_far),
        from_micros(final, micro, micros),
    )
    hidden_got = jnp.concatenate([*hidden_got, hidden_last], axis=0)
    grad_half = jnp.where(first, jnp.concatenate(returned, axis=0), begun)
    return backward_last(grad_half, stored, hidden_got, normed_got, moved, qkv_w)


def solution(mesh):
    placed = (
        P(None, "seq", None),
        P(None, "seq", None),
        P(),
        P("section", None),
        P("section", None),
        P("section", None, None, "tensor"),
        P("section", None, "tensor"),
        P("section", "tensor", None),
        P("section", None),
        P("section", None),
        P("section", None),
        P("section", None, "tensor"),
        P("section", "tensor"),
        P("section", "tensor", None),
        P("section", None),
    )

    def chosen(*arrays):
        pairs = mesh.shape["seq"] == 2 * arrays[0].shape[0]
        cores = mesh.shape["tensor"] == 2 and mesh.shape["section"] == 2
        heads = arrays[7].shape[1] // HEAD_DIM
        if pairs and cores and heads % 2 == 0:
            return micro_local(*arrays)
        return local(*arrays)

    return jax.shard_map(
        chosen,
        mesh=mesh,
        in_specs=placed,
        out_specs=(
            P("section", None, "seq", None),
            P("section", None, "seq", None),
            P("section", "seq"),
            P("section", "seq"),
            P("section", "seq", None, "tensor"),
            P("section", None, ("tensor", "seq")),
            P("section", ("tensor", "seq"), None),
            P("section", "seq"),
            P("section", "seq"),
            P("section", "seq"),
            P("section", "seq", "tensor"),
            P("section", ("tensor", "seq")),
            P("section", ("tensor", "seq"), None),
            P("section", "seq"),
        ),
        check_vma=False,
    )
```

```python
import math
from functools import partial

import jax
import jax.numpy as jnp
from jax import lax
from jax.experimental import pallas as pl
from jax.experimental.pallas import tpu as pltpu
from jax.sharding import PartitionSpec as P

HEAD_DIM = 64


EPS = 1e-05
NEG = -1e30


def passed_along(block, axis, distance):
    devices = range(lax.axis_size(axis))
    route = [(i - distance, i) for i in devices if i - distance in devices]
    return lax.ppermute(block, axis, route)


def layer_norm(values, gain, shift):
    mean = jnp.mean(values, axis=-1, keepdims=True)
    centred = values - mean
    spread = jnp.mean(centred * centred, axis=-1, keepdims=True)
    return centred * lax.rsqrt(spread + EPS) * gain + shift


def doc_number(positions, lengths):
    bounds = jnp.cumsum(lengths, dtype=jnp.int32)
    return jnp.sum(
        (positions[:, None] >= bounds[None, :]).astype(jnp.int32), axis=1, dtype=jnp.int32
    )


def block_width(total, tok_rows):
    return math.gcd(total // tok_rows, max(1, 1024 // tok_rows)) * tok_rows


def block_scores(query, keys, query_pos, query_doc, key_start, lengths):
    count = keys.shape[0]
    scores = jnp.einsum(
        "thd,khd->htk", query, keys, preferred_element_type=jnp.float32
    ) * HEAD_DIM ** (-0.5)
    key_pos = key_start + jnp.arange(count, dtype=jnp.int32)
    key_doc = doc_number(key_pos, lengths)
    allowed = (key_doc[None, :] == query_doc[:, None]) & (key_pos[None, :] <= query_pos[:, None])
    return (scores, allowed[None])


def split_pair(block, heads):
    count = block.shape[0]
    return (
        block[:, 0].reshape(count, heads, HEAD_DIM),
        block[:, 1].reshape(count, heads, HEAD_DIM),
    )


def attend(query, kv_all, query_pos, query_doc, lengths):
    rows, heads = (query.shape[0], query.shape[1])
    width = block_width(kv_all.shape[0], rows)
    blocks = kv_all.reshape(kv_all.shape[0] // width, width, 2, kv_all.shape[2])
    starts = jnp.arange(blocks.shape[0], dtype=jnp.int32) * width

    def total_step(carry, item):
        top, mass = carry
        block, start = item
        keys, values = split_pair(block, heads)
        scores, allowed = block_scores(query, keys, query_pos, query_doc, start, lengths)
        masked = jnp.where(allowed, scores, NEG)
        new_top = jnp.maximum(top, jnp.max(masked, axis=-1))
        weights = jnp.where(allowed, jnp.exp(masked - new_top[..., None]), 0.0)
        return ((new_top, mass * jnp.exp(top - new_top) + jnp.sum(weights, axis=-1)), None)

    start_carry = (jnp.full((heads, rows), NEG, jnp.float32), jnp.zeros((heads, rows), jnp.float32))
    (top, mass), _ = lax.scan(total_step, start_carry, (blocks, starts))
    log_total = top + jnp.log(mass)

    def value_step(running, item):
        block, start = item
        keys, values = split_pair(block, heads)
        scores, allowed = block_scores(query, keys, query_pos, query_doc, start, lengths)
        probs = jnp.where(allowed, jnp.exp(scores - log_total[..., None]), 0.0).astype(jnp.bfloat16)
        return (
            running + jnp.einsum("htk,khd->thd", probs, values, preferred_element_type=jnp.float32),
            None,
        )

    mixed, _ = lax.scan(
        value_step, jnp.zeros((rows, heads, HEAD_DIM), jnp.float32), (blocks, starts)
    )
    return (mixed, log_total)


def tensor_total(partial_value):
    return lax.psum(partial_value.astype(jnp.bfloat16), "tensor").astype(jnp.float32)


def tensor_back(partial_value):
    return lax.psum(partial_value.astype(jnp.bfloat16), "tensor").astype(jnp.float32)


def forward_layer(inputs, lengths, weights):
    (
        gain_one,
        bias_one,
        qkv_w,
        qv_b,
        out_w,
        out_b,
        gain_two,
        bias_two,
        up_w,
        up_b,
        down_w,
        down_b,
    ) = weights
    rows, width = inputs.shape
    inner = qkv_w.shape[2]
    heads = inner // HEAD_DIM
    normed = layer_norm(inputs, gain_one, bias_one).astype(jnp.bfloat16)
    projected = jnp.dot(
        normed, qkv_w.reshape(width, 3 * inner), preferred_element_type=jnp.float32
    ).reshape(rows, 3, inner)
    query = (projected[:, 0] + qv_b[0]).astype(jnp.bfloat16)
    keys = projected[:, 1].astype(jnp.bfloat16)
    values = (projected[:, 2] + qv_b[1]).astype(jnp.bfloat16)
    kv_pair = jnp.stack([keys, values], axis=1)
    kv_all = lax.all_gather(kv_pair, "seq", axis=0, tiled=True)
    query_pos = lax.axis_index("seq") * rows + jnp.arange(rows, dtype=jnp.int32)
    query_doc = doc_number(query_pos, lengths)
    mixed, log_total = attend(
        query.reshape(rows, heads, HEAD_DIM), kv_all, query_pos, query_doc, lengths
    )
    attended = mixed.reshape(rows, inner)
    attended_low = attended.astype(jnp.bfloat16)
    branch = tensor_total(jnp.dot(attended_low, out_w, preferred_element_type=jnp.float32)) + out_b
    middle = inputs + branch
    normed_two = layer_norm(middle, gain_two, bias_two).astype(jnp.bfloat16)
    hidden_pre = jnp.dot(normed_two, up_w, preferred_element_type=jnp.float32) + up_b
    hidden_low = jax.nn.gelu(hidden_pre).astype(jnp.bfloat16)
    result = middle + (
        tensor_total(jnp.dot(hidden_low, down_w, preferred_element_type=jnp.float32)) + down_b
    )
    kept = (
        inputs,
        normed,
        query,
        kv_pair,
        attended,
        log_total,
        middle,
        normed_two,
        hidden_pre,
        hidden_low,
        lengths,
        query_pos,
        query_doc,
    )
    return (result, kept)


def backward_layer(grad_out, kept, weights):
    (
        gain_one,
        bias_one,
        qkv_w,
        qv_b,
        out_w,
        out_b,
        gain_two,
        bias_two,
        up_w,
        up_b,
        down_w,
        down_b,
    ) = weights
    (
        inputs,
        normed,
        query,
        kv_pair,
        attended,
        log_total,
        middle,
        normed_two,
        hidden_pre,
        hidden_low,
        lengths,
        query_pos,
        query_doc,
    ) = kept[:13]
    kv_all = lax.all_gather(kv_pair, "seq", axis=0, tiled=True)
    single = jnp.float32
    rows, inner = attended.shape
    heads = inner // HEAD_DIM
    scale = HEAD_DIM ** (-0.5)
    down_in = grad_out.astype(jnp.bfloat16)
    down_b_grad = jnp.sum(down_in.astype(single), axis=0)
    down_w_grad = jnp.einsum("tf,td->fd", hidden_low, down_in, preferred_element_type=single)
    hidden_grad = jnp.einsum("td,fd->tf", down_in, down_w, preferred_element_type=single)
    _, gelu_back = jax.vjp(jax.nn.gelu, hidden_pre)
    pre_grad = gelu_back(hidden_grad)[0].astype(jnp.bfloat16)
    up_b_grad = jnp.sum(pre_grad.astype(single), axis=0)
    up_w_grad = jnp.einsum("td,tf->df", normed_two, pre_grad, preferred_element_type=single)
    normed_two_grad = tensor_back(
        jnp.einsum("tf,df->td", pre_grad, up_w, preferred_element_type=single)
    )
    _, norm_two_back = jax.vjp(layer_norm, middle, gain_two, bias_two)
    middle_extra, gain_two_grad, bias_two_grad = norm_two_back(normed_two_grad)
    middle_grad = grad_out + middle_extra
    branch_grad = middle_grad.astype(jnp.bfloat16)
    out_b_grad = jnp.sum(branch_grad.astype(single), axis=0)
    out_w_grad = jnp.einsum(
        "th,td->hd", attended.astype(jnp.bfloat16), branch_grad, preferred_element_type=single
    )
    attended_grad = jnp.einsum(
        "td,hd->th", branch_grad, out_w, preferred_element_type=single
    ).astype(jnp.bfloat16)
    grad_heads = attended_grad.reshape(rows, heads, HEAD_DIM)
    query_heads = query.reshape(rows, heads, HEAD_DIM)
    dot_total = jnp.sum(
        grad_heads.astype(single) * attended.reshape(rows, heads, HEAD_DIM), axis=-1
    ).T
    total = kv_all.shape[0]
    width = block_width(total, rows)
    blocks = kv_all.reshape(total // width, width, 2, inner)
    starts = jnp.arange(total // width, dtype=jnp.int32) * width

    def score_grads(block, start):
        keys, values = split_pair(block, heads)
        scores, allowed = block_scores(query_heads, keys, query_pos, query_doc, start, lengths)
        probs = jnp.where(allowed, jnp.exp(scores - log_total[..., None]), 0.0)
        prob_grad = jnp.einsum("thd,khd->htk", grad_heads, values, preferred_element_type=single)
        score_grad = jnp.where(allowed, probs * (prob_grad - dot_total[..., None]), 0.0).astype(
            jnp.bfloat16
        )
        return (keys, probs, score_grad)

    def joined_step(running, item):
        block, start = item
        keys, probs, score_grad = score_grads(block, start)
        running = running + jnp.einsum(
            "htk,khd->thd", score_grad, keys, preferred_element_type=single
        )
        key_grad = (
            jnp.einsum("htk,thd->khd", score_grad, query_heads, preferred_element_type=single)
            * scale
        )
        value_grad = jnp.einsum(
            "htk,thd->khd", probs.astype(jnp.bfloat16), grad_heads, preferred_element_type=single
        )
        return (
            running,
            jnp.stack([key_grad.reshape(width, inner), value_grad.reshape(width, inner)], axis=1),
        )

    query_acc, terms = lax.scan(
        joined_step, jnp.zeros((rows, heads, HEAD_DIM), single), (blocks, starts)
    )
    terms_all = terms.reshape(total, 2, inner)
    pair_grad = lax.psum_scatter(terms_all, "seq", scatter_dimension=0, tiled=True).astype(
        jnp.bfloat16
    )
    query_grad = (query_acc * scale).reshape(rows, inner).astype(jnp.bfloat16)
    proj_grad = jnp.concatenate([query_grad[:, None], pair_grad], axis=1)
    qv_b_grad = jnp.stack(
        [
            jnp.sum(query_grad.astype(single), axis=0),
            jnp.sum(pair_grad[:, 1].astype(single), axis=0),
        ]
    )
    qkv_w_grad = jnp.einsum("td,tch->dch", normed, proj_grad, preferred_element_type=single)
    normed_grad = tensor_back(
        jnp.einsum("tch,dch->td", proj_grad, qkv_w, preferred_element_type=single)
    )
    _, norm_one_back = jax.vjp(layer_norm, inputs, gain_one, bias_one)
    input_extra, gain_one_grad, bias_one_grad = norm_one_back(normed_grad)
    input_grad = middle_grad + input_extra
    grads = (
        gain_one_grad,
        bias_one_grad,
        qkv_w_grad,
        qv_b_grad,
        out_w_grad,
        out_b_grad,
        gain_two_grad,
        bias_two_grad,
        up_w_grad,
        up_b_grad,
        down_w_grad,
        down_b_grad,
    )
    return (input_grad, grads)


def local(
    block_input,
    out_grad,
    doc_lengths,
    ln1_gain,
    ln1_bias,
    qkv_weight,
    qv_bias,
    out_weight,
    out_bias,
    ln2_gain,
    ln2_bias,
    fc1_weight,
    fc1_bias,
    fc2_weight,
    fc2_bias,
):
    weights = (
        ln1_gain[0],
        ln1_bias[0],
        qkv_weight[0],
        qv_bias[0],
        out_weight[0],
        out_bias[0],
        ln2_gain[0],
        ln2_bias[0],
        fc1_weight[0],
        fc1_bias[0],
        fc2_weight[0],
        fc2_bias[0],
    )
    micro_count = block_input.shape[0]
    first = lax.axis_index("section") == 0
    received = jnp.zeros(block_input.shape[1:], jnp.bfloat16)
    outputs = []
    stored = []
    for tick in range(micro_count + 1):
        own = min(tick, micro_count - 1)
        prior = max(tick - 1, 0)
        layer_in = jnp.where(first, block_input[own], received).astype(jnp.float32)
        lengths = jnp.where(first, doc_lengths[own], doc_lengths[prior])
        result, kept = forward_layer(layer_in, lengths, weights)
        result_low = result.astype(jnp.bfloat16)
        outputs.append(result_low)
        stored.append(kept)
        received = passed_along(result_low, "section", 1)
    layer_out = jnp.stack(
        [jnp.where(first, outputs[m], outputs[m + 1]) for m in range(micro_count)]
    )
    totals = jax.tree.map(lambda w: jnp.zeros(w.shape, jnp.float32), weights)
    returned = jnp.zeros(block_input.shape[1:], jnp.bfloat16)
    input_grads = []
    for tick in range(micro_count + 1):
        mine = min(tick, micro_count - 1)
        valid = jnp.where(first, float(tick >= 1), float(tick < micro_count)).astype(jnp.float32)
        upstream = jnp.where(first, returned, out_grad[mine]).astype(jnp.float32)
        kept = jax.tree.map(
            lambda early, late: jnp.where(first, early, late),
            stored[max(tick - 1, 0)],
            stored[min(tick + 1, micro_count)],
        )
        input_grad, grads = backward_layer(upstream, kept, weights)
        totals = jax.tree.map(lambda total, grad: total + valid * grad, totals, grads)
        grad_low = input_grad.astype(jnp.bfloat16)
        input_grads.append(grad_low)
        returned = passed_along(grad_low, "section", -1)
    layer_grad = jnp.stack(
        [jnp.where(first, input_grads[m + 1], input_grads[m]) for m in range(micro_count)]
    )
    (
        gain_one_sum,
        bias_one_sum,
        qkv_sum,
        qv_sum,
        out_w_sum,
        out_b_sum,
        gain_two_sum,
        bias_two_sum,
        up_w_sum,
        up_b_sum,
        down_w_sum,
        down_b_sum,
    ) = totals
    summed = (
        lax.psum_scatter(gain_one_sum, "seq", scatter_dimension=0, tiled=True),
        lax.psum_scatter(bias_one_sum, "seq", scatter_dimension=0, tiled=True),
        lax.psum_scatter(qkv_sum, "seq", scatter_dimension=0, tiled=True),
        lax.psum_scatter(qv_sum, "seq", scatter_dimension=1, tiled=True),
        lax.psum_scatter(out_w_sum, "seq", scatter_dimension=0, tiled=True),
        lax.psum_scatter(out_b_sum, "seq", scatter_dimension=0, tiled=True),
        lax.psum_scatter(gain_two_sum, "seq", scatter_dimension=0, tiled=True),
        lax.psum_scatter(bias_two_sum, "seq", scatter_dimension=0, tiled=True),
        lax.psum_scatter(up_w_sum, "seq", scatter_dimension=0, tiled=True),
        lax.psum_scatter(up_b_sum, "seq", scatter_dimension=0, tiled=True),
        lax.psum_scatter(down_w_sum, "seq", scatter_dimension=0, tiled=True),
        lax.psum_scatter(down_b_sum, "seq", scatter_dimension=0, tiled=True),
    )
    return (
        layer_out[None],
        layer_grad[None],
        summed[0][None],
        summed[1][None],
        summed[2][None],
        summed[3][None],
        summed[4][None],
        summed[5][None],
        summed[6][None],
        summed[7][None],
        summed[8][None],
        summed[9][None],
        summed[10][None],
        summed[11][None],
    )


def swapped_cores(block):
    return lax.ppermute(block, "tensor", [(0, 1), (1, 0)])


def swapped_groups(block):
    return lax.ppermute(block, "seq", [(i, i ^ 1) for i in range(lax.axis_size("seq"))])


def together(*values):
    return lax.optimization_barrier(values)


def picked(block, which, axis):
    return lax.dynamic_index_in_dim(block, which, axis, keepdims=False)


def in_order(mine, other, place, axis):
    return jnp.where(
        place == 0, jnp.stack([mine, other], axis=axis), jnp.stack([other, mine], axis=axis)
    )


def micro_routes(count):
    groups = lax.axis_size("seq") // count
    return [
        [
            (m * groups + g, (m + step) % count * groups + g)
            for m in range(count)
            for g in range(groups)
        ]
        for step in range(1, count)
    ]


def from_micros(blocks, micro, count):
    parts = [picked(blocks, micro, 0)]
    for step, route in enumerate(micro_routes(count), 1):
        parts.append(lax.ppermute(picked(blocks, (micro + step) % count, 0), "seq", route))
    return jnp.stack(parts, axis=0)


def across_micros(blocks, micro, count):
    turned = jnp.roll(from_micros(blocks, micro, count)[::-1], 1, axis=0)
    return lax.dynamic_slice_in_dim(
        jnp.concatenate([turned, turned], axis=0), (count - micro) % count, count, axis=0
    )


def swapped_micros(block, bit, count):
    groups = lax.axis_size("seq") // count
    return lax.ppermute(
        block,
        "seq",
        [((m * groups) + g, (m ^ bit) * groups + g) for m in range(count) for g in range(groups)],
    )


def joined(kept, got):
    return (kept.astype(SINGLE) + got.astype(SINGLE)).astype(LOW)


SINGLE = jnp.float32
LOW = jnp.bfloat16
VMEM_BYTES = 32 * 1024 * 1024
NT = (((1,), (1,)), ((), ()))
TN = (((0,), (0,)), ((), ()))
SCALARS = pl.BlockSpec(memory_space=pltpu.SMEM)
WHOLE = pl.BlockSpec(memory_space=pltpu.VMEM)


def kernel_call(body, name, shapes, scalars, arrays, flops, scratch=()):
    outs = [jax.ShapeDtypeStruct(shape, dtype) for shape, dtype in shapes]
    moved = sum(math.prod(a.shape) * a.dtype.itemsize for a in (*arrays, *outs))
    return pl.pallas_call(
        body,
        out_shape=outs,
        in_specs=[SCALARS] + [WHOLE] * len(arrays),
        out_specs=[WHOLE] * len(outs),
        scratch_shapes=list(scratch),
        compiler_params=pltpu.CompilerParams(vmem_limit_bytes=VMEM_BYTES),
        cost_estimate=pl.CostEstimate(flops=flops, bytes_accessed=moved, transcendentals=0),
        name=name,
    )(scalars, *arrays)


def row_norm(values):
    mean = jnp.mean(values, axis=-1, keepdims=True)
    centred = values - mean
    inverse = lax.rsqrt(jnp.mean(centred * centred, axis=-1, keepdims=True) + EPS)
    return centred * inverse, inverse


def norm_back(shaped, inverse, scaled):
    return inverse * (
        scaled
        - jnp.mean(scaled, axis=-1, keepdims=True)
        - shaped * jnp.mean(scaled * shaped, axis=-1, keepdims=True)
    )


def either(place, mine, other):
    return jnp.where(place == 0, mine, other), jnp.where(place == 0, other, mine)


def column_sum(values):
    return jnp.sum(values, axis=0, keepdims=True)


def norm_kernel(place_ref, x_ref, gain_ref, bias_ref, out_ref):
    for block in range(x_ref.shape[0]):
        shaped, _ = row_norm(x_ref[block].astype(SINGLE))
        out_ref[block] = (shaped * gain_ref[...] + bias_ref[...]).astype(LOW)


def doc_mask(place_ref, docs, first, rows, count):
    key_pos = lax.broadcasted_iota(jnp.int32, (rows, count), 1)
    query_pos = first + lax.broadcasted_iota(jnp.int32, (rows, 1), 0)
    start = jnp.zeros((rows, 1), jnp.int32)
    bound = jnp.int32(0)
    for doc in range(docs):
        bound = bound + place_ref[3 + doc]
        start = jnp.maximum(start, jnp.where(query_pos >= bound, bound, 0))
    return (key_pos <= query_pos) & (key_pos >= start)


def put_side(ref, block, blocks, value):
    side, at = divmod(block, blocks // 2)
    own = value.shape[1]
    ref[at, :, side * own : (side + 1) * own] = value


def from_side(ref, block, blocks):
    side, at = divmod(block, blocks // 2)
    own = ref.shape[2] // 2
    return ref[at, :, side * own : (side + 1) * own]


def attend_kernel(heads, docs, kept, place_ref, *refs):
    core, group = place_ref[0], place_ref[1]
    mine, from_core, from_group, from_far = [refs[at : at + 2] for at in range(0, 8, 2)]
    w_ref, b_ref, out_ref, send_ref, *rest = refs[8:]
    if kept:
        qkv_ref, n_ref, lse_ref = rest
    else:
        own_ref, qkv_ref, n_ref, lse_ref = rest
        own = own_ref.shape[1] // 3
        for part in range(3):
            own_ref[:, part * own : (part + 1) * own] = jnp.where(
                group == 0, w_ref[part, :, :own], w_ref[part, :, own:]
            )
        w_ref = own_ref
    each, half, width = mine[0].shape
    blocks = 2 * each
    rows = 4 * half
    inner = heads * HEAD_DIM
    for block in range(blocks):
        piece, at = divmod(block, each)
        near = either(core, mine[piece][at], from_core[piece][at])
        far = either(core, from_group[piece][at], from_far[piece][at])
        near, far = jnp.concatenate(near, axis=0), jnp.concatenate(far, axis=0)
        n_ref[block * rows : (block + 1) * rows, :] = jnp.concatenate(
            either(group, near, far), axis=0
        )
    for i in range(0, blocks * rows, rows):
        made = jnp.dot(n_ref[i : i + rows, :], w_ref[...], preferred_element_type=SINGLE)
        qkv_ref[i : i + rows, :] = (made + b_ref[...]).astype(LOW)
    lane = lax.broadcasted_iota(jnp.int32, (rows, 128), 1)
    for block in range(blocks):
        i = block * rows
        count = i + rows
        allowed = doc_mask(place_ref, docs, i, rows, count)
        totals = jnp.zeros((rows, 128), SINGLE)
        mixed = []
        for h in range(heads):
            at = h * HEAD_DIM
            query = qkv_ref[i:count, at : at + HEAD_DIM] * LOW(HEAD_DIM**-0.5)
            keys = qkv_ref[:count, inner + at : inner + at + HEAD_DIM]
            values = qkv_ref[:count, 2 * inner + at : 2 * inner + at + HEAD_DIM]
            values = jnp.concatenate([values, jnp.ones((count, HEAD_DIM), LOW)], axis=1)
            scores = lax.dot_general(query, keys, NT, preferred_element_type=SINGLE)
            scores = jnp.where(allowed, scores, NEG)
            top = jnp.max(scores, axis=1, keepdims=True)
            weights = jnp.exp(scores - top).astype(LOW)
            made = jnp.dot(weights, values, preferred_element_type=SINGLE)
            mass = made[:, HEAD_DIM : HEAD_DIM + 1]
            mixed.append(made[:, :HEAD_DIM] * (1.0 / mass))
            totals = jnp.where(lane == h, top + jnp.log(mass), totals)
        out = jnp.concatenate(mixed, axis=1).astype(LOW)
        out_ref[block], send = either(group, out[: rows // 2], out[rows // 2 :])
        put_side(send_ref, block, blocks, send)
        if kept:
            lse_ref[i:count, :] = totals


def attend_back_kernel(heads, docs, last, place_ref, qkv_ref, n_ref, w_ref, do_ref, do_far_ref, out_ref, send_ref, lse_ref, keep_ref, give_ref, *rest):
    if last:
        dw_ref, db_ref, acc_ref = rest
    else:
        (acc_ref,) = rest
    core, group = place_ref[0], place_ref[1]
    blocks = out_ref.shape[0]
    tokens = n_ref.shape[0]
    rows = tokens // blocks
    inner = heads * HEAD_DIM
    for block in range(blocks - 1, -1, -1):
        i = block * rows
        count = i + rows
        allowed = doc_mask(place_ref, docs, i, rows, count)
        far = from_side(do_far_ref, block, blocks)
        grads = jnp.concatenate(either(group, do_ref[block], far), axis=0)
        far = from_side(send_ref, block, blocks)
        outs = jnp.concatenate(either(group, out_ref[block], far), axis=0)
        for h in range(heads):
            at = h * HEAD_DIM
            query = qkv_ref[i:count, at : at + HEAD_DIM] * LOW(HEAD_DIM**-0.5)
            keys = qkv_ref[:count, inner + at : inner + at + HEAD_DIM]
            values = qkv_ref[:count, 2 * inner + at : 2 * inner + at + HEAD_DIM]
            grad = grads[:, at : at + HEAD_DIM]
            out = outs[:, at : at + HEAD_DIM]
            dots = jnp.sum(grad.astype(SINGLE) * out.astype(SINGLE), axis=1, keepdims=True)
            scores = lax.dot_general(query, keys, NT, preferred_element_type=SINGLE)
            probs = jnp.exp(jnp.where(allowed, scores, NEG) - lse_ref[i:count, h : h + 1])
            prob_grad = lax.dot_general(grad, values, NT, preferred_element_type=SINGLE)
            score_grad = (probs * (prob_grad - dots)).astype(LOW)
            query_grad = jnp.dot(score_grad, keys, preferred_element_type=SINGLE)
            acc_ref[at : at + HEAD_DIM, i:count] = query_grad.T * HEAD_DIM**-0.5
            at += inner
            key_grad = jnp.dot(query.T, score_grad, preferred_element_type=SINGLE)
            value_grad = jnp.dot(grad.T, probs.astype(LOW), preferred_element_type=SINGLE)
            if block == blocks - 1:
                acc_ref[at : at + HEAD_DIM, :] = key_grad
                acc_ref[at + inner : at + inner + HEAD_DIM, :] = value_grad
            else:
                acc_ref[at : at + HEAD_DIM, :count] += key_grad
                acc_ref[at + inner : at + inner + HEAD_DIM, :count] += value_grad
    for block in range(blocks):
        i = block * rows
        part = acc_ref[:, i : i + rows].T.astype(LOW)
        made = lax.dot_general(part, w_ref[...], NT, preferred_element_type=SINGLE).astype(LOW)
        near, far = either(group, made[: rows // 2], made[rows // 2 :])
        for place, side in ((0, near), (1, far)):
            keep_ref[place, block], give_ref[place, block] = either(
                core, side[: rows // 4], side[rows // 4 :]
            )
    if last:
        low = acc_ref[...].astype(LOW)
        dw_ref[...] = jnp.dot(low, n_ref[...], preferred_element_type=SINGLE).T.astype(LOW)
        ones = jnp.ones((db_ref.shape[0], low.shape[1]), LOW)
        db_ref[...] = lax.dot_general(ones, low, NT, preferred_element_type=SINGLE)


def project_kernel(place_ref, mine_ref, far_ref, w_ref, out_ref, *rest):
    group = place_ref[1]
    blocks, rows, own = mine_ref.shape
    near_w = w_ref[pl.ds(pl.multiple_of(group * own, own), own), :]
    far_w = w_ref[pl.ds(pl.multiple_of((1 - group) * own, own), own), :]
    for first in range(0, blocks, 2):
        pair = (first, first + 1)
        mine = jnp.concatenate([mine_ref[block] for block in pair], axis=0)
        far = jnp.concatenate([from_side(far_ref, block, blocks) for block in pair], axis=0)
        at = slice(first * rows, (first + 2) * rows)
        out_ref[at, :] = (
            jnp.dot(mine, near_w, preferred_element_type=SINGLE)
            + jnp.dot(far, far_w, preferred_element_type=SINGLE)
        ).astype(LOW)
        if rest:
            rest[0][at, :own], rest[0][at, own:] = either(group, mine, far)


def halves(core, mine_ref, other_ref, block):
    return jnp.concatenate(either(core, mine_ref[block], other_ref[block]), axis=0)


def feed_kernel(kept, place_ref, x_ref, x_far_ref, part_ref, far_ref, out_b_ref, gain_ref, bias_ref, up_ref, up_b_ref, down_ref, down_b_ref, base_ref, give_ref, *rest):
    core = place_ref[0]
    blocks, half, _ = x_ref.shape
    step = 2 * half
    for first in range(0, blocks, 2):
        rows = slice(first * step, (first + 2) * step)
        x = jnp.concatenate(
            [halves(core, x_ref, x_far_ref, block) for block in (first, first + 1)], axis=0
        )
        middle = (
            x.astype(SINGLE)
            + (part_ref[rows, :].astype(SINGLE) + far_ref[rows, :].astype(SINGLE))
            + out_b_ref[...]
        )
        shaped, _ = row_norm(middle)
        normed = (shaped * gain_ref[...] + bias_ref[...]).astype(LOW)
        pre = jnp.dot(normed, up_ref[...], preferred_element_type=SINGLE) + up_b_ref[...]
        hidden = jax.nn.gelu(pre).astype(LOW)
        made = jnp.dot(hidden, down_ref[...], preferred_element_type=SINGLE)
        if kept:
            middle_ref, normed_ref, pre_ref, own_ref, other_ref = rest
            middle_ref[rows, :] = middle
            normed_ref[rows, :] = normed
            pre_ref[rows, :] = pre.astype(LOW)
            cut = own_ref.shape[1]
            own_ref[rows, :], other_ref[rows, :] = hidden[:, :cut], hidden[:, cut:]
        for place in (0, 1):
            at = place * step
            mine, other = either(core, made[at : at + half], made[at + half : at + step])
            own = jnp.where(core == 0, middle[at : at + half], middle[at + half : at + step])
            base_ref[first + place] = own + mine + down_b_ref[...]
            give_ref[first + place] = other.astype(LOW)


def gelu_slope(value):
    rate = math.sqrt(2.0 / math.pi)
    squared = value * value
    bent = jnp.tanh(rate * value * (1.0 + 0.044715 * squared))
    return 0.5 * (1.0 + bent) + 0.5 * value * (1.0 - bent * bent) * (
        rate * (1.0 + 3 * 0.044715 * squared)
    )


def feed_back_kernel(last, place_ref, dy_ref, dy_far_ref, pre_ref, up_ref, down_ref, part_ref, dz_ref, *rest):
    core = place_ref[0]
    blocks, half, _ = dy_ref.shape
    step = 2 * half
    up_sum, down_sum = 0.0, 0.0
    for first in range(0, blocks, 2):
        rows = slice(first * step, (first + 2) * step)
        dz = jnp.concatenate(
            [halves(core, dy_ref, dy_far_ref, block) for block in (first, first + 1)], axis=0
        )
        dz_ref[rows, :] = dz
        grad = lax.dot_general(dz, down_ref[...], NT, preferred_element_type=SINGLE)
        pre_grad = (grad * gelu_slope(pre_ref[rows, :].astype(SINGLE))).astype(LOW)
        part_ref[rows, :] = lax.dot_general(
            pre_grad, up_ref[...], NT, preferred_element_type=SINGLE
        ).astype(LOW)
        if last:
            cut = rest[0].shape[1]
            rest[0][rows, :], rest[1][rows, :] = pre_grad[:, :cut], pre_grad[:, cut:]
            up_sum = up_sum + column_sum(pre_grad.astype(SINGLE))
            down_sum = down_sum + column_sum(dz.astype(SINGLE))
    if last:
        rest[2][...] = up_sum
        rest[3][...] = down_sum


def project_back_kernel(last, place_ref, dz_ref, middle_ref, part_ref, far_ref, gain_ref, w_ref, mine_ref, give_ref, half_ref, *rest):
    core, group = place_ref[0], place_ref[1]
    own = mine_ref.shape[2]
    blocks, half, _ = half_ref.shape
    step = 2 * half
    near_w = w_ref[pl.ds(pl.multiple_of(group * own, own), own), :]
    far_w = w_ref[pl.ds(pl.multiple_of((1 - group) * own, own), own), :]
    sums = [0.0, 0.0, 0.0]
    for first in range(0, blocks, 2):
        rows = slice(first * step, (first + 2) * step)
        shaped, inverse = row_norm(middle_ref[rows, :])
        grad = part_ref[rows, :].astype(SINGLE) + far_ref[rows, :].astype(SINGLE)
        total = dz_ref[rows, :].astype(SINGLE) + norm_back(shaped, inverse, grad * gain_ref[...])
        low = total.astype(LOW)
        mine = lax.dot_general(low, near_w, NT, preferred_element_type=SINGLE).astype(LOW)
        give = lax.dot_general(low, far_w, NT, preferred_element_type=SINGLE).astype(LOW)
        for place in (0, 1):
            at = place * step
            mine_ref[first + place] = mine[at : at + step]
            put_side(give_ref, first + place, blocks, give[at : at + step])
            half_ref[first + place] = jnp.where(
                core == 0, total[at : at + half], total[at + half : at + step]
            )
        if last:
            rest[0][rows, :] = low
            for at, part in enumerate((low.astype(SINGLE), grad * shaped, grad)):
                sums[at] = sums[at] + column_sum(part)
    if last:
        for at in range(3):
            rest[1][at : at + 1, :] = sums[at]


def norm_back_kernel(last, place_ref, x_ref, keep_ref, core_ref, group_ref, rest_ref, gain_ref, dx_ref, *rest):
    sums = [0.0, 0.0]
    for block in range(x_ref.shape[0]):
        shaped, inverse = row_norm(x_ref[block].astype(SINGLE))
        grad = (
            keep_ref[0, block].astype(SINGLE)
            + core_ref[0, block].astype(SINGLE)
            + group_ref[block].astype(SINGLE)
        )
        back = norm_back(shaped, inverse, grad * gain_ref[...])
        dx_ref[block] = (rest_ref[block] + back).astype(LOW)
        if last:
            for at, part in enumerate((grad * shaped, grad)):
                sums[at] = sums[at] + column_sum(part)
    if last:
        for at in range(2):
            rest[0][at : at + 1, :] = sums[at]


def place_kernel(place_ref, mine_ref, other_ref, out_ref):
    core, micro = place_ref[0], place_ref[2]
    blocks, half, _ = mine_ref.shape
    for step in range(blocks):
        at = lax.rem(micro + blocks - step, blocks)
        out_ref[at] = halves(core, mine_ref, other_ref, step)


def pack_kernel(place_ref, one_ref, one_far_ref, branch_ref, down_ref, up_ref, qkv_ref, out_ref):
    group = place_ref[1]
    count = out_ref.shape[0]
    cut = one_ref.shape[1] // count
    wide = up_ref.shape[1] // count
    own = qkv_ref.shape[1] // 3
    slim = 2 * own // count
    full = jnp.concatenate(
        [one_ref[...] + one_far_ref[...], branch_ref[...], down_ref[...]], axis=0
    )
    out_ref[...] = jnp.zeros_like(out_ref)
    nothing = jnp.zeros((1, own), SINGLE)
    hidden = up_ref.shape[1]
    by_group = either(group, up_ref[:, : hidden // 2], up_ref[:, hidden // 2 :])
    for at in range(count):
        out_ref[at, 0:6, 0:cut] = full[:, at * cut : (at + 1) * cut].astype(LOW)
        up = by_group[at % 2][:, at // 2 * wide : (at // 2 + 1) * wide]
        out_ref[at, 6:7, 0:wide] = up.astype(LOW)
    for row, part in ((7, 0), (8, 2)):
        mine = qkv_ref[0:1, part * own : (part + 1) * own]
        both = jnp.concatenate(either(group, mine, nothing), axis=1)
        for at in range(count):
            out_ref[at, row : row + 1, 0:slim] = both[:, at * slim : (at + 1) * slim].astype(LOW)


def unpack_kernel(place_ref, kept_ref, got_ref, *out_refs):
    total = kept_ref[...].astype(SINGLE) + got_ref[...].astype(SINGLE)
    for row in range(6):
        out_refs[row][...] = total[row : row + 1, : out_refs[row].shape[1]]
    out_refs[6][...] = total[6:7, : out_refs[6].shape[1]]
    out_refs[7][...] = total[7:9, : out_refs[7].shape[1]]


def reorder_kernel(blocks, place_ref, up_ref, bias_ref, down_ref, up_out, bias_out, down_out):
    group = place_ref[1]
    hidden, _ = down_ref.shape
    cut = hidden // blocks
    for at in range(blocks // 2):
        near = slice(2 * at * cut, (2 * at + 1) * cut)
        far = slice((2 * at + 1) * cut, (2 * at + 2) * cut)
        first = slice(at * cut, (at + 1) * cut)
        second = slice(hidden // 2 + at * cut, hidden // 2 + (at + 1) * cut)
        for source, out in ((up_ref, up_out), (bias_ref, bias_out)):
            out[:, first], out[:, second] = either(group, source[:, near], source[:, far])
        down_out[first, :], down_out[second, :] = either(group, down_ref[near, :], down_ref[far, :])


def columns_kernel(blocks, place_ref, mine_ref, got_ref, out_ref):
    group = place_ref[1]
    cut = out_ref.shape[1] // blocks
    both = either(group, mine_ref[...], got_ref[...].astype(SINGLE))
    for at in range(blocks):
        piece = slice(at // 2 * cut, (at // 2 + 1) * cut)
        out_ref[:, at * cut : (at + 1) * cut] = both[at % 2][:, piece]


def heads_kernel(place_ref, mine_ref, got_ref, out_ref):
    group = place_ref[1]
    own = mine_ref.shape[1] // 3
    for part in range(3):
        at = slice(part * own, (part + 1) * own)
        out_ref[:, part, :] = jnp.concatenate(
            either(group, mine_ref[:, at], got_ref[:, at].astype(SINGLE)), axis=1
        )


def micro_local(
    block_input,
    out_grad,
    doc_lengths,
    ln1_gain,
    ln1_bias,
    qkv_weight,
    qv_bias,
    out_weight,
    out_bias,
    ln2_gain,
    ln2_bias,
    fc1_weight,
    fc1_bias,
    fc2_weight,
    fc2_bias,
):
    micros, rows, width = block_input.shape
    size = lax.axis_size("seq")
    place = lax.axis_index("seq")
    groups = size // micros
    micro, group = place // groups, place % groups
    core = lax.axis_index("tensor")
    first = lax.axis_index("section") == 0
    inner = out_weight.shape[1]
    own = inner // groups
    heads = own // HEAD_DIM
    hidden = fc1_weight.shape[2]
    docs = doc_lengths.shape[1]
    tokens = rows * size
    local_rows = tokens // groups
    half = rows // 2
    out_w, up_w, down_w = out_weight[0], fc1_weight[0], fc2_weight[0]
    qkv_w = jnp.transpose(qkv_weight[0], (1, 0, 2))
    qv_own = picked(qv_bias[0].reshape(2, groups, own), group, 1)
    qkv_b = jnp.concatenate([qv_own[0], jnp.zeros((own,), SINGLE), qv_own[1]])[None]
    scalars = jnp.concatenate(
        [jnp.stack([core, group, micro]).astype(jnp.int32), picked(doc_lengths, micro, 0)]
    )
    half_shape = (micros, half, width)
    up_w, up_b, down_w = kernel_call(
        partial(reorder_kernel, size),
        "reorder",
        [(up_w.shape, LOW), (fc1_bias.shape, SINGLE), (down_w.shape, LOW)],
        scalars,
        [up_w, fc1_bias, down_w],
        0,
    )
    head_shape = (micros, rows, own)
    side_shape = (micros // 2, rows, 2 * own)
    dense = 2 * local_rows * width
    pairs = 2 * heads * HEAD_DIM * tokens * tokens * 5 // 8

    def run(body, name, shapes, arrays, flops, scratch=()):
        return kernel_call(body, name, shapes, scalars, arrays, flops, scratch)

    def in_pieces(block):
        cut = block.shape[0] // 2
        return [block[:cut], block[cut:]]

    def normed_once(mine):
        return run(
            norm_kernel, "norm", [(mine.shape, LOW)], [mine, ln1_gain, ln1_bias], 8 * mine.size
        )[0]

    def forward(pieces, kept, qkv_w):
        mine = jnp.concatenate(pieces, axis=0)
        normed = [normed_once(piece) for piece in pieces]
        core_half = [swapped_cores(piece) for piece in normed]
        group_half = [swapped_groups(piece) for piece in normed]
        far_half = [swapped_cores(piece) for piece in group_half]
        *pieces, other = together(*normed, *core_half, *group_half, *far_half, swapped_cores(mine))
        made = [((tokens, 3 * own), LOW), ((tokens, width), LOW), ((tokens, 128), SINGLE)]
        out = run(
            partial(attend_kernel, heads, docs, kept),
            "attend",
            [(head_shape, LOW), (side_shape, LOW)]
            + (made if kept else [((width, 3 * own), LOW)]),
            [*pieces, qkv_w, qkv_b],
            2 * pairs + dense * 6 * own,
            () if kept else [pltpu.VMEM(*item) for item in made],
        )
        got = swapped_groups(out[1])
        part, *mixed = run(
            project_kernel,
            "project",
            [((local_rows, width), LOW)] + ([((local_rows, inner), LOW)] if kept else []),
            [out[0], got, out_w],
            dense * inner,
        )
        far_part = swapped_cores(part)
        saved = [
            ((local_rows, width), SINGLE),
            ((local_rows, width), LOW),
            ((local_rows, hidden), LOW),
            ((local_rows, hidden // 2), LOW),
            ((local_rows, hidden // 2), LOW),
        ]
        base, give, *rest = run(
            partial(feed_kernel, kept),
            "feed",
            [(half_shape, SINGLE), (half_shape, LOW)] + (saved if kept else []),
            [
                mine,
                other,
                part,
                far_part,
                out_bias,
                ln2_gain,
                ln2_bias,
                up_w,
                up_b,
                down_w,
                fc2_bias,
            ],
            2 * dense * hidden,
        )
        result = (base + swapped_cores(give).astype(SINGLE)).astype(LOW)
        return result, (mine, out, mixed, rest)

    def feed_back(grad_half, stored, last):
        pre = stored[3][2]
        extra = [((local_rows, hidden // 2), LOW)] * 2 + [
            ((1, hidden), SINGLE),
            ((1, width), SINGLE),
        ]
        return run(
            partial(feed_back_kernel, last),
            "feed_back",
            [((local_rows, width), LOW)] * 2 + (extra if last else []),
            [grad_half, swapped_cores(grad_half), pre, up_w, down_w],
            2 * dense * hidden,
        )

    def project_back(part, far_part, dz, stored, last):
        extra = [((local_rows, width), LOW), ((3, width), SINGLE)]
        return run(
            partial(project_back_kernel, last),
            "project_back",
            [(head_shape, LOW), (side_shape, LOW), (half_shape, SINGLE)]
            + (extra if last else []),
            [dz, stored[3][0], part, far_part, ln2_gain, out_w],
            dense * inner,
        )

    def attend_back(do_mine, do_got, stored, last, qkv_w):
        out_mine, out_send, qkv, normed, totals = stored[1]
        extra = [((width, 3 * own), LOW), ((8, 3 * own), SINGLE)]
        return run(
            partial(attend_back_kernel, heads, docs, last),
            "attend_back",
            [((2, *half_shape), LOW)] * 2 + (extra if last else []),
            [qkv, normed, qkv_w, do_mine, do_got, out_mine, out_send, totals],
            5 * pairs + dense * 6 * own,
            [pltpu.VMEM((3 * own, tokens), SINGLE)],
        )

    def core_sum(keep, give):
        core_got = swapped_cores(give)
        return core_got, joined(keep[1], core_got[1])

    def norm_back_once(mine, keep, core_got, group_got, rest_half, last):
        return run(
            partial(norm_back_kernel, last),
            "norm_back",
            [(mine.shape, LOW)] + ([((2, width), SINGLE)] if last else []),
            [mine, keep, core_got, group_got, rest_half, ln1_gain],
            20 * mine.size,
        )

    def backward(grad_half, stored, qkv_w):
        hidden_far = stored[3][4]
        cut = local_rows // 4
        short = 3 * cut // 4
        hidden_one = swapped_groups(hidden_far[:short])
        part, dz = feed_back(grad_half, stored, False)
        part, dz, hidden_one = together(part, dz, hidden_one)
        do_mine, do_give, rest_half = project_back(part, swapped_cores(part), dz, stored, False)
        do_got, hidden_far = together(swapped_groups(do_give), hidden_far)
        hidden_two = swapped_groups(hidden_far[short : short + 2 * cut])
        keep, give = attend_back(do_mine, do_got, stored, False, qkv_w)
        keep, give, hidden_two = together(keep, give, hidden_two)
        dx = []
        for piece in range(2):
            at = slice(piece * micros // 2, (piece + 1) * micros // 2)
            near, far = keep[:, at], swapped_cores(give[:, at])
            group_got = swapped_groups(joined(near[1], far[1]))
            dx += norm_back_once(
                stored[0][at], near, far, group_got, rest_half[at], False
            )
        return dx, [hidden_one, hidden_two], hidden_far[short + 2 * cut :]

    def weight_grad(*terms):
        made = sum(
            lax.dot_general(left, right, TN, preferred_element_type=SINGLE)
            for left, right in terms
        )
        return made.astype(LOW).reshape(2, 2, -1, made.shape[1])

    def group_parts(parts):
        return picked(parts, group, 2), picked(parts, 1 - group, 2)

    def near_parts(parts):
        return picked(parts, micro % 2, 1), picked(parts, 1 - micro % 2, 1)

    def far_parts(parts):
        return picked(parts, micro // 2, 0), picked(parts, 1 - micro // 2, 0)

    def near_swap(give):
        return swapped_micros(give, 1, micros)

    def far_swap(give):
        return swapped_micros(give, 2, micros)

    def total(kept, got):
        return kept.astype(SINGLE) + got.astype(SINGLE)

    def backward_last(grad_half, stored, hidden_got, normed_got, final, qkv_w):
        normed_two, hidden_own = stored[3][1], stored[3][3]
        cut = micros // 2
        dz_one = swapped_groups(grad_half[:cut])
        part, dz, pre_own, pre_give, up_sum, down_sum = feed_back(grad_half, stored, True)
        part, dz, dz_one, dz_two = together(part, dz, dz_one, grad_half[cut:])
        dz_two = swapped_groups(dz_two)
        do_mine, do_give, rest_half, branch, branch_sums = project_back(
            part, swapped_cores(part), dz, stored, True
        )
        do_give, dz_two = together(do_give, dz_two)

        dz_far = jnp.concatenate([dz_one, dz_two], axis=0)
        dz_far = in_order(dz_far, swapped_cores(dz_far), core, 1).reshape(local_rows, width)
        down_keep, down_give = near_parts(weight_grad((hidden_own, dz), (hidden_got, dz_far)))
        do_got, down_give, pre_give = together(swapped_groups(do_give), down_give, pre_give)

        cut = local_rows // 2
        pre_one = swapped_groups(pre_give[:cut])
        near_down = near_swap(down_give)
        keep, give, qkv_part, qkv_sums = attend_back(do_mine, do_got, stored, True, qkv_w)
        keep, give, qkv_part, near_down, pre_one, branch, final, normed_got = together(
            keep, give, qkv_part, near_down, pre_one, branch, final, normed_got
        )

        core_got, group_give = core_sum(keep, give)
        group_got = swapped_groups(group_give)
        pre_two = swapped_groups(pre_give[cut:])
        down_keep, down_give = far_parts(joined(down_keep, near_down))
        far_down = far_swap(down_give)
        qkv_keep, give = near_parts(qkv_part.reshape(2, 2, -1, 3 * own))
        near_qkv = near_swap(give)
        outputs = turned_back(final)
        normed_got = in_order(normed_got, swapped_cores(normed_got), core, 1)
        normed_got = normed_got.reshape(local_rows, width)
        out_keep, out_give = group_parts(
            weight_grad((stored[2][0], branch)).reshape(2, 2, groups, -1, width)
        )
        group_got, pre_two, far_down, out_give = together(group_got, pre_two, far_down, out_give)

        pre_got = jnp.concatenate([pre_one, pre_two], axis=0)
        up_keep, up_give = near_parts(weight_grad((normed_two, pre_own), (normed_got, pre_got)))
        near_up = near_swap(up_give)
        y_out = swapped_groups(out_give)
        dx, one = norm_back_once(stored[0], keep, core_got, group_got, rest_half, True)
        (vectors,) = run(
            pack_kernel,
            "pack",
            [((size, 16, 256), LOW)],
            [one, swapped_cores(one), branch_sums, down_sum, up_sum, qkv_sums],
            0,
        )
        vector_keep, give = group_parts(vectors.reshape(2, 2, groups, 16, 256))
        y_vector = swapped_groups(give)
        near_qkv, y_vector, y_out, dx = together(near_qkv, y_vector, y_out, dx)

        qkv_keep, give = far_parts(joined(qkv_keep, near_qkv))
        far_qkv = far_swap(give)
        moved = from_micros(dx, micro, micros)
        vector_keep, give = near_parts(joined(vector_keep, y_vector))
        near_vector = near_swap(give)
        near_vector, near_up = together(near_vector, near_up)

        up_keep, up_give = far_parts(joined(up_keep, near_up))
        far_up = far_swap(up_give)
        out_keep, give = near_parts(joined(out_keep, y_out))
        near_out = near_swap(give)
        vector_keep, give = far_parts(joined(vector_keep, near_vector))
        far_vector = far_swap(give)
        qkv_sum = total(qkv_keep, far_qkv).reshape(groups, -1, 3 * own)
        qkv_got = swapped_groups(picked(qkv_sum, 1 - group, 0).astype(LOW))
        near_out, far_vector, far_up, qkv_got, moved = together(
            near_out, far_vector, far_up, qkv_got, moved
        )

        out_keep, give = far_parts(joined(out_keep, near_out))
        far_out = far_swap(give)
        up_sum = total(up_keep, far_up).reshape(groups, -1, hidden // 2)
        up_got = swapped_groups(picked(up_sum, 1 - group, 0).astype(LOW))
        outputs_grad = turned_back(moved)
        down_grad = total(down_keep, far_down)
        (qkv_w_grad,) = run(
            heads_kernel,
            "heads",
            [((width // size, 3, inner), SINGLE)],
            [picked(qkv_sum, group, 0), qkv_got],
            0,
        )
        cut = width // size
        vector = run(
            unpack_kernel,
            "unpack",
            [((1, cut), SINGLE)] * 6
            + [((1, hidden // size), SINGLE), ((2, inner // size), SINGLE)],
            [vector_keep, far_vector],
            0,
        )
        (up_grad,) = run(
            partial(columns_kernel, size),
            "columns",
            [((cut, hidden), SINGLE)],
            [picked(up_sum, group, 0), up_got],
            0,
        )
        return (
            outputs,
            outputs_grad,
            vector[0],
            vector[1],
            qkv_w_grad[None],
            vector[7][None],
            total(out_keep, far_out)[None],
            vector[2],
            vector[3],
            vector[4],
            up_grad[None],
            vector[6],
            down_grad[None],
            vector[5],
        )

    def turned_back(moved):
        return run(
            place_kernel,
            "place",
            [((micros, rows, width), LOW)],
            [moved, swapped_cores(moved)],
            0,
        )[0][None]

    begun = jnp.where(first, block_input, out_grad).reshape(micros, 2, half, width)
    begun = across_micros(picked(begun, core, 1), micro, micros)
    begun, qkv_w, up_w, up_b, down_w = together(begun, qkv_w, up_w, up_b, down_w)
    early, (_, early_out, *_) = forward(in_pieces(begun), False, qkv_w)
    qkv_w = early_out[2]
    received = [passed_along(piece, "section", 1) for piece in in_pieces(early)]
    pieces = [jnp.where(first, *pair) for pair in zip(in_pieces(begun), received)]
    final, stored = forward(pieces, True, qkv_w)
    early_grad, hidden_got, hidden_far = backward(begun, stored, qkv_w)
    normed_far = picked(stored[3][1].reshape(micros, 2, half, width), core, 1)
    returned = [passed_along(early_grad[0], "section", -1)]
    last_grad, final, hidden_far, normed_far = together(
        early_grad[1], final, hidden_far, normed_far
    )
    returned.append(passed_along(last_grad, "section", -1))
    *returned, hidden_last, normed_got, moved = together(
        *returned,
        swapped_groups(hidden_far),
        swapped_groups(normed_far),
        from_micros(final, micro, micros),
    )
    hidden_got = jnp.concatenate([*hidden_got, hidden_last], axis=0)
    grad_half = jnp.where(first, jnp.concatenate(returned, axis=0), begun)
    return backward_last(grad_half, stored, hidden_got, normed_got, moved, qkv_w)


def solution(mesh):
    placed = (
        P(None, "seq", None),
        P(None, "seq", None),
        P(),
        P("section", None),
        P("section", None),
        P("section", None, None, "tensor"),
        P("section", None, "tensor"),
        P("section", "tensor", None),
        P("section", None),
        P("section", None),
        P("section", None),
        P("section", None, "tensor"),
        P("section", "tensor"),
        P("section", "tensor", None),
        P("section", None),
    )

    def chosen(*arrays):
        pairs = mesh.shape["seq"] == 2 * arrays[0].shape[0]
        cores = mesh.shape["tensor"] == 2 and mesh.shape["section"] == 2
        heads = arrays[7].shape[1] // HEAD_DIM
        if pairs and cores and heads % 2 == 0:
            return micro_local(*arrays)
        return local(*arrays)

    return jax.shard_map(
        chosen,
        mesh=mesh,
        in_specs=placed,
        out_specs=(
            P("section", None, "seq", None),
            P("section", None, "seq", None),
            P("section", "seq"),
            P("section", "seq"),
            P("section", "seq", None, "tensor"),
            P("section", None, ("tensor", "seq")),
            P("section", ("tensor", "seq"), None),
            P("section", "seq"),
            P("section", "seq"),
            P("section", "seq"),
            P("section", "seq", "tensor"),
            P("section", ("tensor", "seq")),
            P("section", ("tensor", "seq"), None),
            P("section", "seq"),
        ),
        check_vma=False,
    )
```
